32 devices in a mesh: groups: 2 (over y), row: 8 (over z, core), col: 2 (over x), sub: 1.
Axes of the slice: x: 2, y: 2, z: 4, core: 2. Of those that a mesh axis runs over, the one named last changes fastest.
Arguments:
- pair: float32 [256, 128, 128], P(('groups', 'row'), 'col'), parts along dimension 0, may hold values from -24 to 24
- residue_mask: int32 [256], P('groups'), parts along dimension 0, may hold values 0 or 1
- out_proj: bfloat16 [128, 4, 128], P(None, None, 'sub'), may hold values from -0.5 to 0.5
- out_gate: bfloat16 [128, 128], replicated, may hold values from -0.5 to 0.5
- out_final: bfloat16 [128, 128], replicated, may hold values from -0.5 to 0.5
- in_proj: bfloat16 [128, 4, 128], P(None, None, 'sub'), may hold values from -0.5 to 0.5
- in_gate: bfloat16 [128, 128], replicated, may hold values from -0.5 to 0.5
- in_final: bfloat16 [128, 128], replicated, may hold values from -0.5 to 0.5
Outputs:
- updated: float32 [256, 128, 128], P(('groups', 'row'), 'col'), parts along dimension 0
The draws below stay inside these ranges and needn't reach their ends.
There are 2 independent parts, one for each index of `groups`. The reference program is written for one: setup_inputs(seed, part) draws one part's arguments, and reference() takes and returns one part's arrays. A program takes and returns all parts, laid end to end along the dimension named above; an argument that names none is the same for every part. Nothing has to cross between parts.
All inputs are finite; a program needn't handle non-finite values.
Results may differ from the reference program's by a relative error of at most 0.0029.
Values may be sent and summed in bfloat16 or wider, within the bound.
No kernel may reach another device: no remote copies, remote signals or barrier semaphores. Data moves between devices by JAX's collectives and lax.ppermute only.
A program may use at most 64 MiB of HBM per device.

```python
import math
import jax
import jax.numpy as jnp
from jax import lax

C = 128
HID = 128
N = 128


def draw_pair(key, part):
    key = jax.random.fold_in(key, 11)
    key_base, key_chan, key_cell = jax.random.split(key, 3)
    base = jnp.clip(jax.random.normal(key_base, (N, N, C), jnp.float32), -4.0, 4.0)
    channel_scale = jnp.exp(jax.random.uniform(key_chan, (C,), jnp.float32, math.log(0.3), math.log(3.0)))
    cell_scale = jnp.exp(jax.random.uniform(key_cell, (N, N, 1), jnp.float32, math.log(0.5), math.log(2.0)))
    return base * channel_scale * cell_scale


def place_ends(values, rng, low, top_value):
    longest = values.shape.index(max(values.shape))
    spots = []
    for shift in (0, 1):
        where = [jax.random.randint(jax.random.fold_in(rng, axis), (), 0, length) for axis, length in enumerate(values.shape)]
        where[longest] = (where[longest] + shift) % values.shape[longest]
        spots.append(tuple(where))
    return values.at[spots[0]].set(low).at[spots[1]].set(top_value)


def gaussian(key, shape, spread, most, kind=jnp.bfloat16):
    values = spread * jax.random.normal(key, shape, jnp.float32)
    return jnp.clip(values, min=-most, max=most).astype(kind)


def setup_inputs(seed: int = 0, part: int = 0) -> dict:
    key_of = jax.random.split(jax.random.key(seed), 9)
    own_keys = jax.random.split(jax.random.fold_in(key_of[8], part), 9)
    return {
        "pair": draw_pair(jax.random.fold_in(jax.random.fold_in(key_of[8], part), 71), part),
        "residue_mask": place_ends((jax.random.randint(own_keys[1], (N,), 0, 8) < 7).astype(jnp.int32), jax.random.fold_in(own_keys[1], 1), 0, 1),
        "out_proj": gaussian(key_of[2], (C, 4, HID), C ** -0.5, 0.5),
        "out_gate": gaussian(key_of[3], (C, C), C ** -0.5, 0.5),
        "out_final": gaussian(key_of[4], (HID, C), HID ** -0.5, 0.5),
        "in_proj": gaussian(key_of[5], (C, 4, HID), C ** -0.5, 0.5),
        "in_gate": gaussian(key_of[6], (C, C), C ** -0.5, 0.5),
        "in_final": gaussian(key_of[7], (HID, C), HID ** -0.5, 0.5),
    }


def normalize(values, axis):
    average = lax.optimization_barrier(jnp.mean(values, axis=axis, keepdims=True))
    centred = values - average
    variance = lax.optimization_barrier(jnp.mean(centred * centred, axis=axis, keepdims=True))
    return centred * jax.lax.rsqrt(variance + 1e-05)

def gated_panels(pair, residue_mask, proj):
    normed = normalize(pair, 2).astype(jnp.bfloat16)
    live = residue_mask.astype(jnp.float32)
    pair_mask = live[:, None, None] * live[None, :, None]
    normed_wide = normed.astype(jnp.float32)

    def linear(which):
        return jnp.einsum('ijc,ch->ijh', normed_wide, proj[:, which, :].astype(jnp.float32))
    left_panel = (pair_mask * jax.nn.sigmoid(linear(1)) * linear(0)).astype(jnp.bfloat16)
    right_panel = (pair_mask * jax.nn.sigmoid(linear(3)) * linear(2)).astype(jnp.bfloat16)
    return (normed, left_panel, right_panel)

def update_pair(pair, normed, mixed, gate_w, final_w):
    scaled = normalize(mixed, 2).astype(jnp.bfloat16)
    projected = jnp.einsum('ijh,hc->ijc', scaled.astype(jnp.float32), final_w.astype(jnp.float32))
    gating = jax.nn.sigmoid(jnp.einsum('ijc,cd->ijd', normed.astype(jnp.float32), gate_w.astype(jnp.float32)))
    return pair + gating * projected

def reference(pair, residue_mask, out_proj, out_gate, out_final, in_proj, in_gate, in_final):
    normed, left_panel, right_panel = gated_panels(pair, residue_mask, out_proj)
    mixed = jnp.einsum('ikh,jkh->ijh', left_panel.astype(jnp.float32), right_panel.astype(jnp.float32))
    middle = update_pair(pair, normed, mixed, out_gate, out_final)
    normed, left_panel, right_panel = gated_panels(middle, residue_mask, in_proj)
    mixed = jnp.einsum('kih,kjh->ijh', left_panel.astype(jnp.float32), right_panel.astype(jnp.float32))
    return update_pair(middle, normed, mixed, in_gate, in_final)
```

```python
import functools

import jax
import jax.numpy as jnp
from jax import lax
from jax.experimental import pallas as pl
from jax.experimental.pallas import tpu as pltpu
from jax.sharding import PartitionSpec as P

F32 = jnp.float32
BF16 = jnp.bfloat16
LANES = 128
EPS = 1e-05


def over_channels(values):
    centred = values - jnp.mean(values, axis=0, keepdims=True)
    variance = jnp.mean(centred * centred, axis=0, keepdims=True)
    return centred * lax.rsqrt(variance + EPS)


def from_left(weight, values):
    return lax.dot_general(weight, values, (((0,), (0,)), ((), ())), preferred_element_type=F32)


def live_tile(mask_ref, rows, cols):
    live = mask_ref[...].astype(F32)
    lane = lax.broadcasted_iota(jnp.int32, (rows, LANES), 1)
    sub = lax.broadcasted_iota(jnp.int32, (rows, LANES), 0)
    wide = jnp.broadcast_to(live, (rows, LANES))
    mine = lane == lax.axis_index("row") * rows + sub
    row_live = jnp.sum(jnp.where(mine, wide, 0.0), axis=1, keepdims=True)
    col_live = jnp.where(lane // cols == lax.axis_index("col"), wide, pltpu.roll(wide, cols, 1))
    return row_live * col_live


def panels(normed, proj_ref, mask_ref, msg_ref, tiles, rows, cols):
    side = 2 * lax.axis_index("col")
    first = jax.nn.sigmoid(from_left(proj_ref[side + 1], normed)) * from_left(proj_ref[side], normed)
    second = jax.nn.sigmoid(from_left(proj_ref[3 - side], normed)) * from_left(proj_ref[2 - side], normed)
    hidden = first.shape[0]
    low = lax.broadcasted_iota(jnp.int32, (hidden, LANES), 1) < cols
    for t in range(rows // 2):
        a = first[:, t * LANES : (t + 1) * LANES]
        b = second[:, t * LANES : (t + 1) * LANES]
        tiles[pl.ds(2 * t, hidden, stride=rows), :] = jnp.where(low, a, pltpu.roll(b, cols, 1))
        tiles[pl.ds(2 * t + 1, hidden, stride=rows), :] = jnp.where(low, pltpu.roll(a, cols, 1), b)
    live = live_tile(mask_ref, rows, cols)
    devices, per_device = msg_ref.shape[:2]
    half = per_device // 2
    for d in range(devices):
        for e in range(per_device):
            h = (e // half) * (hidden // 2) + d * half + e % half
            msg_ref[d, e] = (tiles[h * rows : (h + 1) * rows, :] * live).astype(BF16)


def projected(recv_ref, final_ref, tiles, rows, cols):
    values = recv_ref[...].reshape(-1, rows, LANES).astype(F32)
    half = values.shape[0]
    total = jnp.sum(values, axis=0)
    centred = values - ((total + pltpu.roll(total, cols, 1)) / (2 * half))[None]
    square = jnp.sum(centred * centred, axis=0)
    variance = (square + pltpu.roll(square, cols, 1)) / (2 * half)
    tiles[: half * rows, :] = (centred * lax.rsqrt(variance + EPS)[None]).reshape(half * rows, LANES)
    low = lax.broadcasted_iota(jnp.int32, (half, LANES), 1) < cols
    parts = []
    for t in range(rows // 2):
        a = tiles[pl.ds(2 * t, half, stride=rows), :]
        b = tiles[pl.ds(2 * t + 1, half, stride=rows), :]
        upper = jnp.where(low, a, pltpu.roll(b, cols, 1))
        lower = jnp.where(low, pltpu.roll(a, cols, 1), b)
        parts.append(jnp.concatenate([upper, lower], axis=0).astype(BF16))
    return from_left(final_ref[...], jnp.concatenate(parts, axis=1))


def first_kernel(rows, cols, mask_ref, pair_ref, proj_ref, gate_ref, msg_ref, pair_t_ref, gating_ref, tiles):
    pair = pair_ref[...].T
    pair_t_ref[...] = pair
    normed = over_channels(pair).astype(BF16)
    gating_ref[...] = jax.nn.sigmoid(from_left(gate_ref[...], normed))
    panels(normed, proj_ref, mask_ref, msg_ref, tiles, rows, cols)


def middle_kernel(
    rows, cols, mask_ref, recv_ref, pair_t_ref, gating_ref, final_ref, proj_ref, gate_ref, msg_ref, middle_ref, gating2_ref, tiles
):
    middle = pair_t_ref[...] + gating_ref[...] * projected(recv_ref, final_ref, tiles, rows, cols)
    middle_ref[...] = middle
    normed = over_channels(middle).astype(BF16)
    gating2_ref[...] = jax.nn.sigmoid(from_left(gate_ref[...], normed))
    panels(normed, proj_ref, mask_ref, msg_ref, tiles, rows, cols)


def last_kernel(rows, cols, recv_ref, middle_ref, gating_ref, final_ref, out_ref, tiles):
    out = middle_ref[...] + gating_ref[...] * projected(recv_ref, final_ref, tiles, rows, cols)
    out_ref[...] = out.T


def mix_kernel(incoming, cols, recv_ref, msg_ref):
    devices, per_device, rows, _ = recv_ref.shape
    blocks = devices // 2
    half = per_device // 2
    low = lax.broadcasted_iota(jnp.int32, (blocks * rows, LANES), 1) < cols

    def mixed(e):
        even = jnp.concatenate([recv_ref[2 * r, e] for r in range(blocks)], axis=0)
        odd = jnp.concatenate([recv_ref[2 * r + 1, e] for r in range(blocks)], axis=0)
        a = jnp.where(low, even, odd)
        b = jnp.where(low, odd, even)
        if incoming:
            x = lax.dot_general(a, b, (((0,), (0,)), ((), ())), preferred_element_type=F32)
            return pltpu.roll(x, cols, 1), x
        b = jnp.concatenate([b[:, cols:], b[:, :cols]], axis=1)
        x = lax.dot_general(a, b, (((1,), (1,)), ((), ())), preferred_element_type=F32)
        return x, pltpu.roll(x, cols, 1)

    for q in range(half):
        x, x_turned = mixed(q)
        y, y_turned = mixed(q + half)
        left = jnp.where(low, x, y_turned).astype(BF16)
        right = jnp.where(low, x_turned, y).astype(BF16)
        for r in range(blocks):
            msg_ref[2 * r, q] = left[r * rows : (r + 1) * rows]
            msg_ref[2 * r + 1, q] = right[r * rows : (r + 1) * rows]


def call(kernel, out_shape, scratch=()):
    vmem = pl.BlockSpec(memory_space=pltpu.VMEM)

    def run(*args):
        return pl.pallas_call(
            kernel,
            out_shape=out_shape,
            in_specs=[vmem] * len(args),
            out_specs=jax.tree.map(lambda _: vmem, out_shape),
            scratch_shapes=list(scratch),
            compiler_params=pltpu.CompilerParams(vmem_limit_bytes=40 * 1024 * 1024),
        )(*args)

    return run


def by_channel(devices, pair, residue_mask, out_proj, out_gate, out_final, in_proj, in_gate, in_final):
    rows, cols, channels = pair.shape
    hidden = out_proj.shape[2]
    positions = rows * cols
    per_device = hidden // devices
    shape = jax.ShapeDtypeStruct
    exchange = functools.partial(lax.all_to_all, axis_name=("row", "col"), split_axis=0, concat_axis=0, tiled=True)
    panel_msg = shape((devices, per_device, rows, LANES), BF16)
    mixed_msg = shape((devices, per_device // 2, rows, LANES), BF16)
    plane = shape((channels, positions), F32)
    tiles = pltpu.VMEM((hidden * rows, LANES), F32)
    mask = residue_mask.reshape(1, -1)

    msg, pair_t, gating = call(functools.partial(first_kernel, rows, cols), (panel_msg, plane, plane), [tiles])(
        mask, pair.reshape(positions, channels), jnp.swapaxes(out_proj, 0, 1), out_gate
    )
    mixed = call(functools.partial(mix_kernel, False, cols), mixed_msg)(exchange(msg))
    msg, middle, gating = call(functools.partial(middle_kernel, rows, cols), (panel_msg, plane, plane), [tiles])(
        mask, exchange(mixed), pair_t, gating, out_final, jnp.swapaxes(in_proj, 0, 1), in_gate
    )
    mixed = call(functools.partial(mix_kernel, True, cols), mixed_msg)(exchange(msg))
    out = call(functools.partial(last_kernel, rows, cols), shape((positions, channels), F32), [tiles])(
        exchange(mixed), middle, gating, in_final
    )
    return out.reshape(rows, cols, channels)


def normalize(values, axis):
    average = jnp.mean(values, axis=axis, keepdims=True)
    centred = values - average
    variance = jnp.mean(centred * centred, axis=axis, keepdims=True)
    return centred * lax.rsqrt(variance + EPS)


def gated_panels(pair, row_live, col_live, proj):
    normed = normalize(pair, 2).astype(BF16)
    linear = jnp.einsum("ijc,cph->phij", normed, proj, preferred_element_type=F32)
    pair_mask = row_live[:, None] * col_live[None, :]
    left_panel = (pair_mask * jax.nn.sigmoid(linear[1]) * linear[0]).astype(BF16)
    right_panel = (pair_mask * jax.nn.sigmoid(linear[3]) * linear[2]).astype(BF16)
    return (normed, left_panel, right_panel)


def update_pair(pair, normed, mixed, gate_w, final_w):
    all_channels = lax.all_gather(mixed, "sub", axis=0, tiled=True)
    scaled = normalize(all_channels, 0).astype(BF16)
    projected = jnp.einsum("hij,hc->ijc", scaled, final_w, preferred_element_type=F32)
    gating = jax.nn.sigmoid(jnp.einsum("ijc,cd->ijd", normed, gate_w, preferred_element_type=F32))
    return pair + gating * projected


def by_position(pair, residue_mask, out_proj, out_gate, out_final, in_proj, in_gate, in_final):
    row_count = pair.shape[0]
    col_count = pair.shape[1]
    row_start = lax.axis_index("row") * row_count
    col_start = lax.axis_index("col") * col_count
    live = residue_mask.astype(F32)
    row_live = lax.dynamic_slice_in_dim(live, row_start, row_count, 0)
    col_live = lax.dynamic_slice_in_dim(live, col_start, col_count, 0)
    normed, left_panel, right_panel = gated_panels(pair, row_live, col_live, out_proj)
    left_rows, right_rows = (
        lax.all_gather(left_panel, "col", axis=2, tiled=True),
        lax.all_gather(right_panel, "col", axis=2, tiled=True),
    )
    turned = lax.all_to_all(right_rows, "row", split_axis=2, concat_axis=1, tiled=True)
    own_right = lax.dynamic_slice_in_dim(turned, col_start, col_count, 1)
    mixed = jnp.einsum(
        "hik,hjk->hij",
        left_rows,
        lax.all_gather(own_right, "row", axis=2, tiled=True),
        preferred_element_type=F32,
    )
    middle = update_pair(pair, normed, mixed, out_gate, out_final)
    normed, left_panel, right_panel = gated_panels(middle, row_live, col_live, in_proj)
    left_rows = lax.all_gather(left_panel, "col", axis=2, tiled=True)
    turned_left = lax.all_to_all(left_rows, "row", split_axis=2, concat_axis=1, tiled=True)
    mixed_in = jnp.einsum(
        "hki,hkj->hij",
        turned_left,
        lax.all_gather(right_panel, "row", axis=1, tiled=True),
        preferred_element_type=F32,
    )
    return update_pair(middle, normed, mixed_in, in_gate, in_final)


def local(axes, pair, residue_mask, out_proj, *rest):
    rows, cols, channels = pair.shape
    hidden = out_proj.shape[2]
    devices = axes["row"] * axes["col"]
    fits = (
        axes["sub"] == 1
        and axes["col"] == 2
        and residue_mask.shape[0] == LANES
        and cols * 2 == LANES
        and rows % 16 == 0
        and channels == LANES
        and hidden % (2 * devices) == 0
        and hidden % 16 == 0
    )
    plan = functools.partial(by_channel, devices) if fits else by_position
    return plan(pair, residue_mask, out_proj, *rest)


def solution(mesh):
    return jax.shard_map(
        functools.partial(local, dict(mesh.shape)),
        mesh=mesh,
        in_specs=(
            P(("groups", "row"), "col", None),
            P("groups"),
            P(None, None, "sub"),
            P(),
            P(),
            P(None, None, "sub"),
            P(),
            P(),
        ),
        out_specs=P(("groups", "row"), "col", None),
        check_vma=False,
    )
```

```python
import functools

import jax
import jax.numpy as jnp
from jax import lax
from jax.experimental import pallas as pl
from jax.experimental.pallas import tpu as pltpu
from jax.sharding import PartitionSpec as P

F32 = jnp.float32
BF16 = jnp.bfloat16
LANES = 128
CHUNK = 256
EPS = 1e-05


def over_channels(values):
    centred = values - jnp.mean(values, axis=0, keepdims=True)
    variance = jnp.mean(centred * centred, axis=0, keepdims=True)
    return centred * lax.rsqrt(variance + EPS)


def product(weight, values):
    return lax.dot_general(weight, values, (((0,), (0,)), ((), ())), preferred_element_type=F32)


def side_by_side(proj_ref, gate_ref, wide, weights):
    channels, hidden = gate_ref.shape
    wide[...] = proj_ref[...].astype(F32)
    side = 2 * lax.axis_index("col")
    for n, p in enumerate((side, side + 1, 2 - side, 3 - side)):
        weights[:, n * hidden : (n + 1) * hidden] = wide[pl.ds(p, channels, stride=4), :].astype(BF16)
    weights[:, 4 * hidden :] = gate_ref[...]


def live_tile(mask_ref, rows, cols):
    live = mask_ref[...].astype(F32)
    lane = lax.broadcasted_iota(jnp.int32, (rows, LANES), 1)
    sub = lax.broadcasted_iota(jnp.int32, (rows, LANES), 0)
    wide = jnp.broadcast_to(live, (rows, LANES))
    mine = lane == lax.axis_index("row") * rows + sub
    row_live = jnp.sum(jnp.where(mine, wide, 0.0), axis=1, keepdims=True)
    col_live = jnp.where(lane // cols == lax.axis_index("col"), wide, pltpu.roll(wide, cols, 1))
    return row_live * col_live


def panels(normed, weights, live, msg_ref, gating_ref, rows, cols):
    linear = product(weights[...], normed)
    hidden = linear.shape[0] // 5
    gating_ref[...] = jax.nn.sigmoid(linear[4 * hidden :])
    first = jax.nn.sigmoid(linear[hidden : 2 * hidden]) * linear[:hidden]
    second = jax.nn.sigmoid(linear[3 * hidden : 4 * hidden]) * linear[2 * hidden : 3 * hidden]
    low = lax.broadcasted_iota(jnp.int32, (hidden, LANES), 1) < cols
    by_row = []
    for t in range(rows // 2):
        a = first[:, t * LANES : (t + 1) * LANES]
        b = second[:, t * LANES : (t + 1) * LANES]
        for tile in (jnp.where(low, a, pltpu.roll(b, cols, 1)), jnp.where(low, pltpu.roll(a, cols, 1), b)):
            row = len(by_row)
            by_row.append((tile * live[row : row + 1]).astype(BF16))
    by_hidden = jnp.swapaxes(jnp.stack(by_row, axis=0), 0, 1)
    devices, per_device = msg_ref.shape[:2]
    half = per_device // 2
    for d in range(devices):
        msg_ref[d, :half] = by_hidden[d * half : (d + 1) * half]
        msg_ref[d, half:] = by_hidden[hidden // 2 + d * half : hidden // 2 + (d + 1) * half]


def projected(recv_ref, final_ref, tiles, rows, cols):
    values = recv_ref[...].reshape(-1, rows, LANES).astype(F32)
    half = values.shape[0]
    total = jnp.sum(values, axis=0)
    centred = values - ((total + pltpu.roll(total, cols, 1)) / (2 * half))[None]
    square = jnp.sum(centred * centred, axis=0)
    variance = (square + pltpu.roll(square, cols, 1)) / (2 * half)
    tiles[: half * rows, :] = (centred * lax.rsqrt(variance + EPS)[None]).reshape(half * rows, LANES)
    low = lax.broadcasted_iota(jnp.int32, (half, LANES), 1) < cols
    parts = []
    for t in range(rows // 2):
        a = tiles[pl.ds(2 * t, half, stride=rows), :]
        b = tiles[pl.ds(2 * t + 1, half, stride=rows), :]
        upper = jnp.where(low, a, pltpu.roll(b, cols, 1))
        lower = jnp.where(low, pltpu.roll(a, cols, 1), b)
        parts.append(jnp.concatenate([upper, lower], axis=0).astype(BF16))
    return product(final_ref[...], jnp.concatenate(parts, axis=1))


def copies(pairs, done):
    started = [pltpu.make_async_copy(source, target, done.at[n]) for n, (source, target) in enumerate(pairs)]
    for copy in started:
        copy.start()
    return started


def first_kernel(
    rows, cols, pair_hbm, mask_hbm, proj_hbm, gate_hbm, proj2_hbm, gate2_hbm, msg_ref, pair_t_ref, gating_ref, live_ref, weights2,
    pair_ref, mask_ref, proj_ref, gate_ref, proj2_ref, gate2_ref, weights, wide, done,
):
    whole = ((mask_hbm, mask_ref), (proj_hbm, proj_ref), (gate_hbm, gate_ref), (proj2_hbm, proj2_ref), (gate2_hbm, gate2_ref))
    chunks = [slice(at, at + CHUNK) for at in range(0, rows * cols, CHUNK)]
    coming = copies([(pair_hbm.at[at], pair_ref.at[at]) for at in chunks] + list(whole), done)
    for copy in coming[len(chunks) :]:
        copy.wait()
    side_by_side(proj_ref, gate_ref, wide, weights)
    side_by_side(proj2_ref, gate2_ref, wide, weights2)
    for copy in coming[: len(chunks)]:
        copy.wait()
    pair = pair_ref[...].T
    pair_t_ref[...] = pair
    live = live_tile(mask_ref, rows, cols)
    live_ref[...] = live
    panels(over_channels(pair).astype(BF16), weights, live, msg_ref, gating_ref, rows, cols)


def middle_kernel(
    rows, cols, live_ref, weights, final_ref, recv_ref, pair_t_ref, gating_ref, msg_ref, middle_ref, gating2_ref, tiles
):
    middle = pair_t_ref[...] + gating_ref[...] * projected(recv_ref, final_ref, tiles, rows, cols)
    middle_ref[...] = middle
    panels(over_channels(middle).astype(BF16), weights, live_ref[...], msg_ref, gating2_ref, rows, cols)


def last_kernel(rows, cols, recv_ref, middle_ref, gating_ref, final_ref, out_hbm, tiles, out_ref, done):
    change = projected(recv_ref, final_ref, tiles, rows, cols)
    leaving = []
    for n in range(rows * cols // CHUNK):
        at = slice(n * CHUNK, (n + 1) * CHUNK)
        out_ref[at, :] = (middle_ref[:, at] + gating_ref[:, at] * change[:, at]).T
        leaving.append(pltpu.make_async_copy(out_ref.at[at], out_hbm.at[at], done.at[n]))
        leaving[-1].start()
    for copy in leaving:
        copy.wait()


def mix_kernel(incoming, cols, recv_ref, msg_ref):
    devices, per_device, rows, _ = recv_ref.shape
    blocks = devices // 2
    half = per_device // 2
    low = lax.broadcasted_iota(jnp.int32, (blocks * rows, LANES), 1) < cols

    def mixed(e):
        even = jnp.concatenate([recv_ref[2 * r, e] for r in range(blocks)], axis=0)
        odd = jnp.concatenate([recv_ref[2 * r + 1, e] for r in range(blocks)], axis=0)
        a = jnp.where(low, even, odd)
        b = jnp.where(low, odd, even)
        if incoming:
            x = lax.dot_general(a, b, (((0,), (0,)), ((), ())), preferred_element_type=F32)
            return pltpu.roll(x, cols, 1), x
        b = pltpu.roll(b.astype(F32), cols, 1).astype(BF16)
        x = lax.dot_general(a, b, (((1,), (1,)), ((), ())), preferred_element_type=F32)
        return x, pltpu.roll(x, cols, 1)

    for q in range(half):
        x, x_turned = mixed(q)
        y, y_turned = mixed(q + half)
        left = jnp.where(low, x, y_turned).astype(BF16)
        right = jnp.where(low, x_turned, y).astype(BF16)
        for r in range(blocks):
            msg_ref[2 * r, q] = left[r * rows : (r + 1) * rows]
            msg_ref[2 * r + 1, q] = right[r * rows : (r + 1) * rows]


def call(kernel, out_shape, scratch=(), far=(0, False)):
    vmem = pl.BlockSpec(memory_space=pltpu.VMEM)
    hbm = pl.BlockSpec(memory_space=pltpu.HBM)
    far_args, far_outs = far

    def run(*args):
        args = [pltpu.with_memory_space_constraint(a, pltpu.HBM) for a in args[:far_args]] + list(args[far_args:])
        return pl.pallas_call(
            kernel,
            out_shape=out_shape,
            in_specs=[hbm] * far_args + [vmem] * (len(args) - far_args),
            out_specs=jax.tree.map(lambda _: hbm if far_outs else vmem, out_shape),
            scratch_shapes=list(scratch),
            compiler_params=pltpu.CompilerParams(vmem_limit_bytes=40 * 1024 * 1024),
        )(*args)

    return run


def by_channel(devices, pair, residue_mask, out_proj, out_gate, out_final, in_proj, in_gate, in_final):
    rows, cols, channels = pair.shape
    hidden = out_proj.shape[2]
    positions = rows * cols
    per_device = hidden // devices
    shape = jax.ShapeDtypeStruct
    exchange = functools.partial(lax.all_to_all, axis_name=("row", "col"), split_axis=0, concat_axis=0, tiled=True)
    panel_msg = shape((devices, per_device, rows, LANES), BF16)
    mixed_msg = shape((devices, per_device // 2, rows, LANES), BF16)
    plane = shape((channels, positions), F32)
    mask = residue_mask.reshape(1, -1)
    by_position = pltpu.VMEM((positions, channels), F32)
    tiles = pltpu.VMEM((positions, LANES), F32)
    weights = (channels, 5 * hidden)
    chunks = positions // CHUNK

    far = (pair.reshape(positions, channels), mask, out_proj.reshape(-1, hidden), out_gate, in_proj.reshape(-1, hidden), in_gate)
    near = [pltpu.VMEM(a.shape, a.dtype) for a in far] + [pltpu.VMEM(weights, BF16), pltpu.VMEM((4 * channels, hidden), F32), pltpu.SemaphoreType.DMA((chunks + 5,))]
    outs = (panel_msg, plane, plane, shape((rows, LANES), F32), shape(weights, BF16))
    msg, pair_t, gating, live, weights = call(functools.partial(first_kernel, rows, cols), outs, near, (6, False))(*far)
    mixed = call(functools.partial(mix_kernel, False, cols), mixed_msg)(exchange(msg))
    outs = (panel_msg, plane, plane)
    msg, middle, gating = call(functools.partial(middle_kernel, rows, cols), outs, [tiles])(
        live, weights, out_final, exchange(mixed), pair_t, gating
    )
    mixed = call(functools.partial(mix_kernel, True, cols), mixed_msg)(exchange(msg))
    near = [tiles, by_position, pltpu.SemaphoreType.DMA((chunks,))]
    out = call(functools.partial(last_kernel, rows, cols), shape((positions, channels), F32), near, (0, True))(
        exchange(mixed), middle, gating, in_final
    )
    return out.reshape(rows, cols, channels)


def normalize(values, axis):
    average = jnp.mean(values, axis=axis, keepdims=True)
    centred = values - average
    variance = jnp.mean(centred * centred, axis=axis, keepdims=True)
    return centred * lax.rsqrt(variance + EPS)


def gated_panels(pair, row_live, col_live, proj):
    normed = normalize(pair, 2).astype(BF16)
    linear = jnp.einsum("ijc,cph->phij", normed, proj, preferred_element_type=F32)
    pair_mask = row_live[:, None] * col_live[None, :]
    left_panel = (pair_mask * jax.nn.sigmoid(linear[1]) * linear[0]).astype(BF16)
    right_panel = (pair_mask * jax.nn.sigmoid(linear[3]) * linear[2]).astype(BF16)
    return (normed, left_panel, right_panel)


def update_pair(pair, normed, mixed, gate_w, final_w):
    all_channels = lax.all_gather(mixed, "sub", axis=0, tiled=True)
    scaled = normalize(all_channels, 0).astype(BF16)
    projected = jnp.einsum("hij,hc->ijc", scaled, final_w, preferred_element_type=F32)
    gating = jax.nn.sigmoid(jnp.einsum("ijc,cd->ijd", normed, gate_w, preferred_element_type=F32))
    return pair + gating * projected


def by_position(pair, residue_mask, out_proj, out_gate, out_final, in_proj, in_gate, in_final):
    row_count = pair.shape[0]
    col_count = pair.shape[1]
    row_start = lax.axis_index("row") * row_count
    col_start = lax.axis_index("col") * col_count
    live = residue_mask.astype(F32)
    row_live = lax.dynamic_slice_in_dim(live, row_start, row_count, 0)
    col_live = lax.dynamic_slice_in_dim(live, col_start, col_count, 0)
    normed, left_panel, right_panel = gated_panels(pair, row_live, col_live, out_proj)
    left_rows, right_rows = (
        lax.all_gather(left_panel, "col", axis=2, tiled=True),
        lax.all_gather(right_panel, "col", axis=2, tiled=True),
    )
    turned = lax.all_to_all(right_rows, "row", split_axis=2, concat_axis=1, tiled=True)
    own_right = lax.dynamic_slice_in_dim(turned, col_start, col_count, 1)
    mixed = jnp.einsum(
        "hik,hjk->hij",
        left_rows,
        lax.all_gather(own_right, "row", axis=2, tiled=True),
        preferred_element_type=F32,
    )
    middle = update_pair(pair, normed, mixed, out_gate, out_final)
    normed, left_panel, right_panel = gated_panels(middle, row_live, col_live, in_proj)
    left_rows = lax.all_gather(left_panel, "col", axis=2, tiled=True)
    turned_left = lax.all_to_all(left_rows, "row", split_axis=2, concat_axis=1, tiled=True)
    mixed_in = jnp.einsum(
        "hki,hkj->hij",
        turned_left,
        lax.all_gather(right_panel, "row", axis=1, tiled=True),
        preferred_element_type=F32,
    )
    return update_pair(middle, normed, mixed_in, in_gate, in_final)


def local(axes, pair, residue_mask, out_proj, *rest):
    rows, cols, channels = pair.shape
    hidden = out_proj.shape[2]
    devices = axes["row"] * axes["col"]
    fits = (
        axes["sub"] == 1
        and axes["col"] == 2
        and residue_mask.shape[0] == LANES
        and cols * 2 == LANES
        and rows % 16 == 0
        and rows * cols % CHUNK == 0
        and channels == LANES
        and hidden == channels
        and hidden % (2 * devices) == 0
        and hidden % 16 == 0
    )
    plan = functools.partial(by_channel, devices) if fits else by_position
    return plan(pair, residue_mask, out_proj, *rest)


def solution(mesh):
    return jax.shard_map(
        functools.partial(local, dict(mesh.shape)),
        mesh=mesh,
        in_specs=(
            P(("groups", "row"), "col", None),
            P("groups"),
            P(None, None, "sub"),
            P(),
            P(),
            P(None, None, "sub"),
            P(),
            P(),
        ),
        out_specs=P(("groups", "row"), "col", None),
        check_vma=False,
    )
```

```python
import functools

import jax
import jax.numpy as jnp
from jax import lax
from jax.experimental import pallas as pl
from jax.experimental.pallas import tpu as pltpu
from jax.sharding import PartitionSpec as P

F32 = jnp.float32
BF16 = jnp.bfloat16
LANES = 128
CHUNK = 256
EPS = 1e-05


def over_channels(values):
    centred = values - jnp.mean(values, axis=0, keepdims=True)
    variance = jnp.mean(centred * centred, axis=0, keepdims=True)
    return centred * lax.rsqrt(variance + EPS)


def product(weight, values):
    return lax.dot_general(weight, values, (((0,), (0,)), ((), ())), preferred_element_type=F32)


def side_by_side(proj_ref, gate_ref, wide, weights):
    channels, hidden = gate_ref.shape
    wide[...] = proj_ref[...].astype(F32)
    side = 2 * lax.axis_index("col")
    for n, p in enumerate((side, side + 1, 2 - side, 3 - side)):
        weights[:, n * hidden : (n + 1) * hidden] = wide[pl.ds(p, channels, stride=4), :].astype(BF16)
    weights[:, 4 * hidden :] = gate_ref[...]


def live_tile(mask_ref, rows, cols):
    live = mask_ref[...].astype(F32)
    lane = lax.broadcasted_iota(jnp.int32, (rows, LANES), 1)
    sub = lax.broadcasted_iota(jnp.int32, (rows, LANES), 0)
    wide = jnp.broadcast_to(live, (rows, LANES))
    mine = lane == lax.axis_index("row") * rows + sub
    row_live = jnp.sum(jnp.where(mine, wide, 0.0), axis=1, keepdims=True)
    col_live = jnp.where(lane // cols == lax.axis_index("col"), wide, pltpu.roll(wide, cols, 1))
    return row_live * col_live


def panels(normed, weights, live, msg_ref, gating_ref, rows, cols):
    linear = product(weights[...], normed)
    hidden = linear.shape[0] // 5
    gating_ref[...] = jax.nn.sigmoid(linear[4 * hidden :])
    first = jax.nn.sigmoid(linear[hidden : 2 * hidden]) * linear[:hidden]
    second = jax.nn.sigmoid(linear[3 * hidden : 4 * hidden]) * linear[2 * hidden : 3 * hidden]
    low = lax.broadcasted_iota(jnp.int32, (hidden, LANES), 1) < cols
    by_row = []
    for t in range(rows // 2):
        a = first[:, t * LANES : (t + 1) * LANES]
        b = second[:, t * LANES : (t + 1) * LANES]
        for tile in (jnp.where(low, a, pltpu.roll(b, cols, 1)), jnp.where(low, pltpu.roll(a, cols, 1), b)):
            row = len(by_row)
            by_row.append((tile * live[row : row + 1]).astype(BF16))
    by_hidden = jnp.swapaxes(jnp.stack(by_row, axis=0), 0, 1)
    devices, per_device = msg_ref.shape[:2]
    half = per_device // 2
    for d in range(devices):
        msg_ref[d, :half] = by_hidden[d * half : (d + 1) * half]
        msg_ref[d, half:] = by_hidden[hidden // 2 + d * half : hidden // 2 + (d + 1) * half]


def projected(recv_ref, final_ref, tiles, rows, cols):
    half = final_ref.shape[0] // 2
    values = jnp.sum(recv_ref[...].reshape(-1, half, rows, LANES).astype(F32), axis=0)
    total = jnp.sum(values, axis=0)
    centred = values - ((total + pltpu.roll(total, cols, 1)) / (2 * half))[None]
    square = jnp.sum(centred * centred, axis=0)
    variance = (square + pltpu.roll(square, cols, 1)) / (2 * half)
    tiles[: half * rows, :] = (centred * lax.rsqrt(variance + EPS)[None]).reshape(half * rows, LANES)
    low = lax.broadcasted_iota(jnp.int32, (half, LANES), 1) < cols
    parts = []
    for t in range(rows // 2):
        a = tiles[pl.ds(2 * t, half, stride=rows), :]
        b = tiles[pl.ds(2 * t + 1, half, stride=rows), :]
        upper = jnp.where(low, a, pltpu.roll(b, cols, 1))
        lower = jnp.where(low, pltpu.roll(a, cols, 1), b)
        parts.append(jnp.concatenate([upper, lower], axis=0).astype(BF16))
    return product(final_ref[...], jnp.concatenate(parts, axis=1))


def copies(pairs, done):
    started = [pltpu.make_async_copy(source, target, done.at[n]) for n, (source, target) in enumerate(pairs)]
    for copy in started:
        copy.start()
    return started


def first_kernel(
    rows, cols, pair_hbm, mask_hbm, proj_hbm, gate_hbm, proj2_hbm, gate2_hbm, msg_ref, pair_t_ref, gating_ref, live_ref, weights2,
    pair_ref, mask_ref, proj_ref, gate_ref, proj2_ref, gate2_ref, weights, wide, done,
):
    whole = ((mask_hbm, mask_ref), (proj_hbm, proj_ref), (gate_hbm, gate_ref), (proj2_hbm, proj2_ref), (gate2_hbm, gate2_ref))
    chunks = [slice(at, at + CHUNK) for at in range(0, rows * cols, CHUNK)]
    coming = copies([(pair_hbm.at[at], pair_ref.at[at]) for at in chunks] + list(whole), done)
    for copy in coming[len(chunks) :]:
        copy.wait()
    side_by_side(proj_ref, gate_ref, wide, weights)
    side_by_side(proj2_ref, gate2_ref, wide, weights2)
    for copy in coming[: len(chunks)]:
        copy.wait()
    pair = pair_ref[...].T
    pair_t_ref[...] = pair
    live = live_tile(mask_ref, rows, cols)
    live_ref[...] = live
    panels(over_channels(pair).astype(BF16), weights, live, msg_ref, gating_ref, rows, cols)


def middle_kernel(
    rows, cols, live_ref, weights, final_ref, recv_ref, pair_t_ref, gating_ref, msg_ref, middle_ref, gating2_ref, tiles
):
    middle = pair_t_ref[...] + gating_ref[...] * projected(recv_ref, final_ref, tiles, rows, cols)
    middle_ref[...] = middle
    panels(over_channels(middle).astype(BF16), weights, live_ref[...], msg_ref, gating2_ref, rows, cols)


def last_kernel(rows, cols, recv_ref, middle_ref, gating_ref, final_ref, out_hbm, tiles, out_ref, done):
    change = projected(recv_ref, final_ref, tiles, rows, cols)
    leaving = []
    for n in range(rows * cols // CHUNK):
        at = slice(n * CHUNK, (n + 1) * CHUNK)
        out_ref[at, :] = (middle_ref[:, at] + gating_ref[:, at] * change[:, at]).T
        leaving.append(pltpu.make_async_copy(out_ref.at[at], out_hbm.at[at], done.at[n]))
        leaving[-1].start()
    for copy in leaving:
        copy.wait()


def mix_kernel(incoming, cols, recv_ref, msg_ref):
    sources, per_device, rows, _ = recv_ref.shape
    half = per_device // 2

    def low(x):
        return lax.broadcasted_iota(jnp.int32, x.shape, 1) < cols

    def mixed(e):
        even = jnp.concatenate([recv_ref[r, e] for r in range(0, sources, 2)], axis=0)
        odd = jnp.concatenate([recv_ref[r, e] for r in range(1, sources, 2)], axis=0)
        a = jnp.where(low(even), even, odd)
        b = jnp.where(low(even), odd, even)
        if incoming:
            x = lax.dot_general(a, b, (((0,), (0,)), ((), ())), preferred_element_type=F32)
            return pltpu.roll(x, cols, 1), x
        b = pltpu.roll(b.astype(F32), cols, 1).astype(BF16)
        x = lax.dot_general(a, b, (((1,), (1,)), ((), ())), preferred_element_type=F32)
        return x, pltpu.roll(x, cols, 1)

    for q in range(half):
        x, x_turned = mixed(q)
        y, y_turned = mixed(q + half)
        left = jnp.where(low(x), x, y_turned).astype(BF16)
        right = jnp.where(low(x), x_turned, y).astype(BF16)
        for r in range(msg_ref.shape[0] // 2):
            msg_ref[2 * r, q] = left[r * rows : (r + 1) * rows]
            msg_ref[2 * r + 1, q] = right[r * rows : (r + 1) * rows]


def call(kernel, out_shape, scratch=(), far=(0, False)):
    vmem = pl.BlockSpec(memory_space=pltpu.VMEM)
    hbm = pl.BlockSpec(memory_space=pltpu.HBM)
    far_args, far_outs = far

    def run(*args):
        args = [pltpu.with_memory_space_constraint(a, pltpu.HBM) for a in args[:far_args]] + list(args[far_args:])
        return pl.pallas_call(
            kernel,
            out_shape=out_shape,
            in_specs=[hbm] * far_args + [vmem] * (len(args) - far_args),
            out_specs=jax.tree.map(lambda _: hbm if far_outs else vmem, out_shape),
            scratch_shapes=list(scratch),
            compiler_params=pltpu.CompilerParams(vmem_limit_bytes=40 * 1024 * 1024),
        )(*args)

    return run


def by_channel(devices, pair, residue_mask, out_proj, out_gate, out_final, in_proj, in_gate, in_final):
    rows, cols, channels = pair.shape
    hidden = out_proj.shape[2]
    positions = rows * cols
    shape = jax.ShapeDtypeStruct
    near = devices // 2
    halves = [list(range(near)), list(range(near, devices))]
    exchange = functools.partial(lax.all_to_all, axis_name=("row", "col"), split_axis=0, concat_axis=0, tiled=True)
    exchange_near = functools.partial(exchange, axis_index_groups=halves)

    def messages(targets, tiles):
        return shape((targets, tiles, rows, LANES), BF16)

    plane = shape((channels, positions), F32)
    mask = residue_mask.reshape(1, -1)
    by_position = pltpu.VMEM((positions, channels), F32)
    tiles = pltpu.VMEM((positions, LANES), F32)
    weights = (channels, 5 * hidden)
    chunks = positions // CHUNK

    far = (pair.reshape(positions, channels), mask, out_proj.reshape(-1, hidden), out_gate, in_proj.reshape(-1, hidden), in_gate)
    scratch = [pltpu.VMEM(a.shape, a.dtype) for a in far] + [pltpu.VMEM(weights, BF16), pltpu.VMEM((4 * channels, hidden), F32), pltpu.SemaphoreType.DMA((chunks + 5,))]
    outs = (messages(devices, hidden // devices), plane, plane, shape((rows, LANES), F32), shape(weights, BF16))
    msg, pair_t, gating, live, weights = call(functools.partial(first_kernel, rows, cols), outs, scratch, (6, False))(*far)
    mixed = call(functools.partial(mix_kernel, False, cols), messages(devices, hidden // devices // 2))(exchange(msg))
    outs = (messages(near, hidden // near), plane, plane)
    msg, middle, gating = call(functools.partial(middle_kernel, rows, cols), outs, [tiles])(
        live, weights, out_final, exchange(mixed), pair_t, gating
    )
    mixed = call(functools.partial(mix_kernel, True, cols), messages(devices, hidden // near // 2))(exchange_near(msg))
    scratch = [tiles, by_position, pltpu.SemaphoreType.DMA((chunks,))]
    out = call(functools.partial(last_kernel, rows, cols), shape((positions, channels), F32), scratch, (0, True))(
        exchange(mixed), middle, gating, in_final
    )
    return out.reshape(rows, cols, channels)


def normalize(values, axis):
    average = jnp.mean(values, axis=axis, keepdims=True)
    centred = values - average
    variance = jnp.mean(centred * centred, axis=axis, keepdims=True)
    return centred * lax.rsqrt(variance + EPS)


def gated_panels(pair, row_live, col_live, proj):
    normed = normalize(pair, 2).astype(BF16)
    linear = jnp.einsum("ijc,cph->phij", normed, proj, preferred_element_type=F32)
    pair_mask = row_live[:, None] * col_live[None, :]
    left_panel = (pair_mask * jax.nn.sigmoid(linear[1]) * linear[0]).astype(BF16)
    right_panel = (pair_mask * jax.nn.sigmoid(linear[3]) * linear[2]).astype(BF16)
    return (normed, left_panel, right_panel)


def update_pair(pair, normed, mixed, gate_w, final_w):
    all_channels = lax.all_gather(mixed, "sub", axis=0, tiled=True)
    scaled = normalize(all_channels, 0).astype(BF16)
    projected = jnp.einsum("hij,hc->ijc", scaled, final_w, preferred_element_type=F32)
    gating = jax.nn.sigmoid(jnp.einsum("ijc,cd->ijd", normed, gate_w, preferred_element_type=F32))
    return pair + gating * projected


def by_position(pair, residue_mask, out_proj, out_gate, out_final, in_proj, in_gate, in_final):
    row_count = pair.shape[0]
    col_count = pair.shape[1]
    row_start = lax.axis_index("row") * row_count
    col_start = lax.axis_index("col") * col_count
    live = residue_mask.astype(F32)
    row_live = lax.dynamic_slice_in_dim(live, row_start, row_count, 0)
    col_live = lax.dynamic_slice_in_dim(live, col_start, col_count, 0)
    normed, left_panel, right_panel = gated_panels(pair, row_live, col_live, out_proj)
    left_rows, right_rows = (
        lax.all_gather(left_panel, "col", axis=2, tiled=True),
        lax.all_gather(right_panel, "col", axis=2, tiled=True),
    )
    turned = lax.all_to_all(right_rows, "row", split_axis=2, concat_axis=1, tiled=True)
    own_right = lax.dynamic_slice_in_dim(turned, col_start, col_count, 1)
    mixed = jnp.einsum(
        "hik,hjk->hij",
        left_rows,
        lax.all_gather(own_right, "row", axis=2, tiled=True),
        preferred_element_type=F32,
    )
    middle = update_pair(pair, normed, mixed, out_gate, out_final)
    normed, left_panel, right_panel = gated_panels(middle, row_live, col_live, in_proj)
    left_rows = lax.all_gather(left_panel, "col", axis=2, tiled=True)
    turned_left = lax.all_to_all(left_rows, "row", split_axis=2, concat_axis=1, tiled=True)
    mixed_in = jnp.einsum(
        "hki,hkj->hij",
        turned_left,
        lax.all_gather(right_panel, "row", axis=1, tiled=True),
        preferred_element_type=F32,
    )
    return update_pair(middle, normed, mixed_in, in_gate, in_final)


def local(axes, pair, residue_mask, out_proj, *rest):
    rows, cols, channels = pair.shape
    hidden = out_proj.shape[2]
    devices = axes["row"] * axes["col"]
    fits = (
        axes["sub"] == 1
        and axes["col"] == 2
        and residue_mask.shape[0] == LANES
        and cols * 2 == LANES
        and rows % 16 == 0
        and rows * cols % CHUNK == 0
        and channels == LANES
        and hidden == channels
        and hidden % (2 * devices) == 0
        and axes["row"] % 2 == 0
        and hidden % 16 == 0
    )
    plan = functools.partial(by_channel, devices) if fits else by_position
    return plan(pair, residue_mask, out_proj, *rest)


def solution(mesh):
    return jax.shard_map(
        functools.partial(local, dict(mesh.shape)),
        mesh=mesh,
        in_specs=(
            P(("groups", "row"), "col", None),
            P("groups"),
            P(None, None, "sub"),
            P(),
            P(),
            P(None, None, "sub"),
            P(),
            P(),
        ),
        out_specs=P(("groups", "row"), "col", None),
        check_vma=False,
    )
```

```python
import functools

import jax
import jax.numpy as jnp
from jax import lax
from jax.experimental import pallas as pl
from jax.experimental.pallas import tpu as pltpu
from jax.sharding import PartitionSpec as P

F32 = jnp.float32
BF16 = jnp.bfloat16
LANES = 128
CHUNK = 256
NEAR = 8
SIBLING = 2
STEPS = (0, 1, 4, 5)
EPS = 1e-05


def over_channels(values):
    centred = values - jnp.mean(values, axis=0, keepdims=True)
    variance = jnp.mean(centred * centred, axis=0, keepdims=True)
    return centred * lax.rsqrt(variance + EPS)


def product(weight, values):
    return lax.dot_general(weight, values, (((0,), (0,)), ((), ())), preferred_element_type=F32)


def side_by_side(proj_ref, gate_ref, wide, weights, order):
    channels, hidden = gate_ref.shape
    wide[...] = proj_ref[...].astype(F32)
    col = lax.axis_index("col")
    for n in range(4):
        if order == "panels":
            panel = wide[pl.ds(n + 2 * col if n < 2 else n - 2 * col, channels, stride=4), :]
        else:
            panel = wide[pl.ds(n, channels, stride=4), :]
            panel = jnp.where(col == 1, pltpu.roll(panel, hidden // 2, 1), panel)
        weights[:, n * hidden : (n + 1) * hidden] = panel.astype(BF16)
    weights[:, 4 * hidden :] = gate_ref[...]


def live_tile(mask_ref, rows, cols):
    live = mask_ref[...].astype(F32)
    lane = lax.broadcasted_iota(jnp.int32, (rows, LANES), 1)
    sub = lax.broadcasted_iota(jnp.int32, (rows, LANES), 0)
    wide = jnp.broadcast_to(live, (rows, LANES))
    mine = lane == lax.axis_index("row") * rows + sub
    row_live = jnp.sum(jnp.where(mine, wide, 0.0), axis=1, keepdims=True)
    col_live = jnp.where(lane // cols == lax.axis_index("col"), wide, pltpu.roll(wide, cols, 1))
    return row_live * col_live


def panels(normed, weights, gating_ref):
    linear = product(weights[...], normed)
    hidden = linear.shape[0] // 5
    gating_ref[...] = jax.nn.sigmoid(linear[4 * hidden :])
    first = jax.nn.sigmoid(linear[hidden : 2 * hidden]) * linear[:hidden]
    second = jax.nn.sigmoid(linear[3 * hidden : 4 * hidden]) * linear[2 * hidden : 3 * hidden]
    return first, second


def paired(first, second, live, cols):
    low = lax.broadcasted_iota(jnp.int32, (first.shape[0], LANES), 1) < cols
    by_row = []
    for t in range(live.shape[0] // 2):
        a = first[:, t * LANES : (t + 1) * LANES]
        b = second[:, t * LANES : (t + 1) * LANES]
        for tile in (jnp.where(low, a, pltpu.roll(b, cols, 1)), jnp.where(low, pltpu.roll(a, cols, 1), b)):
            row = len(by_row)
            by_row.append((tile * live[row : row + 1]).astype(BF16))
    return jnp.swapaxes(jnp.stack(by_row, axis=0), 0, 1)


def projected(recv_ref, final_ref, tiles, rows, cols):
    half = final_ref.shape[0] // 2
    values = jnp.sum(recv_ref[...].reshape(-1, half, rows, LANES).astype(F32), axis=0)
    total = jnp.sum(values, axis=0)
    centred = values - ((total + pltpu.roll(total, cols, 1)) / (2 * half))[None]
    square = jnp.sum(centred * centred, axis=0)
    variance = (square + pltpu.roll(square, cols, 1)) / (2 * half)
    tiles[: half * rows, :] = (centred * lax.rsqrt(variance + EPS)[None]).reshape(half * rows, LANES)
    low = lax.broadcasted_iota(jnp.int32, (half, LANES), 1) < cols
    parts = []
    for t in range(rows // 2):
        a = tiles[pl.ds(2 * t, half, stride=rows), :]
        b = tiles[pl.ds(2 * t + 1, half, stride=rows), :]
        upper = jnp.where(low, a, pltpu.roll(b, cols, 1))
        lower = jnp.where(low, pltpu.roll(a, cols, 1), b)
        parts.append(jnp.concatenate([upper, lower], axis=0).astype(BF16))
    return product(final_ref[...], jnp.concatenate(parts, axis=1))


def copies(pairs, done):
    started = [pltpu.make_async_copy(source, target, done.at[n]) for n, (source, target) in enumerate(pairs)]
    for copy in started:
        copy.start()
    return started


def near_index():
    return (lax.axis_index("row") * 2 + lax.axis_index("col")) % NEAR


def first_kernel(
    rows, cols, pair_hbm, mask_hbm, proj_hbm, gate_hbm, proj2_hbm, gate2_hbm,
    b_ref, keep_ref, give_ref, pair_t_ref, gating_ref, live_ref, weights2,
    pair_ref, mask_ref, proj_ref, gate_ref, proj2_ref, gate2_ref, weights, wide, by_near, done,
):
    whole = ((mask_hbm, mask_ref), (proj_hbm, proj_ref), (gate_hbm, gate_ref), (proj2_hbm, proj2_ref), (gate2_hbm, gate2_ref))
    chunks = [slice(at, at + CHUNK) for at in range(0, rows * cols, CHUNK)]
    coming = copies([(pair_hbm.at[at], pair_ref.at[at]) for at in chunks] + list(whole), done)
    for copy in coming[len(chunks) :]:
        copy.wait()
    side_by_side(proj_ref, gate_ref, wide, weights, "halves")
    side_by_side(proj2_ref, gate2_ref, wide, weights2, "panels")
    for copy in coming[: len(chunks)]:
        copy.wait()
    pair = pair_ref[...].T
    pair_t_ref[...] = pair
    live = live_tile(mask_ref, rows, cols)
    live_ref[...] = live
    a, b = panels(over_channels(pair).astype(BF16), weights, gating_ref)
    half = a.shape[0] // 2
    b_tiles = paired(b[:half], b[half:], live, cols).reshape((NEAR,) + b_ref.shape[1:])
    b_ref[:NEAR] = b_tiles
    b_ref[NEAR:] = b_tiles
    by_near[...] = paired(a[:half], a[half:], live, cols).reshape(by_near.shape)
    me = near_index()
    for n, step in enumerate(STEPS):
        keep_ref[n] = by_near[me ^ step]
        give_ref[n] = by_near[me ^ step ^ SIBLING]


def forward_kernel(keep_ref, got_ref, *out_refs):
    for n, out_ref in enumerate(out_refs):
        out_ref[0] = keep_ref[n + 1]
        out_ref[1] = got_ref[n + 1]


def middle_kernel(
    rows, cols, live_ref, weights, final_ref, recv_ref, pair_t_ref, gating_ref, msg_ref, middle_ref, gating2_ref, tiles
):
    middle = pair_t_ref[...] + gating_ref[...] * projected(recv_ref, final_ref, tiles, rows, cols)
    middle_ref[...] = middle
    a, b = panels(over_channels(middle).astype(BF16), weights, gating2_ref)
    hidden = a.shape[0]
    by_hidden = paired(a, b, live_ref[...], cols)
    devices, per_device = msg_ref.shape[:2]
    half = per_device // 2
    for d in range(devices):
        msg_ref[d, :half] = by_hidden[d * half : (d + 1) * half]
        msg_ref[d, half:] = by_hidden[hidden // 2 + d * half : hidden // 2 + (d + 1) * half]


def last_kernel(rows, cols, recv_ref, middle_ref, gating_ref, final_ref, out_hbm, tiles, out_ref, done):
    change = projected(recv_ref, final_ref, tiles, rows, cols)
    leaving = []
    for n in range(rows * cols // CHUNK):
        at = slice(n * CHUNK, (n + 1) * CHUNK)
        out_ref[at, :] = (middle_ref[:, at] + gating_ref[:, at] * change[:, at]).T
        leaving.append(pltpu.make_async_copy(out_ref.at[at], out_hbm.at[at], done.at[n]))
        leaving[-1].start()
    for copy in leaving:
        copy.wait()


def low_of(x, cols):
    return lax.broadcasted_iota(jnp.int32, x.shape, 1) < cols


def both(ref, e):
    sources = ref.shape[0]
    return [jnp.concatenate([ref[r, e] for r in range(odd, sources, 2)], axis=0) for odd in (0, 1)]


def put(left, right, msg_ref, q):
    rows = msg_ref.shape[2]
    for r in range(msg_ref.shape[0] // 2):
        msg_ref[2 * r, q] = left[r * rows : (r + 1) * rows].astype(BF16)
        msg_ref[2 * r + 1, q] = right[r * rows : (r + 1) * rows].astype(BF16)


def outgoing_kernel(cols, b_ref, keep_ref, got_ref, *refs):
    *moved_refs, msg_ref, a_ref = refs
    me = near_index()
    for n, step in enumerate(STEPS):
        own, other = (keep_ref.at[0], got_ref.at[0]) if n == 0 else (moved_refs[n - 1].at[0], moved_refs[n - 1].at[1])
        a_ref[me ^ step] = own[...]
        a_ref[me ^ step ^ SIBLING] = other[...]
    for q in range(msg_ref.shape[1]):
        even, odd = both(a_ref, q)
        low = low_of(even, cols)
        a, a2 = jnp.where(low, even, odd), jnp.where(low, odd, even)
        even, odd = both(b_ref, q)
        low = low_of(even, cols)
        b, b2 = jnp.where(low, even, odd), jnp.where(low, odd, even)
        x = lax.dot_general(a, b, (((1,), (1,)), ((), ())), preferred_element_type=F32)
        y = lax.dot_general(a2, b2, (((1,), (1,)), ((), ())), preferred_element_type=F32)
        low = low_of(x, cols)
        put(jnp.where(low, x, pltpu.roll(y, cols, 1)), jnp.where(low, pltpu.roll(x, cols, 1), y), msg_ref, q)


def incoming_kernel(cols, recv_ref, msg_ref):
    half = msg_ref.shape[1]

    def mixed(e):
        even, odd = both(recv_ref, e)
        low = low_of(even, cols)
        a, b = jnp.where(low, even, odd), jnp.where(low, odd, even)
        return lax.dot_general(a, b, (((0,), (0,)), ((), ())), preferred_element_type=F32)

    for q in range(half):
        x, y = mixed(q), mixed(q + half)
        low = low_of(x, cols)
        put(jnp.where(low, pltpu.roll(x, cols, 1), y), jnp.where(low, x, pltpu.roll(y, cols, 1)), msg_ref, q)


def call(kernel, out_shape, scratch=(), far=(0, False)):
    vmem = pl.BlockSpec(memory_space=pltpu.VMEM)
    hbm = pl.BlockSpec(memory_space=pltpu.HBM)
    far_args, far_outs = far

    def run(*args):
        args = [pltpu.with_memory_space_constraint(a, pltpu.HBM) for a in args[:far_args]] + list(args[far_args:])
        return pl.pallas_call(
            kernel,
            out_shape=out_shape,
            in_specs=[hbm] * far_args + [vmem] * (len(args) - far_args),
            out_specs=jax.tree.map(lambda _: hbm if far_outs else vmem, out_shape),
            scratch_shapes=list(scratch),
            compiler_params=pltpu.CompilerParams(vmem_limit_bytes=40 * 1024 * 1024),
        )(*args)

    return run


def by_channel(devices, pair, residue_mask, out_proj, out_gate, out_final, in_proj, in_gate, in_final):
    rows, cols, channels = pair.shape
    hidden = out_proj.shape[2]
    positions = rows * cols
    shape = jax.ShapeDtypeStruct
    axes = ("row", "col")
    halves = [list(range(NEAR)), list(range(NEAR, devices))]
    exchange = functools.partial(lax.all_to_all, axis_name=axes, split_axis=0, concat_axis=0, tiled=True)
    exchange_near = functools.partial(exchange, axis_index_groups=halves)

    def swap(values, step):
        return lax.ppermute(values, axes, [(d, d ^ step) for d in range(devices)])

    def messages(targets, tiles):
        return shape((targets, tiles, rows, LANES), BF16)

    plane = shape((channels, positions), F32)
    mask = residue_mask.reshape(1, -1)
    by_position = pltpu.VMEM((positions, channels), F32)
    tiles = pltpu.VMEM((positions, LANES), F32)
    weights = (channels, 5 * hidden)
    chunks = positions // CHUNK
    pairs = hidden // NEAR // 2
    steps = messages(len(STEPS), pairs)

    far = (pair.reshape(positions, channels), mask, out_proj.reshape(-1, hidden), out_gate, in_proj.reshape(-1, hidden), in_gate)
    outs = (messages(devices, pairs), steps, steps, plane, plane, shape((rows, LANES), F32), shape(weights, BF16))
    scratch = [pltpu.VMEM(a.shape, a.dtype) for a in far]
    scratch += [pltpu.VMEM(weights, BF16), pltpu.VMEM((4 * channels, hidden), F32)]
    scratch += [pltpu.VMEM(messages(NEAR, pairs).shape, BF16), pltpu.SemaphoreType.DMA((chunks + 5,))]
    b, keep, give, pair_t, gating, live, weights = call(functools.partial(first_kernel, rows, cols), outs, scratch, (6, False))(*far)
    b = exchange(b)
    got = swap(give, SIBLING)
    moving = call(forward_kernel, (messages(2, pairs),) * (len(STEPS) - 1))(keep, got)
    moved = [swap(block, step) for block, step in zip(moving, STEPS[1:])]
    scratch = [pltpu.VMEM(messages(NEAR, pairs).shape, BF16)]
    mixed = call(functools.partial(outgoing_kernel, cols), messages(NEAR, pairs), scratch)(b, keep, got, *moved)
    outs = (messages(NEAR, 2 * pairs), plane, plane)
    msg, middle, gating = call(functools.partial(middle_kernel, rows, cols), outs, [tiles])(
        live, weights, out_final, exchange_near(mixed), pair_t, gating
    )
    mixed = call(functools.partial(incoming_kernel, cols), messages(devices, pairs))(exchange_near(msg))
    scratch = [tiles, by_position, pltpu.SemaphoreType.DMA((chunks,))]
    out = call(functools.partial(last_kernel, rows, cols), shape((positions, channels), F32), scratch, (0, True))(
        exchange(mixed), middle, gating, in_final
    )
    return out.reshape(rows, cols, channels)


def normalize(values, axis):
    average = jnp.mean(values, axis=axis, keepdims=True)
    centred = values - average
    variance = jnp.mean(centred * centred, axis=axis, keepdims=True)
    return centred * lax.rsqrt(variance + EPS)


def gated_panels(pair, row_live, col_live, proj):
    normed = normalize(pair, 2).astype(BF16)
    linear = jnp.einsum("ijc,cph->phij", normed, proj, preferred_element_type=F32)
    pair_mask = row_live[:, None] * col_live[None, :]
    left_panel = (pair_mask * jax.nn.sigmoid(linear[1]) * linear[0]).astype(BF16)
    right_panel = (pair_mask * jax.nn.sigmoid(linear[3]) * linear[2]).astype(BF16)
    return (normed, left_panel, right_panel)


def update_pair(pair, normed, mixed, gate_w, final_w):
    all_channels = lax.all_gather(mixed, "sub", axis=0, tiled=True)
    scaled = normalize(all_channels, 0).astype(BF16)
    projected = jnp.einsum("hij,hc->ijc", scaled, final_w, preferred_element_type=F32)
    gating = jax.nn.sigmoid(jnp.einsum("ijc,cd->ijd", normed, gate_w, preferred_element_type=F32))
    return pair + gating * projected


def by_position(pair, residue_mask, out_proj, out_gate, out_final, in_proj, in_gate, in_final):
    row_count = pair.shape[0]
    col_count = pair.shape[1]
    row_start = lax.axis_index("row") * row_count
    col_start = lax.axis_index("col") * col_count
    live = residue_mask.astype(F32)
    row_live = lax.dynamic_slice_in_dim(live, row_start, row_count, 0)
    col_live = lax.dynamic_slice_in_dim(live, col_start, col_count, 0)
    normed, left_panel, right_panel = gated_panels(pair, row_live, col_live, out_proj)
    left_rows, right_rows = (
        lax.all_gather(left_panel, "col", axis=2, tiled=True),
        lax.all_gather(right_panel, "col", axis=2, tiled=True),
    )
    turned = lax.all_to_all(right_rows, "row", split_axis=2, concat_axis=1, tiled=True)
    own_right = lax.dynamic_slice_in_dim(turned, col_start, col_count, 1)
    mixed = jnp.einsum(
        "hik,hjk->hij",
        left_rows,
        lax.all_gather(own_right, "row", axis=2, tiled=True),
        preferred_element_type=F32,
    )
    middle = update_pair(pair, normed, mixed, out_gate, out_final)
    normed, left_panel, right_panel = gated_panels(middle, row_live, col_live, in_proj)
    left_rows = lax.all_gather(left_panel, "col", axis=2, tiled=True)
    turned_left = lax.all_to_all(left_rows, "row", split_axis=2, concat_axis=1, tiled=True)
    mixed_in = jnp.einsum(
        "hki,hkj->hij",
        turned_left,
        lax.all_gather(right_panel, "row", axis=1, tiled=True),
        preferred_element_type=F32,
    )
    return update_pair(middle, normed, mixed_in, in_gate, in_final)


def local(axes, pair, residue_mask, out_proj, *rest):
    rows, cols, channels = pair.shape
    hidden = out_proj.shape[2]
    devices = axes["row"] * axes["col"]
    fits = (
        axes["sub"] == 1
        and axes["col"] == 2
        and residue_mask.shape[0] == LANES
        and cols * 2 == LANES
        and rows % 16 == 0
        and rows * cols % CHUNK == 0
        and channels == LANES
        and hidden == channels
        and devices == 2 * NEAR
        and hidden % (2 * NEAR) == 0
        and hidden % 16 == 0
    )
    plan = functools.partial(by_channel, devices) if fits else by_position
    return plan(pair, residue_mask, out_proj, *rest)


def solution(mesh):
    return jax.shard_map(
        functools.partial(local, dict(mesh.shape)),
        mesh=mesh,
        in_specs=(
            P(("groups", "row"), "col", None),
            P("groups"),
            P(None, None, "sub"),
            P(),
            P(),
            P(None, None, "sub"),
            P(),
            P(),
        ),
        out_specs=P(("groups", "row"), "col", None),
        check_vma=False,
    )
```

```python
import functools

import jax
import jax.numpy as jnp
from jax import lax
from jax.experimental import pallas as pl
from jax.experimental.pallas import tpu as pltpu
from jax.sharding import PartitionSpec as P

F32 = jnp.float32
BF16 = jnp.bfloat16
LANES = 128
CHUNK = 256
NEAR = 8
SIBLING = 2
STEPS = (0, 5, 4, 1)
EPS = 1e-05


def over_channels(values):
    centred = values - jnp.mean(values, axis=0, keepdims=True)
    variance = jnp.mean(centred * centred, axis=0, keepdims=True)
    return centred * lax.rsqrt(variance + EPS)


def product(weight, values):
    return lax.dot_general(weight, values, (((0,), (0,)), ((), ())), preferred_element_type=F32)


def side_by_side(proj_ref, wide, weights, order):
    channels, hidden = weights.shape[0], weights.shape[1] // 4
    wide[...] = proj_ref[...].astype(F32)
    col = lax.axis_index("col")
    for n in range(4):
        if order == "panels":
            panel = wide[pl.ds(n + 2 * col if n < 2 else n - 2 * col, channels, stride=4), :]
        else:
            panel = wide[pl.ds(n, channels, stride=4), :]
            panel = jnp.where(col == 1, pltpu.roll(panel, hidden // 2, 1), panel)
        weights[:, n * hidden : (n + 1) * hidden] = panel.astype(BF16)


def live_tile(mask_ref, rows, cols):
    live = mask_ref[...].astype(F32)
    lane = lax.broadcasted_iota(jnp.int32, (rows, LANES), 1)
    sub = lax.broadcasted_iota(jnp.int32, (rows, LANES), 0)
    wide = jnp.broadcast_to(live, (rows, LANES))
    mine = lane == lax.axis_index("row") * rows + sub
    row_live = jnp.sum(jnp.where(mine, wide, 0.0), axis=1, keepdims=True)
    col_live = jnp.where(lane // cols == lax.axis_index("col"), wide, pltpu.roll(wide, cols, 1))
    return row_live * col_live


def panel(normed, weights, which):
    hidden = weights.shape[1] // 4
    linear = product(weights[:, 2 * which * hidden : 2 * (which + 1) * hidden], normed)
    return jax.nn.sigmoid(linear[hidden:]) * linear[:hidden]


def panels(normed, weights):
    hidden = weights.shape[1] // 4
    linear = product(weights[...], normed)
    return [jax.nn.sigmoid(linear[(p + 1) * hidden : (p + 2) * hidden]) * linear[p * hidden : (p + 1) * hidden] for p in (0, 2)]


def gate_kernel(normed_ref, gate_ref, gating_ref):
    gating_ref[...] = jax.nn.sigmoid(product(gate_ref[...], normed_ref[...]))


def paired(first, second, live, cols):
    low = lax.broadcasted_iota(jnp.int32, (first.shape[0], LANES), 1) < cols
    by_row = []
    for t in range(live.shape[0] // 2):
        a = first[:, t * LANES : (t + 1) * LANES]
        b = second[:, t * LANES : (t + 1) * LANES]
        for tile in (jnp.where(low, a, pltpu.roll(b, cols, 1)), jnp.where(low, pltpu.roll(a, cols, 1), b)):
            row = len(by_row)
            by_row.append((tile * live[row : row + 1]).astype(BF16))
    return jnp.swapaxes(jnp.stack(by_row, axis=0), 0, 1)


def projected(recv_ref, final_ref, tiles, rows, cols):
    half = final_ref.shape[0] // 2
    values = jnp.sum(recv_ref[...].reshape(-1, half, rows, LANES).astype(F32), axis=0)
    total = jnp.sum(values, axis=0)
    centred = values - ((total + pltpu.roll(total, cols, 1)) / (2 * half))[None]
    square = jnp.sum(centred * centred, axis=0)
    variance = (square + pltpu.roll(square, cols, 1)) / (2 * half)
    tiles[: half * rows, :] = (centred * lax.rsqrt(variance + EPS)[None]).reshape(half * rows, LANES)
    low = lax.broadcasted_iota(jnp.int32, (half, LANES), 1) < cols
    parts = []
    for t in range(rows // 2):
        a = tiles[pl.ds(2 * t, half, stride=rows), :]
        b = tiles[pl.ds(2 * t + 1, half, stride=rows), :]
        upper = jnp.where(low, a, pltpu.roll(b, cols, 1))
        lower = jnp.where(low, pltpu.roll(a, cols, 1), b)
        parts.append(jnp.concatenate([upper, lower], axis=0).astype(BF16))
    return product(final_ref[...], jnp.concatenate(parts, axis=1))


def copies(pairs, done):
    started = [pltpu.make_async_copy(source, target, done.at[n]) for n, (source, target) in enumerate(pairs)]
    for copy in started:
        copy.start()
    return started


def near_index():
    return (lax.axis_index("row") * 2 + lax.axis_index("col")) % NEAR


def hand_out(by_near, keep_ref, give_ref):
    me = near_index()
    for n, step in enumerate(STEPS):
        keep_ref[n] = by_near[me ^ step]
        give_ref[n] = by_near[me ^ step ^ SIBLING]


def take_in(refs, by_near):
    keep_ref, got_ref, *moved_refs = refs
    me = near_index()
    by_near[me] = keep_ref[0]
    by_near[me ^ SIBLING] = got_ref[0]
    for step, moved_ref in zip(STEPS[1:], moved_refs):
        by_near[me ^ step] = moved_ref[0]
        by_near[me ^ step ^ SIBLING] = moved_ref[1]


def first_kernel(
    rows, cols, pair_hbm, mask_hbm, proj_hbm, proj2_hbm, b_hbm, keep_ref, give_ref, pair_t_ref, normed_ref, live_ref, weights2,
    pair_ref, mask_ref, proj_ref, proj2_ref, weights, wide, b_tiles, by_near, done,
):
    chunks = [slice(at, at + CHUNK) for at in range(0, rows * cols, CHUNK)]
    whole = [(mask_hbm, mask_ref), (proj_hbm, proj_ref), (proj2_hbm, proj2_ref)]
    coming = copies([(pair_hbm.at[at], pair_ref.at[at]) for at in chunks] + whole, done)
    for copy in coming[len(chunks) :]:
        copy.wait()
    side_by_side(proj_ref, wide, weights, "halves")
    side_by_side(proj2_ref, wide, weights2, "panels")
    live = live_tile(mask_ref, rows, cols)
    live_ref[...] = live
    for copy in coming[: len(chunks)]:
        copy.wait()
    pair = pair_ref[...].T
    pair_t_ref[...] = pair
    normed = over_channels(pair).astype(BF16)
    normed_ref[...] = normed
    b = panel(normed, weights, 1)
    half = b.shape[0] // 2
    b_tiles[...] = paired(b[:half], b[half:], live, cols).reshape(b_tiles.shape)
    leaving = copies([(b_tiles, b_hbm.at[:NEAR]), (b_tiles, b_hbm.at[NEAR:])], done)
    a = panel(normed, weights, 0)
    by_near[...] = paired(a[:half], a[half:], live, cols).reshape(by_near.shape)
    hand_out(by_near, keep_ref, give_ref)
    for copy in leaving:
        copy.wait()


def forward_kernel(keep_ref, got_ref, *out_refs):
    for n, out_ref in enumerate(out_refs):
        out_ref[0] = keep_ref[n + 1]
        out_ref[1] = got_ref[n + 1]


def middle_kernel(rows, cols, live_ref, weights, final_ref, pair_t_ref, gating_ref, *refs):
    *came_refs, keep_ref, give_ref, middle_ref, normed_ref, tiles, came, by_near = refs
    take_in(came_refs, came)
    middle = pair_t_ref[...] + gating_ref[...] * projected(came, final_ref, tiles, rows, cols)
    middle_ref[...] = middle
    normed = over_channels(middle).astype(BF16)
    normed_ref[...] = normed
    a, b = panels(normed, weights)
    hidden = a.shape[0]
    by_hidden = paired(a, b, live_ref[...], cols)
    devices, per_device = by_near.shape[:2]
    half = per_device // 2
    for d in range(devices):
        by_near[d, :half] = by_hidden[d * half : (d + 1) * half]
        by_near[d, half:] = by_hidden[hidden // 2 + d * half : hidden // 2 + (d + 1) * half]
    hand_out(by_near, keep_ref, give_ref)


def last_kernel(rows, cols, recv_ref, middle_ref, gating_ref, final_ref, out_hbm, tiles, out_ref, done):
    change = projected(recv_ref, final_ref, tiles, rows, cols)
    leaving = []
    for n in range(rows * cols // CHUNK):
        at = slice(n * CHUNK, (n + 1) * CHUNK)
        out_ref[at, :] = (middle_ref[:, at] + gating_ref[:, at] * change[:, at]).T
        leaving.append(pltpu.make_async_copy(out_ref.at[at], out_hbm.at[at], done.at[n]))
        leaving[-1].start()
    for copy in leaving:
        copy.wait()


def low_of(x, cols):
    return lax.broadcasted_iota(jnp.int32, x.shape, 1) < cols


def both(ref, e):
    sources = ref.shape[0]
    return [jnp.concatenate([ref[r, e] for r in range(odd, sources, 2)], axis=0) for odd in (0, 1)]


def put(left, right, msg_ref, q):
    rows = msg_ref.shape[2]
    for r in range(msg_ref.shape[0] // 2):
        msg_ref[2 * r, q] = left[r * rows : (r + 1) * rows].astype(BF16)
        msg_ref[2 * r + 1, q] = right[r * rows : (r + 1) * rows].astype(BF16)


def outgoing_kernel(cols, b_ref, *refs):
    *came_refs, keep_ref, give_ref, a_ref, msg_ref = refs
    take_in(came_refs, a_ref)
    for q in range(msg_ref.shape[1]):
        even, odd = both(a_ref, q)
        low = low_of(even, cols)
        a, a2 = jnp.where(low, even, odd), jnp.where(low, odd, even)
        even, odd = both(b_ref, q)
        low = low_of(even, cols)
        b, b2 = jnp.where(low, even, odd), jnp.where(low, odd, even)
        x = lax.dot_general(a, b, (((1,), (1,)), ((), ())), preferred_element_type=F32)
        y = lax.dot_general(a2, b2, (((1,), (1,)), ((), ())), preferred_element_type=F32)
        low = low_of(x, cols)
        put(jnp.where(low, x, pltpu.roll(y, cols, 1)), jnp.where(low, pltpu.roll(x, cols, 1), y), msg_ref, q)
    hand_out(msg_ref, keep_ref, give_ref)


def incoming_kernel(cols, *refs):
    *came_refs, msg_ref, recv_ref = refs
    take_in(came_refs, recv_ref)
    half = msg_ref.shape[1]

    def mixed(e):
        even, odd = both(recv_ref, e)
        low = low_of(even, cols)
        a, b = jnp.where(low, even, odd), jnp.where(low, odd, even)
        return lax.dot_general(a, b, (((0,), (0,)), ((), ())), preferred_element_type=F32)

    for q in range(half):
        x, y = mixed(q), mixed(q + half)
        low = low_of(x, cols)
        put(jnp.where(low, pltpu.roll(x, cols, 1), y), jnp.where(low, x, pltpu.roll(y, cols, 1)), msg_ref, q)


def call(kernel, out_shape, scratch=(), far=(0, 0), flops=0, transcendentals=0):
    vmem = pl.BlockSpec(memory_space=pltpu.VMEM)
    hbm = pl.BlockSpec(memory_space=pltpu.HBM)
    far_args, far_outs = far

    def run(*args):
        args = [pltpu.with_memory_space_constraint(a, pltpu.HBM) for a in args[:far_args]] + list(args[far_args:])
        return pl.pallas_call(
            kernel,
            out_shape=tuple(out_shape),
            in_specs=[hbm] * far_args + [vmem] * (len(args) - far_args),
            out_specs=(hbm,) * far_outs + (vmem,) * (len(out_shape) - far_outs),
            scratch_shapes=list(scratch),
            compiler_params=pltpu.CompilerParams(vmem_limit_bytes=40 * 1024 * 1024),
            cost_estimate=pl.CostEstimate(
                flops=flops, transcendentals=transcendentals, bytes_accessed=sum(a.size * a.dtype.itemsize for a in (*args, *out_shape))
            ),
        )(*args)

    return run


def by_channel(devices, pair, residue_mask, out_proj, out_gate, out_final, in_proj, in_gate, in_final):
    rows, cols, channels = pair.shape
    hidden = out_proj.shape[2]
    positions = rows * cols
    shape = jax.ShapeDtypeStruct
    axes = ("row", "col")
    exchange = functools.partial(lax.all_to_all, axis_name=axes, split_axis=0, concat_axis=0, tiled=True)

    def swap(values, step):
        return lax.ppermute(values, axes, [(d, d ^ step) for d in range(devices)])

    def within_half(keep, give):
        got = swap(give, SIBLING)
        moving = call(forward_kernel, (shape((2,) + keep.shape[1:], BF16),) * (len(STEPS) - 1))(keep, got)
        return (keep, got, *(swap(block, step) for block, step in zip(moving, STEPS[1:])))

    def messages(targets, tiles):
        return shape((targets, tiles, rows, LANES), BF16)

    def near_tiles(tiles):
        return pltpu.VMEM(messages(NEAR, tiles).shape, BF16)

    plane = shape((channels, positions), F32)
    half_plane = shape((channels, positions), BF16)
    mask = residue_mask.reshape(1, -1)
    by_position = pltpu.VMEM((positions, channels), F32)
    tiles = pltpu.VMEM((positions, LANES), F32)
    weights = (channels, 4 * hidden)
    chunks = positions // CHUNK
    pairs = hidden // NEAR // 2
    steps = (messages(len(STEPS), pairs),) * 2
    wide_steps = (messages(len(STEPS), 2 * pairs),) * 2
    gate = call(gate_kernel, [plane], flops=2 * channels * channels * positions, transcendentals=channels * positions)

    far = (pair.reshape(positions, channels), mask, out_proj.reshape(-1, hidden), in_proj.reshape(-1, hidden))
    outs = (messages(devices, pairs), *steps, plane, half_plane, shape((rows, LANES), F32), shape(weights, BF16))
    scratch = [pltpu.VMEM(a.shape, a.dtype) for a in far]
    scratch += [pltpu.VMEM(weights, BF16), pltpu.VMEM((4 * channels, hidden), F32)]
    scratch += [near_tiles(pairs), near_tiles(pairs), pltpu.SemaphoreType.DMA((chunks + 3,))]
    b, keep, give, pair_t, normed, live, weights = call(functools.partial(first_kernel, rows, cols), outs, scratch, (4, 1))(*far)
    b = exchange(b)
    a = within_half(keep, give)
    (gating,) = gate(normed, out_gate)
    keep, give = call(functools.partial(outgoing_kernel, cols), steps, [near_tiles(pairs)] * 2)(b, *a)
    scratch = [tiles, near_tiles(pairs), near_tiles(2 * pairs)]
    keep, give, middle, normed = call(functools.partial(middle_kernel, rows, cols), (*wide_steps, plane, half_plane), scratch)(
        live, weights, out_final, pair_t, gating, *within_half(keep, give)
    )
    came = within_half(keep, give)
    gating, came = lax.optimization_barrier((gate(normed, in_gate)[0], came))
    (mixed,) = call(functools.partial(incoming_kernel, cols), [messages(devices, pairs)], [near_tiles(2 * pairs)])(*came)
    scratch = [tiles, by_position, pltpu.SemaphoreType.DMA((chunks,))]
    (out,) = call(functools.partial(last_kernel, rows, cols), [shape((positions, channels), F32)], scratch, (0, 1))(
        exchange(mixed), middle, gating, in_final
    )
    return out.reshape(rows, cols, channels)


def normalize(values, axis):
    average = jnp.mean(values, axis=axis, keepdims=True)
    centred = values - average
    variance = jnp.mean(centred * centred, axis=axis, keepdims=True)
    return centred * lax.rsqrt(variance + EPS)


def gated_panels(pair, row_live, col_live, proj):
    normed = normalize(pair, 2).astype(BF16)
    linear = jnp.einsum("ijc,cph->phij", normed, proj, preferred_element_type=F32)
    pair_mask = row_live[:, None] * col_live[None, :]
    left_panel = (pair_mask * jax.nn.sigmoid(linear[1]) * linear[0]).astype(BF16)
    right_panel = (pair_mask * jax.nn.sigmoid(linear[3]) * linear[2]).astype(BF16)
    return (normed, left_panel, right_panel)


def update_pair(pair, normed, mixed, gate_w, final_w):
    all_channels = lax.all_gather(mixed, "sub", axis=0, tiled=True)
    scaled = normalize(all_channels, 0).astype(BF16)
    projected = jnp.einsum("hij,hc->ijc", scaled, final_w, preferred_element_type=F32)
    gating = jax.nn.sigmoid(jnp.einsum("ijc,cd->ijd", normed, gate_w, preferred_element_type=F32))
    return pair + gating * projected


def by_position(pair, residue_mask, out_proj, out_gate, out_final, in_proj, in_gate, in_final):
    row_count = pair.shape[0]
    col_count = pair.shape[1]
    row_start = lax.axis_index("row") * row_count
    col_start = lax.axis_index("col") * col_count
    live = residue_mask.astype(F32)
    row_live = lax.dynamic_slice_in_dim(live, row_start, row_count, 0)
    col_live = lax.dynamic_slice_in_dim(live, col_start, col_count, 0)
    normed, left_panel, right_panel = gated_panels(pair, row_live, col_live, out_proj)
    left_rows, right_rows = (
        lax.all_gather(left_panel, "col", axis=2, tiled=True),
        lax.all_gather(right_panel, "col", axis=2, tiled=True),
    )
    turned = lax.all_to_all(right_rows, "row", split_axis=2, concat_axis=1, tiled=True)
    own_right = lax.dynamic_slice_in_dim(turned, col_start, col_count, 1)
    mixed = jnp.einsum(
        "hik,hjk->hij",
        left_rows,
        lax.all_gather(own_right, "row", axis=2, tiled=True),
        preferred_element_type=F32,
    )
    middle = update_pair(pair, normed, mixed, out_gate, out_final)
    normed, left_panel, right_panel = gated_panels(middle, row_live, col_live, in_proj)
    left_rows = lax.all_gather(left_panel, "col", axis=2, tiled=True)
    turned_left = lax.all_to_all(left_rows, "row", split_axis=2, concat_axis=1, tiled=True)
    mixed_in = jnp.einsum(
        "hki,hkj->hij",
        turned_left,
        lax.all_gather(right_panel, "row", axis=1, tiled=True),
        preferred_element_type=F32,
    )
    return update_pair(middle, normed, mixed_in, in_gate, in_final)


def local(axes, pair, residue_mask, out_proj, *rest):
    rows, cols, channels = pair.shape
    hidden = out_proj.shape[2]
    devices = axes["row"] * axes["col"]
    fits = (
        axes["sub"] == 1
        and axes["col"] == 2
        and residue_mask.shape[0] == LANES
        and cols * 2 == LANES
        and rows % 16 == 0
        and rows * cols % CHUNK == 0
        and channels == LANES
        and hidden == channels
        and devices == 2 * NEAR
        and hidden % (2 * NEAR) == 0
        and hidden % 16 == 0
    )
    plan = functools.partial(by_channel, devices) if fits else by_position
    return plan(pair, residue_mask, out_proj, *rest)


def solution(mesh):
    return jax.shard_map(
        functools.partial(local, dict(mesh.shape)),
        mesh=mesh,
        in_specs=(
            P(("groups", "row"), "col", None),
            P("groups"),
            P(None, None, "sub"),
            P(),
            P(),
            P(None, None, "sub"),
            P(),
            P(),
        ),
        out_specs=P(("groups", "row"), "col", None),
        check_vma=False,
    )
```

```python
import functools

import jax
import jax.numpy as jnp
from jax import lax
from jax.experimental import pallas as pl
from jax.experimental.pallas import tpu as pltpu
from jax.sharding import PartitionSpec as P

F32 = jnp.float32
BF16 = jnp.bfloat16
LANES = 128
CHUNK = 256
NEAR = 8
SIBLING = 2
NEAR_STEPS = (0, 5, 4, 1)
ALL_STEPS = (0, 13, 12, 5, 9, 8, 4, 1)
EPS = 1e-05


def over_channels(values):
    centred = values - jnp.mean(values, axis=0, keepdims=True)
    variance = jnp.mean(centred * centred, axis=0, keepdims=True)
    return centred * lax.rsqrt(variance + EPS)


def product(weight, values):
    return lax.dot_general(weight, values, (((0,), (0,)), ((), ())), preferred_element_type=F32)


def side_by_side(proj_ref, wide, weights, order):
    channels, hidden = weights.shape[0], weights.shape[1] // 4
    wide[...] = proj_ref[...].astype(F32)
    col = lax.axis_index("col")
    for n in range(4):
        if order == "panels":
            panel = wide[pl.ds(n + 2 * col if n < 2 else n - 2 * col, channels, stride=4), :]
        else:
            panel = wide[pl.ds(n, channels, stride=4), :]
            panel = jnp.where(col == 1, pltpu.roll(panel, hidden // 2, 1), panel)
        weights[:, n * hidden : (n + 1) * hidden] = panel.astype(BF16)


def live_tile(mask_ref, rows, cols):
    live = mask_ref[...].astype(F32)
    lane = lax.broadcasted_iota(jnp.int32, (rows, LANES), 1)
    sub = lax.broadcasted_iota(jnp.int32, (rows, LANES), 0)
    wide = jnp.broadcast_to(live, (rows, LANES))
    mine = lane == lax.axis_index("row") * rows + sub
    row_live = jnp.sum(jnp.where(mine, wide, 0.0), axis=1, keepdims=True)
    col_live = jnp.where(lane // cols == lax.axis_index("col"), wide, pltpu.roll(wide, cols, 1))
    return row_live * col_live


def panels(normed, weights):
    hidden = weights.shape[1] // 4
    linear = product(weights[...], normed)
    return [jax.nn.sigmoid(linear[(p + 1) * hidden : (p + 2) * hidden]) * linear[p * hidden : (p + 1) * hidden] for p in (0, 2)]


def gate_kernel(normed_ref, gate_ref, gating_ref):
    gating_ref[...] = jax.nn.sigmoid(product(gate_ref[...], normed_ref[...]))


def paired(first, second, live, cols):
    low = lax.broadcasted_iota(jnp.int32, (first.shape[0], LANES), 1) < cols
    by_row = []
    for t in range(live.shape[0] // 2):
        a = first[:, t * LANES : (t + 1) * LANES]
        b = second[:, t * LANES : (t + 1) * LANES]
        for tile in (jnp.where(low, a, pltpu.roll(b, cols, 1)), jnp.where(low, pltpu.roll(a, cols, 1), b)):
            row = len(by_row)
            by_row.append((tile * live[row : row + 1]).astype(BF16))
    return jnp.swapaxes(jnp.stack(by_row, axis=0), 0, 1)


def projected(recv_ref, final_ref, tiles, rows, cols):
    half = final_ref.shape[0] // 2
    values = jnp.sum(recv_ref[...].reshape(-1, half, rows, LANES).astype(F32), axis=0)
    total = jnp.sum(values, axis=0)
    centred = values - ((total + pltpu.roll(total, cols, 1)) / (2 * half))[None]
    square = jnp.sum(centred * centred, axis=0)
    variance = (square + pltpu.roll(square, cols, 1)) / (2 * half)
    tiles[: half * rows, :] = (centred * lax.rsqrt(variance + EPS)[None]).reshape(half * rows, LANES)
    low = lax.broadcasted_iota(jnp.int32, (half, LANES), 1) < cols
    parts = []
    for t in range(rows // 2):
        a = tiles[pl.ds(2 * t, half, stride=rows), :]
        b = tiles[pl.ds(2 * t + 1, half, stride=rows), :]
        upper = jnp.where(low, a, pltpu.roll(b, cols, 1))
        lower = jnp.where(low, pltpu.roll(a, cols, 1), b)
        parts.append(jnp.concatenate([upper, lower], axis=0).astype(BF16))
    return product(final_ref[...], jnp.concatenate(parts, axis=1))


def copies(pairs, done):
    started = [pltpu.make_async_copy(source, target, done.at[n]) for n, (source, target) in enumerate(pairs)]
    for copy in started:
        copy.start()
    return started


def own_index():
    return lax.axis_index("row") * 2 + lax.axis_index("col")


def hand_out(tiles, steps, keep_ref, give_ref):
    me = own_index()
    count = tiles.shape[0]
    for n, step in enumerate(steps):
        keep_ref[n] = tiles[(me ^ step) % count]
        give_ref[n] = tiles[(me ^ step ^ SIBLING) % count]


def forward_kernel(keep_ref, got_ref, *out_refs):
    for n, out_ref in enumerate(out_refs):
        out_ref[0] = keep_ref[n + 1]
        out_ref[1] = got_ref[n + 1]


def take_in(refs, steps, tiles):
    keep_ref, got_ref, *moved_refs = refs
    me = own_index()
    count = tiles.shape[0]
    tiles[me % count] = keep_ref[0]
    tiles[(me ^ SIBLING) % count] = got_ref[0]
    for step, moved_ref in zip(steps[1:], moved_refs):
        tiles[(me ^ step) % count] = moved_ref[0]
        tiles[(me ^ step ^ SIBLING) % count] = moved_ref[1]


def forward_panels_kernel(keep_ref, got_ref, *out_refs):
    for step, out_ref in zip(ALL_STEPS[1:], out_refs):
        n = NEAR_STEPS.index(step % NEAR)
        for core, ref in enumerate((keep_ref, got_ref)):
            if step < NEAR:
                out_ref[core, 0] = ref[0, n]
                out_ref[core, 1] = ref[1, n]
            else:
                out_ref[core] = ref[1, n]


def take_in_panels(refs, a_tiles, b_tiles):
    keep_ref, got_ref, *moved_refs = refs
    me = own_index()
    for step, ref in ((0, keep_ref), (SIBLING, got_ref)):
        a_tiles[(me ^ step) % NEAR] = ref[0, 0]
        b_tiles[me ^ step] = ref[1, 0]
    for step, moved_ref in zip(ALL_STEPS[1:], moved_refs):
        for core, source in enumerate((me ^ step, me ^ step ^ SIBLING)):
            if step < NEAR:
                a_tiles[source % NEAR] = moved_ref[core, 0]
                b_tiles[source] = moved_ref[core, 1]
            else:
                b_tiles[source] = moved_ref[core]


def first_kernel(
    rows, cols, pair_hbm, mask_hbm, proj_hbm, proj2_hbm, keep_ref, give_ref, pair_t_ref, normed_ref, live_ref, weights2,
    pair_ref, mask_ref, proj_ref, proj2_ref, weights, wide, by_near, done,
):
    chunks = [slice(at, at + CHUNK) for at in range(0, rows * cols, CHUNK)]
    whole = [(mask_hbm, mask_ref), (proj_hbm, proj_ref), (proj2_hbm, proj2_ref)]
    coming = copies([(pair_hbm.at[at], pair_ref.at[at]) for at in chunks] + whole, done)
    for copy in coming[len(chunks) :]:
        copy.wait()
    side_by_side(proj_ref, wide, weights, "halves")
    side_by_side(proj2_ref, wide, weights2, "panels")
    live = live_tile(mask_ref, rows, cols)
    live_ref[...] = live
    for copy in coming[: len(chunks)]:
        copy.wait()
    pair = pair_ref[...].T
    pair_t_ref[...] = pair
    normed = over_channels(pair).astype(BF16)
    normed_ref[...] = normed
    for n, values in enumerate(panels(normed, weights)):
        half = values.shape[0] // 2
        by_near[...] = paired(values[:half], values[half:], live, cols).reshape(by_near.shape)
        hand_out(by_near, NEAR_STEPS, keep_ref.at[n], give_ref.at[n])


def middle_kernel(rows, cols, live_ref, weights, final_ref, pair_t_ref, gating_ref, *refs):
    *came_refs, keep_ref, give_ref, middle_ref, normed_ref, tiles, came, by_near = refs
    take_in(came_refs, NEAR_STEPS, came)
    middle = pair_t_ref[...] + gating_ref[...] * projected(came, final_ref, tiles, rows, cols)
    middle_ref[...] = middle
    normed = over_channels(middle).astype(BF16)
    normed_ref[...] = normed
    a, b = panels(normed, weights)
    hidden = a.shape[0]
    by_hidden = paired(a, b, live_ref[...], cols)
    devices, per_device = by_near.shape[:2]
    half = per_device // 2
    for d in range(devices):
        by_near[d, :half] = by_hidden[d * half : (d + 1) * half]
        by_near[d, half:] = by_hidden[hidden // 2 + d * half : hidden // 2 + (d + 1) * half]
    hand_out(by_near, NEAR_STEPS, keep_ref, give_ref)


def last_kernel(rows, cols, middle_ref, gating_ref, final_ref, *refs):
    *came_refs, out_hbm, tiles, came, out_ref, done = refs
    take_in(came_refs, ALL_STEPS, came)
    change = projected(came, final_ref, tiles, rows, cols)
    leaving = []
    for n in range(rows * cols // CHUNK):
        at = slice(n * CHUNK, (n + 1) * CHUNK)
        out_ref[at, :] = (middle_ref[:, at] + gating_ref[:, at] * change[:, at]).T
        leaving.append(pltpu.make_async_copy(out_ref.at[at], out_hbm.at[at], done.at[n]))
        leaving[-1].start()
    for copy in leaving:
        copy.wait()


def low_of(x, cols):
    return lax.broadcasted_iota(jnp.int32, x.shape, 1) < cols


def both(ref, e):
    sources = ref.shape[0]
    return [jnp.concatenate([ref[r, e] for r in range(odd, sources, 2)], axis=0) for odd in (0, 1)]


def put(left, right, msg_ref, q):
    rows = msg_ref.shape[2]
    for r in range(msg_ref.shape[0] // 2):
        msg_ref[2 * r, q] = left[r * rows : (r + 1) * rows].astype(BF16)
        msg_ref[2 * r + 1, q] = right[r * rows : (r + 1) * rows].astype(BF16)


def outgoing_kernel(cols, *refs):
    *came_refs, keep_ref, give_ref, a_ref, b_ref, msg_ref = refs
    take_in_panels(came_refs, a_ref, b_ref)
    for q in range(msg_ref.shape[1]):
        even, odd = both(a_ref, q)
        low = low_of(even, cols)
        a, a2 = jnp.where(low, even, odd), jnp.where(low, odd, even)
        even, odd = both(b_ref, q)
        low = low_of(even, cols)
        b, b2 = jnp.where(low, even, odd), jnp.where(low, odd, even)
        x = lax.dot_general(a, b, (((1,), (1,)), ((), ())), preferred_element_type=F32)
        y = lax.dot_general(a2, b2, (((1,), (1,)), ((), ())), preferred_element_type=F32)
        low = low_of(x, cols)
        put(jnp.where(low, x, pltpu.roll(y, cols, 1)), jnp.where(low, pltpu.roll(x, cols, 1), y), msg_ref, q)
    hand_out(msg_ref, NEAR_STEPS, keep_ref, give_ref)


def incoming_kernel(cols, *refs):
    *came_refs, keep_ref, give_ref, recv_ref, msg_ref = refs
    take_in(came_refs, NEAR_STEPS, recv_ref)
    half = msg_ref.shape[1]

    def mixed(e):
        even, odd = both(recv_ref, e)
        low = low_of(even, cols)
        a, b = jnp.where(low, even, odd), jnp.where(low, odd, even)
        return lax.dot_general(a, b, (((0,), (0,)), ((), ())), preferred_element_type=F32)

    for q in range(half):
        x, y = mixed(q), mixed(q + half)
        low = low_of(x, cols)
        put(jnp.where(low, pltpu.roll(x, cols, 1), y), jnp.where(low, x, pltpu.roll(y, cols, 1)), msg_ref, q)
    hand_out(msg_ref, ALL_STEPS, keep_ref, give_ref)


def call(kernel, out_shape, scratch=(), far=(0, 0), flops=0, transcendentals=0):
    vmem = pl.BlockSpec(memory_space=pltpu.VMEM)
    hbm = pl.BlockSpec(memory_space=pltpu.HBM)
    far_args, far_outs = far

    def run(*args):
        args = [pltpu.with_memory_space_constraint(a, pltpu.HBM) for a in args[:far_args]] + list(args[far_args:])
        return pl.pallas_call(
            kernel,
            out_shape=tuple(out_shape),
            in_specs=[hbm] * far_args + [vmem] * (len(args) - far_args),
            out_specs=(hbm,) * far_outs + (vmem,) * (len(out_shape) - far_outs),
            scratch_shapes=list(scratch),
            compiler_params=pltpu.CompilerParams(vmem_limit_bytes=40 * 1024 * 1024),
            cost_estimate=pl.CostEstimate(
                flops=flops, transcendentals=transcendentals, bytes_accessed=sum(a.size * a.dtype.itemsize for a in (*args, *out_shape))
            ),
        )(*args)

    return run


def by_channel(devices, pair, residue_mask, out_proj, out_gate, out_final, in_proj, in_gate, in_final):
    rows, cols, channels = pair.shape
    hidden = out_proj.shape[2]
    positions = rows * cols
    shape = jax.ShapeDtypeStruct
    axes = ("row", "col")

    def swap(values, step):
        return lax.ppermute(values, axes, [(d, d ^ step) for d in range(devices)])

    def exchange(keep, give, steps):
        got = swap(give, SIBLING)
        moving = call(forward_kernel, [shape((2,) + keep.shape[1:], BF16)] * (len(steps) - 1))(keep, got)
        return (keep, got, *(swap(block, step) for block, step in zip(moving, steps[1:])))

    def exchange_panels(keep, give):
        got = swap(give, SIBLING)
        one = keep.shape[2:]
        outs = [shape((2, 2) + one if step < NEAR else (2,) + one, BF16) for step in ALL_STEPS[1:]]
        moving = call(forward_panels_kernel, outs)(keep, got)
        return (keep, got, *(swap(block, step) for block, step in zip(moving, ALL_STEPS[1:])))

    def messages(targets, tiles):
        return shape((targets, tiles, rows, LANES), BF16)

    def scratch_tiles(targets, tiles):
        return pltpu.VMEM(messages(targets, tiles).shape, BF16)

    plane = shape((channels, positions), F32)
    half_plane = shape((channels, positions), BF16)
    mask = residue_mask.reshape(1, -1)
    by_position = pltpu.VMEM((positions, channels), F32)
    tiles = pltpu.VMEM((positions, LANES), F32)
    weights = (channels, 4 * hidden)
    chunks = positions // CHUNK
    pairs = hidden // NEAR // 2
    panel_steps = (shape((2, len(NEAR_STEPS), pairs, rows, LANES), BF16),) * 2
    near_steps = (messages(len(NEAR_STEPS), pairs),) * 2
    wide_near_steps = (messages(len(NEAR_STEPS), 2 * pairs),) * 2
    all_steps = (messages(len(ALL_STEPS), pairs),) * 2
    gate = call(gate_kernel, [plane], flops=2 * channels * channels * positions, transcendentals=channels * positions)

    far = (pair.reshape(positions, channels), mask, out_proj.reshape(-1, hidden), in_proj.reshape(-1, hidden))
    outs = (*panel_steps, plane, half_plane, shape((rows, LANES), F32), shape(weights, BF16))
    scratch = [pltpu.VMEM(a.shape, a.dtype) for a in far]
    scratch += [pltpu.VMEM(weights, BF16), pltpu.VMEM((4 * channels, hidden), F32)]
    scratch += [scratch_tiles(NEAR, pairs), pltpu.SemaphoreType.DMA((chunks + 3,))]
    keep, give, pair_t, normed, live, weights = call(functools.partial(first_kernel, rows, cols), outs, scratch, (4, 0))(*far)
    came = exchange_panels(keep, give)
    gating, came = lax.optimization_barrier((gate(normed, out_gate)[0], came))

    scratch = [scratch_tiles(NEAR, pairs), scratch_tiles(devices, pairs), scratch_tiles(NEAR, pairs)]
    keep, give = call(functools.partial(outgoing_kernel, cols), near_steps, scratch)(*came)
    came = exchange(keep, give, NEAR_STEPS)

    scratch = [tiles, scratch_tiles(NEAR, pairs), scratch_tiles(NEAR, 2 * pairs)]
    outs = (*wide_near_steps, plane, half_plane)
    keep, give, middle, normed = call(functools.partial(middle_kernel, rows, cols), outs, scratch)(
        live, weights, out_final, pair_t, gating, *came
    )
    came = exchange(keep, give, NEAR_STEPS)
    gating, came = lax.optimization_barrier((gate(normed, in_gate)[0], came))

    scratch = [scratch_tiles(NEAR, 2 * pairs), scratch_tiles(devices, pairs)]
    keep, give = call(functools.partial(incoming_kernel, cols), all_steps, scratch)(*came)
    came = exchange(keep, give, ALL_STEPS)

    scratch = [tiles, scratch_tiles(devices, pairs), by_position, pltpu.SemaphoreType.DMA((chunks,))]
    outs = [shape((positions, channels), F32)]
    (out,) = call(functools.partial(last_kernel, rows, cols), outs, scratch, (0, 1))(middle, gating, in_final, *came)
    return out.reshape(rows, cols, channels)


def normalize(values, axis):
    average = jnp.mean(values, axis=axis, keepdims=True)
    centred = values - average
    variance = jnp.mean(centred * centred, axis=axis, keepdims=True)
    return centred * lax.rsqrt(variance + EPS)


def gated_panels(pair, row_live, col_live, proj):
    normed = normalize(pair, 2).astype(BF16)
    linear = jnp.einsum("ijc,cph->phij", normed, proj, preferred_element_type=F32)
    pair_mask = row_live[:, None] * col_live[None, :]
    left_panel = (pair_mask * jax.nn.sigmoid(linear[1]) * linear[0]).astype(BF16)
    right_panel = (pair_mask * jax.nn.sigmoid(linear[3]) * linear[2]).astype(BF16)
    return (normed, left_panel, right_panel)


def update_pair(pair, normed, mixed, gate_w, final_w):
    all_channels = lax.all_gather(mixed, "sub", axis=0, tiled=True)
    scaled = normalize(all_channels, 0).astype(BF16)
    projected = jnp.einsum("hij,hc->ijc", scaled, final_w, preferred_element_type=F32)
    gating = jax.nn.sigmoid(jnp.einsum("ijc,cd->ijd", normed, gate_w, preferred_element_type=F32))
    return pair + gating * projected


def by_position(pair, residue_mask, out_proj, out_gate, out_final, in_proj, in_gate, in_final):
    row_count = pair.shape[0]
    col_count = pair.shape[1]
    row_start = lax.axis_index("row") * row_count
    col_start = lax.axis_index("col") * col_count
    live = residue_mask.astype(F32)
    row_live = lax.dynamic_slice_in_dim(live, row_start, row_count, 0)
    col_live = lax.dynamic_slice_in_dim(live, col_start, col_count, 0)
    normed, left_panel, right_panel = gated_panels(pair, row_live, col_live, out_proj)
    left_rows, right_rows = (
        lax.all_gather(left_panel, "col", axis=2, tiled=True),
        lax.all_gather(right_panel, "col", axis=2, tiled=True),
    )
    turned = lax.all_to_all(right_rows, "row", split_axis=2, concat_axis=1, tiled=True)
    own_right = lax.dynamic_slice_in_dim(turned, col_start, col_count, 1)
    mixed = jnp.einsum(
        "hik,hjk->hij",
        left_rows,
        lax.all_gather(own_right, "row", axis=2, tiled=True),
        preferred_element_type=F32,
    )
    middle = update_pair(pair, normed, mixed, out_gate, out_final)
    normed, left_panel, right_panel = gated_panels(middle, row_live, col_live, in_proj)
    left_rows = lax.all_gather(left_panel, "col", axis=2, tiled=True)
    turned_left = lax.all_to_all(left_rows, "row", split_axis=2, concat_axis=1, tiled=True)
    mixed_in = jnp.einsum(
        "hki,hkj->hij",
        turned_left,
        lax.all_gather(right_panel, "row", axis=1, tiled=True),
        preferred_element_type=F32,
    )
    return update_pair(middle, normed, mixed_in, in_gate, in_final)


def local(axes, pair, residue_mask, out_proj, *rest):
    rows, cols, channels = pair.shape
    hidden = out_proj.shape[2]
    devices = axes["row"] * axes["col"]
    fits = (
        axes["sub"] == 1
        and axes["col"] == 2
        and residue_mask.shape[0] == LANES
        and cols * 2 == LANES
        and rows % 16 == 0
        and rows * cols % CHUNK == 0
        and channels == LANES
        and hidden == channels
        and devices == 2 * NEAR
        and hidden % (2 * NEAR) == 0
        and hidden % 16 == 0
    )
    plan = functools.partial(by_channel, devices) if fits else by_position
    return plan(pair, residue_mask, out_proj, *rest)


def solution(mesh):
    return jax.shard_map(
        functools.partial(local, dict(mesh.shape)),
        mesh=mesh,
        in_specs=(
            P(("groups", "row"), "col", None),
            P("groups"),
            P(None, None, "sub"),
            P(),
            P(),
            P(None, None, "sub"),
            P(),
            P(),
        ),
        out_specs=P(("groups", "row"), "col", None),
        check_vma=False,
    )
```

```python
import functools

import jax
import jax.numpy as jnp
from jax import lax
from jax.experimental import pallas as pl
from jax.experimental.pallas import tpu as pltpu
from jax.sharding import PartitionSpec as P

F32 = jnp.float32
BF16 = jnp.bfloat16
LANES = 128
CHUNK = 256
NEAR = 8
SIBLING = 2
NEAR_STEPS = (0, 5, 4, 1)
ALL_STEPS = (0, 13, 12, 5, 9, 8, 4, 1)
CHIPS = len(NEAR_STEPS)
EPS = 1e-05


def over_channels(values):
    centred = values - jnp.mean(values, axis=0, keepdims=True)
    variance = jnp.mean(centred * centred, axis=0, keepdims=True)
    return centred * lax.rsqrt(variance + EPS)


def product(weight, values):
    return lax.dot_general(weight, values, (((0,), (0,)), ((), ())), preferred_element_type=F32)


def side_by_side(proj_ref, wide, weights, order):
    channels, hidden = weights.shape[0], weights.shape[1] // 4
    wide[...] = proj_ref[...].astype(F32)
    col = lax.axis_index("col")
    for n in range(4):
        if order == "panels":
            panel = wide[pl.ds(n + 2 * col if n < 2 else n - 2 * col, channels, stride=4), :]
        else:
            panel = wide[pl.ds(n, channels, stride=4), :]
            panel = jnp.where(col == 1, pltpu.roll(panel, hidden // 2, 1), panel)
        weights[:, n * hidden : (n + 1) * hidden] = panel.astype(BF16)


def live_tile(mask_ref, rows, cols):
    live = mask_ref[...].astype(F32)
    lane = lax.broadcasted_iota(jnp.int32, (rows, LANES), 1)
    sub = lax.broadcasted_iota(jnp.int32, (rows, LANES), 0)
    wide = jnp.broadcast_to(live, (rows, LANES))
    mine = lane == lax.axis_index("row") * rows + sub
    row_live = jnp.sum(jnp.where(mine, wide, 0.0), axis=1, keepdims=True)
    col_live = jnp.where(lane // cols == lax.axis_index("col"), wide, pltpu.roll(wide, cols, 1))
    return row_live * col_live


def panels(normed, weights):
    hidden = weights.shape[1] // 4
    linear = product(weights[...], normed)
    return [jax.nn.sigmoid(linear[(p + 1) * hidden : (p + 2) * hidden]) * linear[p * hidden : (p + 1) * hidden] for p in (0, 2)]


def gate_kernel(normed_ref, gate_ref, gating_ref):
    gating_ref[...] = jax.nn.sigmoid(product(gate_ref[...], normed_ref[...]))


def paired(first, second, live, cols):
    low = lax.broadcasted_iota(jnp.int32, (first.shape[0], LANES), 1) < cols
    by_row = []
    for t in range(live.shape[0] // 2):
        a = first[:, t * LANES : (t + 1) * LANES]
        b = second[:, t * LANES : (t + 1) * LANES]
        for tile in (jnp.where(low, a, pltpu.roll(b, cols, 1)), jnp.where(low, pltpu.roll(a, cols, 1), b)):
            row = len(by_row)
            by_row.append((tile * live[row : row + 1]).astype(BF16))
    return jnp.swapaxes(jnp.stack(by_row, axis=0), 0, 1)


def projected(recv_ref, final_ref, tiles, rows, cols):
    half = final_ref.shape[0] // 2
    values = jnp.sum(recv_ref[...].reshape(-1, half, rows, LANES).astype(F32), axis=0)
    total = jnp.sum(values, axis=0)
    centred = values - ((total + pltpu.roll(total, cols, 1)) / (2 * half))[None]
    square = jnp.sum(centred * centred, axis=0)
    variance = (square + pltpu.roll(square, cols, 1)) / (2 * half)
    tiles[: half * rows, :] = (centred * lax.rsqrt(variance + EPS)[None]).reshape(half * rows, LANES)
    low = lax.broadcasted_iota(jnp.int32, (half, LANES), 1) < cols
    parts = []
    for t in range(rows // 2):
        a = tiles[pl.ds(2 * t, half, stride=rows), :]
        b = tiles[pl.ds(2 * t + 1, half, stride=rows), :]
        upper = jnp.where(low, a, pltpu.roll(b, cols, 1))
        lower = jnp.where(low, pltpu.roll(a, cols, 1), b)
        parts.append(jnp.concatenate([upper, lower], axis=0).astype(BF16))
    return product(final_ref[...], jnp.concatenate(parts, axis=1))


def copies(pairs, done):
    started = [pltpu.make_async_copy(source, target, done.at[n]) for n, (source, target) in enumerate(pairs)]
    for copy in started:
        copy.start()
    return started


def own_index():
    return lax.axis_index("row") * 2 + lax.axis_index("col")


def hand_out(tiles, steps, keep_ref, give_ref):
    me = own_index()
    count = tiles.shape[0]
    for n, step in enumerate(steps):
        keep_ref[n] = tiles[(me ^ step) % count]
        give_ref[n] = tiles[(me ^ step ^ SIBLING) % count]


def forward_kernel(keep_ref, got_ref, *out_refs):
    for n, out_ref in enumerate(out_refs):
        out_ref[0] = keep_ref[n + 1]
        out_ref[1] = got_ref[n + 1]


def take_in(refs, steps, tiles):
    keep_ref, got_ref, *moved_refs = refs
    me = own_index()
    count = tiles.shape[0]
    tiles[me % count] = keep_ref[0]
    tiles[(me ^ SIBLING) % count] = got_ref[0]
    for step, moved_ref in zip(steps[1:], moved_refs):
        tiles[(me ^ step) % count] = moved_ref[0]
        tiles[(me ^ step ^ SIBLING) % count] = moved_ref[1]


def chip_blocks(tiles, index):
    base = (index % tiles.shape[0]) & ~SIBLING
    return base, base | SIBLING


def chip_of(index):
    return (index // 4 % 2) * 2 + index % 2


def all_b_kernel(*refs):
    *came_refs, out_ref = refs
    for n, ref in enumerate(came_refs):
        out_ref[n] = ref[1] if n < CHIPS else ref[...]


def first_kernel(rows, cols, pair_hbm, mask_hbm, proj_hbm, proj2_hbm, *refs):
    both_refs, b_refs = refs[:CHIPS], refs[CHIPS : 2 * CHIPS]
    pair_t_ref, normed_ref, live_ref, weights2 = refs[2 * CHIPS : 2 * CHIPS + 4]
    pair_ref, mask_ref, proj_ref, proj2_ref, weights, wide, by_near, done = refs[2 * CHIPS + 4 :]
    chunks = [slice(at, at + CHUNK) for at in range(0, rows * cols, CHUNK)]
    whole = [(mask_hbm, mask_ref), (proj_hbm, proj_ref), (proj2_hbm, proj2_ref)]
    coming = copies([(pair_hbm.at[at], pair_ref.at[at]) for at in chunks] + whole, done)
    for copy in coming[len(chunks) :]:
        copy.wait()
    side_by_side(proj_ref, wide, weights, "halves")
    side_by_side(proj2_ref, wide, weights2, "panels")
    live = live_tile(mask_ref, rows, cols)
    live_ref[...] = live
    for copy in coming[: len(chunks)]:
        copy.wait()
    pair = pair_ref[...].T
    pair_t_ref[...] = pair
    normed = over_channels(pair).astype(BF16)
    normed_ref[...] = normed
    for p, values in enumerate(panels(normed, weights)):
        half = values.shape[0] // 2
        by_near[...] = paired(values[:half], values[half:], live, cols).reshape(by_near.shape)
        for step, both_ref, b_ref in zip(NEAR_STEPS, both_refs, b_refs):
            for n, block in enumerate(chip_blocks(by_near, own_index() ^ step)):
                both_ref[p, n] = by_near[block]
                if p == 1:
                    b_ref[n] = by_near[block]


def middle_kernel(rows, cols, live_ref, weights, final_ref, pair_t_ref, gating_ref, *refs):
    *came_refs, keep_ref, give_ref, middle_ref, normed_ref, tiles, came, by_near = refs
    for step, ref in zip(NEAR_STEPS, came_refs):
        for n, block in enumerate(chip_blocks(came, own_index() ^ step)):
            came[block] = ref[n]
    middle = pair_t_ref[...] + gating_ref[...] * projected(came, final_ref, tiles, rows, cols)
    middle_ref[...] = middle
    normed = over_channels(middle).astype(BF16)
    normed_ref[...] = normed
    a, b = panels(normed, weights)
    hidden = a.shape[0]
    by_hidden = paired(a, b, live_ref[...], cols)
    devices, per_device = by_near.shape[:2]
    half = per_device // 2
    for d in range(devices):
        by_near[d, :half] = by_hidden[d * half : (d + 1) * half]
        by_near[d, half:] = by_hidden[hidden // 2 + d * half : hidden // 2 + (d + 1) * half]
    hand_out(by_near, NEAR_STEPS, keep_ref, give_ref)


def last_kernel(rows, cols, middle_ref, gating_ref, final_ref, *refs):
    *came_refs, out_hbm, tiles, came, out_ref, done = refs
    take_in(came_refs, ALL_STEPS, came)
    change = projected(came, final_ref, tiles, rows, cols)
    leaving = []
    for n in range(rows * cols // CHUNK):
        at = slice(n * CHUNK, (n + 1) * CHUNK)
        out_ref[at, :] = (middle_ref[:, at] + gating_ref[:, at] * change[:, at]).T
        leaving.append(pltpu.make_async_copy(out_ref.at[at], out_hbm.at[at], done.at[n]))
        leaving[-1].start()
    for copy in leaving:
        copy.wait()


def low_of(x, cols):
    return lax.broadcasted_iota(jnp.int32, x.shape, 1) < cols


def both(ref, e):
    sources = ref.shape[0]
    return [jnp.concatenate([ref[r, e] for r in range(odd, sources, 2)], axis=0) for odd in (0, 1)]


def put(left, right, msg_ref, q):
    rows = msg_ref.shape[2]
    for r in range(msg_ref.shape[0] // 2):
        msg_ref[2 * r, q] = left[r * rows : (r + 1) * rows].astype(BF16)
        msg_ref[2 * r + 1, q] = right[r * rows : (r + 1) * rows].astype(BF16)


def outgoing_kernel(cols, *refs):
    both_refs, far_refs, sibling_ref = refs[:CHIPS], refs[CHIPS : 2 * CHIPS], refs[2 * CHIPS]
    *out_refs, a_ref, b_ref, msg_ref = refs[2 * CHIPS + 1 :]
    me = own_index()
    one = a_ref.shape[1:]
    for n, step in enumerate(NEAR_STEPS):
        a_ref[chip_of(me ^ step)] = both_refs[n][0].reshape(one)
        b_ref[me ^ step] = both_refs[n][1].reshape(one)
        b_ref[me ^ step ^ SIBLING] = sibling_ref[n].reshape(one)
        b_ref[me ^ step ^ NEAR] = far_refs[n][...].reshape(one)
        b_ref[me ^ step ^ NEAR ^ SIBLING] = sibling_ref[CHIPS + n].reshape(one)
    for q in range(msg_ref.shape[1]):
        even, odd = both(a_ref, q)
        low = low_of(even, cols)
        a, a2 = jnp.where(low, even, odd), jnp.where(low, odd, even)
        even, odd = both(b_ref, q)
        low = low_of(even, cols)
        b, b2 = jnp.where(low, even, odd), jnp.where(low, odd, even)
        x = lax.dot_general(a, b, (((1,), (1,)), ((), ())), preferred_element_type=F32)
        y = lax.dot_general(a2, b2, (((1,), (1,)), ((), ())), preferred_element_type=F32)
        low = low_of(x, cols)
        put(jnp.where(low, x, pltpu.roll(y, cols, 1)), jnp.where(low, pltpu.roll(x, cols, 1), y), msg_ref, q)
    for step, out_ref in zip(NEAR_STEPS, out_refs):
        out_ref[...] = msg_ref[chip_of(me ^ step)].reshape(out_ref.shape)


def incoming_kernel(cols, *refs):
    *came_refs, keep_ref, give_ref, recv_ref, msg_ref = refs
    take_in(came_refs, NEAR_STEPS, recv_ref)
    half = msg_ref.shape[1]

    def mixed(e):
        even, odd = both(recv_ref, e)
        low = low_of(even, cols)
        a, b = jnp.where(low, even, odd), jnp.where(low, odd, even)
        return lax.dot_general(a, b, (((0,), (0,)), ((), ())), preferred_element_type=F32)

    for q in range(half):
        x, y = mixed(q), mixed(q + half)
        low = low_of(x, cols)
        put(jnp.where(low, pltpu.roll(x, cols, 1), y), jnp.where(low, x, pltpu.roll(y, cols, 1)), msg_ref, q)
    hand_out(msg_ref, ALL_STEPS, keep_ref, give_ref)


def call(kernel, out_shape, scratch=(), far=(0, 0), flops=0, transcendentals=0):
    vmem = pl.BlockSpec(memory_space=pltpu.VMEM)
    hbm = pl.BlockSpec(memory_space=pltpu.HBM)
    far_args, far_outs = far

    def run(*args):
        args = [pltpu.with_memory_space_constraint(a, pltpu.HBM) for a in args[:far_args]] + list(args[far_args:])
        return pl.pallas_call(
            kernel,
            out_shape=tuple(out_shape),
            in_specs=[hbm] * far_args + [vmem] * (len(args) - far_args),
            out_specs=(hbm,) * far_outs + (vmem,) * (len(out_shape) - far_outs),
            scratch_shapes=list(scratch),
            compiler_params=pltpu.CompilerParams(vmem_limit_bytes=40 * 1024 * 1024),
            cost_estimate=pl.CostEstimate(
                flops=flops, transcendentals=transcendentals, bytes_accessed=sum(a.size * a.dtype.itemsize for a in (*args, *out_shape))
            ),
        )(*args)

    return run


def by_channel(devices, pair, residue_mask, out_proj, out_gate, out_final, in_proj, in_gate, in_final):
    rows, cols, channels = pair.shape
    hidden = out_proj.shape[2]
    positions = rows * cols
    shape = jax.ShapeDtypeStruct
    axes = ("row", "col")

    def swap(values, step):
        return lax.ppermute(values, axes, [(d, d ^ step) for d in range(devices)])

    def exchange(keep, give, steps):
        got = swap(give, SIBLING)
        moving = call(forward_kernel, [shape((2,) + keep.shape[1:], BF16)] * (len(steps) - 1))(keep, got)
        return (keep, got, *(swap(block, step) for block, step in zip(moving, steps[1:])))

    def exchange_panels(both, b):
        moved = {0: both[0]}
        for step in ALL_STEPS[1:]:
            n = NEAR_STEPS.index(step % NEAR)
            moved[step] = swap(both[n] if step < NEAR else b[n], step)
        near = [moved[step] for step in NEAR_STEPS]
        far = [moved[step ^ NEAR] for step in NEAR_STEPS]
        (all_b,) = call(all_b_kernel, [shape((2 * CHIPS,) + both[0].shape[1:], BF16)])(*near, *far)
        return (*near, *far, swap(all_b, SIBLING))

    def messages(targets, tiles):
        return shape((targets, tiles, rows, LANES), BF16)

    def scratch_tiles(targets, tiles):
        return pltpu.VMEM(messages(targets, tiles).shape, BF16)

    plane = shape((channels, positions), F32)
    half_plane = shape((channels, positions), BF16)
    mask = residue_mask.reshape(1, -1)
    by_position = pltpu.VMEM((positions, channels), F32)
    tiles = pltpu.VMEM((positions, LANES), F32)
    weights = (channels, 4 * hidden)
    chunks = positions // CHUNK
    pairs = hidden // NEAR // 2
    per_chip = (messages(2, pairs),) * CHIPS
    both_per_chip = (shape((2, 2, pairs, rows, LANES), BF16),) * CHIPS
    wide_near_steps = (messages(len(NEAR_STEPS), 2 * pairs),) * 2
    all_steps = (messages(len(ALL_STEPS), pairs),) * 2
    gate = call(gate_kernel, [plane], flops=2 * channels * channels * positions, transcendentals=channels * positions)

    far = (pair.reshape(positions, channels), mask, out_proj.reshape(-1, hidden), in_proj.reshape(-1, hidden))
    outs = (*both_per_chip, *per_chip, plane, half_plane, shape((rows, LANES), F32), shape(weights, BF16))
    scratch = [pltpu.VMEM(a.shape, a.dtype) for a in far]
    scratch += [pltpu.VMEM(weights, BF16), pltpu.VMEM((4 * channels, hidden), F32)]
    scratch += [scratch_tiles(NEAR, pairs), pltpu.SemaphoreType.DMA((chunks + 3,))]
    outs = call(functools.partial(first_kernel, rows, cols), outs, scratch, (4, 0))(*far)
    pair_t, normed, live, weights = outs[2 * CHIPS :]
    came = exchange_panels(outs[:CHIPS], outs[CHIPS : 2 * CHIPS])
    gating, came = lax.optimization_barrier((gate(normed, out_gate)[0], came))

    scratch = [scratch_tiles(CHIPS, 2 * pairs), scratch_tiles(devices, 2 * pairs), scratch_tiles(CHIPS, 2 * pairs)]
    own, *others = call(functools.partial(outgoing_kernel, cols), per_chip, scratch)(*came)
    came = (own, *(swap(block, step) for block, step in zip(others, NEAR_STEPS[1:])))

    scratch = [tiles, scratch_tiles(NEAR, pairs), scratch_tiles(NEAR, 2 * pairs)]
    outs = (*wide_near_steps, plane, half_plane)
    keep, give, middle, normed = call(functools.partial(middle_kernel, rows, cols), outs, scratch)(
        live, weights, out_final, pair_t, gating, *came
    )
    came = exchange(keep, give, NEAR_STEPS)
    gating, came = lax.optimization_barrier((gate(normed, in_gate)[0], came))

    scratch = [scratch_tiles(NEAR, 2 * pairs), scratch_tiles(devices, pairs)]
    keep, give = call(functools.partial(incoming_kernel, cols), all_steps, scratch)(*came)
    came = exchange(keep, give, ALL_STEPS)

    scratch = [tiles, scratch_tiles(devices, pairs), by_position, pltpu.SemaphoreType.DMA((chunks,))]
    outs = [shape((positions, channels), F32)]
    (out,) = call(functools.partial(last_kernel, rows, cols), outs, scratch, (0, 1))(middle, gating, in_final, *came)
    return out.reshape(rows, cols, channels)


def normalize(values, axis):
    average = jnp.mean(values, axis=axis, keepdims=True)
    centred = values - average
    variance = jnp.mean(centred * centred, axis=axis, keepdims=True)
    return centred * lax.rsqrt(variance + EPS)


def gated_panels(pair, row_live, col_live, proj):
    normed = normalize(pair, 2).astype(BF16)
    linear = jnp.einsum("ijc,cph->phij", normed, proj, preferred_element_type=F32)
    pair_mask = row_live[:, None] * col_live[None, :]
    left_panel = (pair_mask * jax.nn.sigmoid(linear[1]) * linear[0]).astype(BF16)
    right_panel = (pair_mask * jax.nn.sigmoid(linear[3]) * linear[2]).astype(BF16)
    return (normed, left_panel, right_panel)


def update_pair(pair, normed, mixed, gate_w, final_w):
    all_channels = lax.all_gather(mixed, "sub", axis=0, tiled=True)
    scaled = normalize(all_channels, 0).astype(BF16)
    projected = jnp.einsum("hij,hc->ijc", scaled, final_w, preferred_element_type=F32)
    gating = jax.nn.sigmoid(jnp.einsum("ijc,cd->ijd", normed, gate_w, preferred_element_type=F32))
    return pair + gating * projected


def by_position(pair, residue_mask, out_proj, out_gate, out_final, in_proj, in_gate, in_final):
    row_count = pair.shape[0]
    col_count = pair.shape[1]
    row_start = lax.axis_index("row") * row_count
    col_start = lax.axis_index("col") * col_count
    live = residue_mask.astype(F32)
    row_live = lax.dynamic_slice_in_dim(live, row_start, row_count, 0)
    col_live = lax.dynamic_slice_in_dim(live, col_start, col_count, 0)
    normed, left_panel, right_panel = gated_panels(pair, row_live, col_live, out_proj)
    left_rows, right_rows = (
        lax.all_gather(left_panel, "col", axis=2, tiled=True),
        lax.all_gather(right_panel, "col", axis=2, tiled=True),
    )
    turned = lax.all_to_all(right_rows, "row", split_axis=2, concat_axis=1, tiled=True)
    own_right = lax.dynamic_slice_in_dim(turned, col_start, col_count, 1)
    mixed = jnp.einsum(
        "hik,hjk->hij",
        left_rows,
        lax.all_gather(own_right, "row", axis=2, tiled=True),
        preferred_element_type=F32,
    )
    middle = update_pair(pair, normed, mixed, out_gate, out_final)
    normed, left_panel, right_panel = gated_panels(middle, row_live, col_live, in_proj)
    left_rows = lax.all_gather(left_panel, "col", axis=2, tiled=True)
    turned_left = lax.all_to_all(left_rows, "row", split_axis=2, concat_axis=1, tiled=True)
    mixed_in = jnp.einsum(
        "hki,hkj->hij",
        turned_left,
        lax.all_gather(right_panel, "row", axis=1, tiled=True),
        preferred_element_type=F32,
    )
    return update_pair(middle, normed, mixed_in, in_gate, in_final)


def local(axes, pair, residue_mask, out_proj, *rest):
    rows, cols, channels = pair.shape
    hidden = out_proj.shape[2]
    devices = axes["row"] * axes["col"]
    fits = (
        axes["sub"] == 1
        and axes["col"] == 2
        and residue_mask.shape[0] == LANES
        and cols * 2 == LANES
        and rows % 16 == 0
        and rows * cols % CHUNK == 0
        and channels == LANES
        and hidden == channels
        and devices == 2 * NEAR
        and hidden % (2 * NEAR) == 0
        and hidden % 16 == 0
    )
    plan = functools.partial(by_channel, devices) if fits else by_position
    return plan(pair, residue_mask, out_proj, *rest)


def solution(mesh):
    return jax.shard_map(
        functools.partial(local, dict(mesh.shape)),
        mesh=mesh,
        in_specs=(
            P(("groups", "row"), "col", None),
            P("groups"),
            P(None, None, "sub"),
            P(),
            P(),
            P(None, None, "sub"),
            P(),
            P(),
        ),
        out_specs=P(("groups", "row"), "col", None),
        check_vma=False,
    )
```

```python
import functools

import jax
import jax.numpy as jnp
from jax import lax
from jax.experimental import pallas as pl
from jax.experimental.pallas import tpu as pltpu
from jax.sharding import PartitionSpec as P

F32 = jnp.float32
BF16 = jnp.bfloat16
LANES = 128
CHUNK = 512
NEAR = 8
SIBLING = 2
NEAR_STEPS = (0, 5, 4, 1)
ALL_STEPS = (0, 13, 12, 5, 9, 8, 4, 1)
CHIPS = len(NEAR_STEPS)
EPS = 1e-05


def over_channels(values):
    centred = values - jnp.mean(values, axis=0, keepdims=True)
    variance = jnp.mean(centred * centred, axis=0, keepdims=True)
    return centred * lax.rsqrt(variance + EPS)


def product(weight, values):
    return lax.dot_general(weight, values, (((0,), (0,)), ((), ())), preferred_element_type=F32)


def side_by_side(proj_ref, wide, weights, order):
    channels, hidden = weights.shape[0], weights.shape[1] // 4
    wide[...] = proj_ref[...].astype(F32)
    col = lax.axis_index("col")
    for n in range(4):
        if order == "panels":
            panel = wide[pl.ds(n + 2 * col if n < 2 else n - 2 * col, channels, stride=4), :]
        else:
            panel = wide[pl.ds(n, channels, stride=4), :]
            panel = jnp.where(col == 1, pltpu.roll(panel, hidden // 2, 1), panel)
        weights[:, n * hidden : (n + 1) * hidden] = panel.astype(BF16)


def live_tile(mask_ref, rows, cols):
    live = mask_ref[...].astype(F32)
    lane = lax.broadcasted_iota(jnp.int32, (rows, LANES), 1)
    sub = lax.broadcasted_iota(jnp.int32, (rows, LANES), 0)
    wide = jnp.broadcast_to(live, (rows, LANES))
    mine = lane == lax.axis_index("row") * rows + sub
    row_live = jnp.sum(jnp.where(mine, wide, 0.0), axis=1, keepdims=True)
    col_live = jnp.where(lane // cols == lax.axis_index("col"), wide, pltpu.roll(wide, cols, 1))
    return row_live * col_live


def panels(normed, weights):
    hidden = weights.shape[1] // 4
    linear = product(weights[...], normed)
    return [jax.nn.sigmoid(linear[(p + 1) * hidden : (p + 2) * hidden]) * linear[p * hidden : (p + 1) * hidden] for p in (0, 2)]


def gate_kernel(normed_ref, gate_ref, gating_ref):
    gating_ref[...] = jax.nn.sigmoid(product(gate_ref[...], normed_ref[...]))


def paired(first, second, live, cols):
    low = lax.broadcasted_iota(jnp.int32, (first.shape[0], LANES), 1) < cols
    by_row = []
    for t in range(live.shape[0] // 2):
        a = first[:, t * LANES : (t + 1) * LANES]
        b = second[:, t * LANES : (t + 1) * LANES]
        for tile in (jnp.where(low, a, pltpu.roll(b, cols, 1)), jnp.where(low, pltpu.roll(a, cols, 1), b)):
            row = len(by_row)
            by_row.append((tile * live[row : row + 1]).astype(BF16))
    return jnp.swapaxes(jnp.stack(by_row, axis=0), 0, 1)


def summed(values):
    chains = values.reshape((values.shape[0] // 8, 8) + values.shape[1:])
    return jnp.sum(jnp.sum(chains, axis=0), axis=0)


def projected(recv_ref, final_ref, rows, cols):
    half = final_ref.shape[0] // 2
    values = jnp.sum(recv_ref[...].reshape(-1, half, rows, LANES).astype(F32), axis=0)
    total = summed(values)
    centred = values - ((total + pltpu.roll(total, cols, 1)) / (2 * half))[None]
    square = summed(centred * centred)
    variance = (square + pltpu.roll(square, cols, 1)) / (2 * half)
    scaled = jnp.swapaxes((centred * lax.rsqrt(variance + EPS)[None]).astype(BF16), 0, 1).astype(F32)
    low = lax.broadcasted_iota(jnp.int32, (half, LANES), 1) < cols
    parts = []
    for t in range(rows // 2):
        a, b = scaled[2 * t], scaled[2 * t + 1]
        upper = jnp.where(low, a, pltpu.roll(b, cols, 1))
        lower = jnp.where(low, pltpu.roll(a, cols, 1), b)
        parts.append(jnp.concatenate([upper, lower], axis=0).astype(BF16))
    return product(final_ref[...], jnp.concatenate(parts, axis=1))


def copies(pairs, done):
    started = [pltpu.make_async_copy(source, target, done.at[n]) for n, (source, target) in enumerate(pairs)]
    for copy in started:
        copy.start()
    return started


def own_index():
    return lax.axis_index("row") * 2 + lax.axis_index("col")


def hand_out(tiles, steps, keep_ref, give_ref):
    me = own_index()
    count = tiles.shape[0]
    for n, step in enumerate(steps):
        keep_ref[n] = tiles[(me ^ step) % count]
        give_ref[n] = tiles[(me ^ step ^ SIBLING) % count]


def forward_kernel(keep_ref, got_ref, *out_refs):
    for n, out_ref in enumerate(out_refs):
        out_ref[0] = keep_ref[n + 1]
        out_ref[1] = got_ref[n + 1]


def take_in(refs, steps, tiles):
    keep_ref, got_ref, *moved_refs = refs
    me = own_index()
    count = tiles.shape[0]
    tiles[me % count] = keep_ref[0]
    tiles[(me ^ SIBLING) % count] = got_ref[0]
    for step, moved_ref in zip(steps[1:], moved_refs):
        tiles[(me ^ step) % count] = moved_ref[0]
        tiles[(me ^ step ^ SIBLING) % count] = moved_ref[1]


def chip_blocks(tiles, index):
    base = (index % tiles.shape[0]) & ~SIBLING
    return base, base | SIBLING


def chip_of(index):
    return (index // 4 % 2) * 2 + index % 2


def all_b_kernel(*refs):
    *came_refs, out_ref = refs
    for n, ref in enumerate(came_refs):
        out_ref[n] = ref[1] if n < CHIPS else ref[...]


def second_weights_kernel(proj_ref, weights, wide):
    side_by_side(proj_ref, wide, weights, "panels")


def first_kernel(rows, cols, pair_hbm, mask_hbm, proj_hbm, *refs):
    both_refs, b_refs = refs[:CHIPS], refs[CHIPS : 2 * CHIPS]
    pair_t_ref, normed_ref, live_ref = refs[2 * CHIPS : 2 * CHIPS + 3]
    pair_ref, mask_ref, proj_ref, weights, wide, by_near, done = refs[2 * CHIPS + 3 :]
    chunks = [slice(at, at + CHUNK) for at in range(0, rows * cols, CHUNK)]
    whole = [(mask_hbm, mask_ref), (proj_hbm, proj_ref)]
    coming = copies([(pair_hbm.at[at], pair_ref.at[at]) for at in chunks] + whole, done)
    for copy in coming[len(chunks) :]:
        copy.wait()
    side_by_side(proj_ref, wide, weights, "halves")
    live = live_tile(mask_ref, rows, cols)
    live_ref[...] = live
    for copy in coming[: len(chunks)]:
        copy.wait()
    pair = pair_ref[...].T
    pair_t_ref[...] = pair
    normed = over_channels(pair).astype(BF16)
    normed_ref[...] = normed
    for p, values in enumerate(panels(normed, weights)):
        half = values.shape[0] // 2
        by_near[...] = paired(values[:half], values[half:], live, cols).reshape(by_near.shape)
        for step, both_ref, b_ref in zip(NEAR_STEPS, both_refs, b_refs):
            for n, block in enumerate(chip_blocks(by_near, own_index() ^ step)):
                both_ref[p, n] = by_near[block]
                if p == 1:
                    b_ref[n] = by_near[block]


def middle_kernel(rows, cols, live_ref, weights, final_ref, pair_t_ref, gating_ref, *refs):
    *came_refs, keep_ref, give_ref, middle_ref, normed_ref, came, by_near = refs
    for step, ref in zip(NEAR_STEPS, came_refs):
        for n, block in enumerate(chip_blocks(came, own_index() ^ step)):
            came[block] = ref[n]
    middle = pair_t_ref[...] + gating_ref[...] * projected(came, final_ref, rows, cols)
    middle_ref[...] = middle
    normed = over_channels(middle).astype(BF16)
    normed_ref[...] = normed
    a, b = panels(normed, weights)
    hidden = a.shape[0]
    by_hidden = paired(a, b, live_ref[...], cols)
    devices, per_device = by_near.shape[:2]
    half = per_device // 2
    for d in range(devices):
        by_near[d, :half] = by_hidden[d * half : (d + 1) * half]
        by_near[d, half:] = by_hidden[hidden // 2 + d * half : hidden // 2 + (d + 1) * half]
    hand_out(by_near, NEAR_STEPS, keep_ref, give_ref)


def last_kernel(rows, cols, middle_ref, gating_ref, final_ref, *refs):
    *came_refs, out_hbm, came, out_ref, done = refs
    take_in(came_refs, ALL_STEPS, came)
    change = projected(came, final_ref, rows, cols)
    leaving = []
    for n in range(rows * cols // CHUNK):
        at = slice(n * CHUNK, (n + 1) * CHUNK)
        out_ref[at, :] = (middle_ref[:, at] + gating_ref[:, at] * change[:, at]).T
        leaving.append(pltpu.make_async_copy(out_ref.at[at], out_hbm.at[at], done.at[n]))
        leaving[-1].start()
    for copy in leaving:
        copy.wait()


def low_of(x, cols):
    return lax.broadcasted_iota(jnp.int32, x.shape, 1) < cols


def both(ref, e):
    sources = ref.shape[0]
    return [jnp.concatenate([ref[r, e] for r in range(odd, sources, 2)], axis=0) for odd in (0, 1)]


def put(left, right, msg_ref, q):
    rows = msg_ref.shape[2]
    for r in range(msg_ref.shape[0] // 2):
        msg_ref[2 * r, q] = left[r * rows : (r + 1) * rows].astype(BF16)
        msg_ref[2 * r + 1, q] = right[r * rows : (r + 1) * rows].astype(BF16)


def outgoing_kernel(cols, *refs):
    both_refs, far_refs, sibling_ref = refs[:CHIPS], refs[CHIPS : 2 * CHIPS], refs[2 * CHIPS]
    *out_refs, a_ref, b_ref, msg_ref = refs[2 * CHIPS + 1 :]
    me = own_index()
    one = a_ref.shape[1:]
    for n, step in enumerate(NEAR_STEPS):
        a_ref[chip_of(me ^ step)] = both_refs[n][0].reshape(one)
        b_ref[me ^ step] = both_refs[n][1].reshape(one)
        b_ref[me ^ step ^ SIBLING] = sibling_ref[n].reshape(one)
        b_ref[me ^ step ^ NEAR] = far_refs[n][...].reshape(one)
        b_ref[me ^ step ^ NEAR ^ SIBLING] = sibling_ref[CHIPS + n].reshape(one)
    for q in range(msg_ref.shape[1]):
        even, odd = both(a_ref, q)
        low = low_of(even, cols)
        a, a2 = jnp.where(low, even, odd), jnp.where(low, odd, even)
        even, odd = both(b_ref, q)
        low = low_of(even, cols)
        b, b2 = jnp.where(low, even, odd), jnp.where(low, odd, even)
        x = lax.dot_general(a, b, (((1,), (1,)), ((), ())), preferred_element_type=F32)
        y = lax.dot_general(a2, b2, (((1,), (1,)), ((), ())), preferred_element_type=F32)
        low = low_of(x, cols)
        put(jnp.where(low, x, pltpu.roll(y, cols, 1)), jnp.where(low, pltpu.roll(x, cols, 1), y), msg_ref, q)
    for step, out_ref in zip(NEAR_STEPS, out_refs):
        out_ref[...] = msg_ref[chip_of(me ^ step)].reshape(out_ref.shape)


def incoming_kernel(cols, *refs):
    *came_refs, keep_ref, give_ref, recv_ref, msg_ref = refs
    take_in(came_refs, NEAR_STEPS, recv_ref)
    half = msg_ref.shape[1]

    def mixed(e):
        even, odd = both(recv_ref, e)
        low = low_of(even, cols)
        a, b = jnp.where(low, even, odd), jnp.where(low, odd, even)
        return lax.dot_general(a, b, (((0,), (0,)), ((), ())), preferred_element_type=F32)

    for q in range(half):
        x, y = mixed(q), mixed(q + half)
        low = low_of(x, cols)
        put(jnp.where(low, pltpu.roll(x, cols, 1), y), jnp.where(low, x, pltpu.roll(y, cols, 1)), msg_ref, q)
    hand_out(msg_ref, ALL_STEPS, keep_ref, give_ref)


def call(kernel, out_shape, scratch=(), far=(0, 0), flops=0, transcendentals=0):
    vmem = pl.BlockSpec(memory_space=pltpu.VMEM)
    hbm = pl.BlockSpec(memory_space=pltpu.HBM)
    far_args, far_outs = far

    def run(*args):
        args = [pltpu.with_memory_space_constraint(a, pltpu.HBM) for a in args[:far_args]] + list(args[far_args:])
        return pl.pallas_call(
            kernel,
            out_shape=tuple(out_shape),
            in_specs=[hbm] * far_args + [vmem] * (len(args) - far_args),
            out_specs=(hbm,) * far_outs + (vmem,) * (len(out_shape) - far_outs),
            scratch_shapes=list(scratch),
            compiler_params=pltpu.CompilerParams(vmem_limit_bytes=40 * 1024 * 1024),
            cost_estimate=pl.CostEstimate(
                flops=flops, transcendentals=transcendentals, bytes_accessed=sum(a.size * a.dtype.itemsize for a in (*args, *out_shape))
            ),
        )(*args)

    return run


def by_channel(devices, pair, residue_mask, out_proj, out_gate, out_final, in_proj, in_gate, in_final):
    rows, cols, channels = pair.shape
    hidden = out_proj.shape[2]
    positions = rows * cols
    shape = jax.ShapeDtypeStruct
    axes = ("row", "col")

    def swap(values, step):
        return lax.ppermute(values, axes, [(d, d ^ step) for d in range(devices)])

    def exchange(keep, give, steps):
        got = swap(give, SIBLING)
        moving = call(forward_kernel, [shape((2,) + keep.shape[1:], BF16)] * (len(steps) - 1))(keep, got)
        return (keep, got, *(swap(block, step) for block, step in zip(moving, steps[1:])))

    def exchange_panels(both, b):
        moved = {0: both[0]}
        for step in ALL_STEPS[1:]:
            n = NEAR_STEPS.index(step % NEAR)
            moved[step] = swap(both[n] if step < NEAR else b[n], step)
        near = [moved[step] for step in NEAR_STEPS]
        far = [moved[step ^ NEAR] for step in NEAR_STEPS]
        (all_b,) = call(all_b_kernel, [shape((2 * CHIPS,) + both[0].shape[1:], BF16)])(*near, *far)
        return (*near, *far, swap(all_b, SIBLING))

    def messages(targets, tiles):
        return shape((targets, tiles, rows, LANES), BF16)

    def scratch_tiles(targets, tiles):
        return pltpu.VMEM(messages(targets, tiles).shape, BF16)

    plane = shape((channels, positions), F32)
    half_plane = shape((channels, positions), BF16)
    mask = residue_mask.reshape(1, -1)
    by_position = pltpu.VMEM((positions, channels), F32)
    weights = (channels, 4 * hidden)
    chunks = positions // CHUNK
    pairs = hidden // NEAR // 2
    per_chip = (messages(2, pairs),) * CHIPS
    both_per_chip = (shape((2, 2, pairs, rows, LANES), BF16),) * CHIPS
    wide_near_steps = (messages(len(NEAR_STEPS), 2 * pairs),) * 2
    all_steps = (messages(len(ALL_STEPS), pairs),) * 2
    gate = call(gate_kernel, [plane], flops=2 * channels * channels * positions, transcendentals=channels * positions)

    far = (pair.reshape(positions, channels), mask, out_proj.reshape(-1, hidden))
    outs = (*both_per_chip, *per_chip, plane, half_plane, shape((rows, LANES), F32))
    scratch = [pltpu.VMEM(a.shape, a.dtype) for a in far]
    wide = pltpu.VMEM((4 * channels, hidden), F32)
    scratch += [pltpu.VMEM(weights, BF16), wide]
    scratch += [scratch_tiles(NEAR, pairs), pltpu.SemaphoreType.DMA((chunks + 2,))]
    outs = call(functools.partial(first_kernel, rows, cols), outs, scratch, (3, 0))(*far)
    pair_t, normed, live = outs[2 * CHIPS :]
    came = exchange_panels(outs[:CHIPS], outs[CHIPS : 2 * CHIPS])
    (weights,) = call(second_weights_kernel, [shape(weights, BF16)], [wide])(in_proj.reshape(-1, hidden))
    gating, weights, came = lax.optimization_barrier((gate(normed, out_gate)[0], weights, came))

    scratch = [scratch_tiles(CHIPS, 2 * pairs), scratch_tiles(devices, 2 * pairs), scratch_tiles(CHIPS, 2 * pairs)]
    own, *others = call(functools.partial(outgoing_kernel, cols), per_chip, scratch)(*came)
    came = (own, *(swap(block, step) for block, step in zip(others, NEAR_STEPS[1:])))

    scratch = [scratch_tiles(NEAR, pairs), scratch_tiles(NEAR, 2 * pairs)]
    outs = (*wide_near_steps, plane, half_plane)
    keep, give, middle, normed = call(functools.partial(middle_kernel, rows, cols), outs, scratch)(
        live, weights, out_final, pair_t, gating, *came
    )
    came = exchange(keep, give, NEAR_STEPS)
    gating, came = lax.optimization_barrier((gate(normed, in_gate)[0], came))

    scratch = [scratch_tiles(NEAR, 2 * pairs), scratch_tiles(devices, pairs)]
    keep, give = call(functools.partial(incoming_kernel, cols), all_steps, scratch)(*came)
    came = exchange(keep, give, ALL_STEPS)

    scratch = [scratch_tiles(devices, pairs), by_position, pltpu.SemaphoreType.DMA((chunks,))]
    outs = [shape((positions, channels), F32)]
    (out,) = call(functools.partial(last_kernel, rows, cols), outs, scratch, (0, 1))(middle, gating, in_final, *came)
    return out.reshape(rows, cols, channels)


def normalize(values, axis):
    average = jnp.mean(values, axis=axis, keepdims=True)
    centred = values - average
    variance = jnp.mean(centred * centred, axis=axis, keepdims=True)
    return centred * lax.rsqrt(variance + EPS)


def gated_panels(pair, row_live, col_live, proj):
    normed = normalize(pair, 2).astype(BF16)
    linear = jnp.einsum("ijc,cph->phij", normed, proj, preferred_element_type=F32)
    pair_mask = row_live[:, None] * col_live[None, :]
    left_panel = (pair_mask * jax.nn.sigmoid(linear[1]) * linear[0]).astype(BF16)
    right_panel = (pair_mask * jax.nn.sigmoid(linear[3]) * linear[2]).astype(BF16)
    return (normed, left_panel, right_panel)


def update_pair(pair, normed, mixed, gate_w, final_w):
    all_channels = lax.all_gather(mixed, "sub", axis=0, tiled=True)
    scaled = normalize(all_channels, 0).astype(BF16)
    projected = jnp.einsum("hij,hc->ijc", scaled, final_w, preferred_element_type=F32)
    gating = jax.nn.sigmoid(jnp.einsum("ijc,cd->ijd", normed, gate_w, preferred_element_type=F32))
    return pair + gating * projected


def by_position(pair, residue_mask, out_proj, out_gate, out_final, in_proj, in_gate, in_final):
    row_count = pair.shape[0]
    col_count = pair.shape[1]
    row_start = lax.axis_index("row") * row_count
    col_start = lax.axis_index("col") * col_count
    live = residue_mask.astype(F32)
    row_live = lax.dynamic_slice_in_dim(live, row_start, row_count, 0)
    col_live = lax.dynamic_slice_in_dim(live, col_start, col_count, 0)
    normed, left_panel, right_panel = gated_panels(pair, row_live, col_live, out_proj)
    left_rows, right_rows = (
        lax.all_gather(left_panel, "col", axis=2, tiled=True),
        lax.all_gather(right_panel, "col", axis=2, tiled=True),
    )
    turned = lax.all_to_all(right_rows, "row", split_axis=2, concat_axis=1, tiled=True)
    own_right = lax.dynamic_slice_in_dim(turned, col_start, col_count, 1)
    mixed = jnp.einsum(
        "hik,hjk->hij",
        left_rows,
        lax.all_gather(own_right, "row", axis=2, tiled=True),
        preferred_element_type=F32,
    )
    middle = update_pair(pair, normed, mixed, out_gate, out_final)
    normed, left_panel, right_panel = gated_panels(middle, row_live, col_live, in_proj)
    left_rows = lax.all_gather(left_panel, "col", axis=2, tiled=True)
    turned_left = lax.all_to_all(left_rows, "row", split_axis=2, concat_axis=1, tiled=True)
    mixed_in = jnp.einsum(
        "hki,hkj->hij",
        turned_left,
        lax.all_gather(right_panel, "row", axis=1, tiled=True),
        preferred_element_type=F32,
    )
    return update_pair(middle, normed, mixed_in, in_gate, in_final)


def local(axes, pair, residue_mask, out_proj, *rest):
    rows, cols, channels = pair.shape
    hidden = out_proj.shape[2]
    devices = axes["row"] * axes["col"]
    fits = (
        axes["sub"] == 1
        and axes["col"] == 2
        and residue_mask.shape[0] == LANES
        and cols * 2 == LANES
        and rows % 16 == 0
        and rows * cols % CHUNK == 0
        and channels == LANES
        and hidden == channels
        and devices == 2 * NEAR
        and hidden % (2 * NEAR) == 0
        and hidden % 16 == 0
    )
    plan = functools.partial(by_channel, devices) if fits else by_position
    return plan(pair, residue_mask, out_proj, *rest)


def solution(mesh):
    return jax.shard_map(
        functools.partial(local, dict(mesh.shape)),
        mesh=mesh,
        in_specs=(
            P(("groups", "row"), "col", None),
            P("groups"),
            P(None, None, "sub"),
            P(),
            P(),
            P(None, None, "sub"),
            P(),
            P(),
        ),
        out_specs=P(("groups", "row"), "col", None),
        check_vma=False,
    )
```

```python
import functools

import jax
import jax.numpy as jnp
from jax import lax
from jax.experimental import pallas as pl
from jax.experimental.pallas import tpu as pltpu
from jax.sharding import PartitionSpec as P

F32 = jnp.float32
BF16 = jnp.bfloat16
LANES = 128
CHUNK = 512
NEAR = 8
SIBLING = 2
NEAR_STEPS = (0, 5, 4, 1)
ALL_STEPS = (0, 13, 12, 5, 9, 8, 4, 1)
CHIPS = len(NEAR_STEPS)
EPS = 1e-05


def over_channels(values):
    centred = values - jnp.mean(values, axis=0, keepdims=True)
    variance = jnp.mean(centred * centred, axis=0, keepdims=True)
    return centred * lax.rsqrt(variance + EPS)


def product(weight, values):
    return lax.dot_general(weight, values, (((0,), (0,)), ((), ())), preferred_element_type=F32)


def panels_of(proj_ref, wide, channels):
    wide[...] = proj_ref[...].astype(F32)
    return [wide[pl.ds(n, channels, stride=4), :] for n in range(4)]


def first_weights(proj_ref, wide, weights):
    channels, hidden = weights.shape[0], weights.shape[1] // 4
    odd = lax.axis_index("col") == 1
    for n, panel in enumerate(panels_of(proj_ref, wide, channels)):
        panel = jnp.where(odd, pltpu.roll(panel, hidden // 2, 1), panel)
        weights[:, n * hidden : (n + 1) * hidden] = panel.astype(BF16)


def second_weights_kernel(proj_ref, weights, wide):
    channels, hidden = weights.shape[0], weights.shape[1] // 4
    quarter = hidden // 4
    odd = lax.axis_index("col") == 1
    upper = lax.axis_index("row") % 2 == 1
    a, a_gate, b, b_gate = panels_of(proj_ref, wide, channels)
    panels = [jnp.where(odd, b, a), jnp.where(odd, b_gate, a_gate), jnp.where(odd, a, b), jnp.where(odd, a_gate, b_gate)]
    lane = lax.broadcasted_iota(jnp.int32, (channels, hidden), 1)
    kept, given = [], []
    for panel in panels:
        shifted = pltpu.roll(panel, hidden - quarter, 1)
        lower_part = jnp.where(lane < quarter, panel, shifted)
        upper_part = jnp.where(lane < quarter, shifted, pltpu.roll(panel, hidden // 2, 1))
        kept.append(jnp.where(upper, upper_part, lower_part))
        given.append(jnp.where(upper, lower_part, upper_part))
    for n, (x, y) in enumerate(((kept[0], kept[1]), (kept[2], kept[3]), (given[0], given[1]), (given[2], given[3]))):
        both = jnp.where(lane < hidden // 2, x, pltpu.roll(y, hidden // 2, 1))
        weights[:, n * hidden : (n + 1) * hidden] = both.astype(BF16)


def live_tile(mask_ref, rows, cols):
    live = mask_ref[...].astype(F32)
    lane = lax.broadcasted_iota(jnp.int32, (rows, LANES), 1)
    sub = lax.broadcasted_iota(jnp.int32, (rows, LANES), 0)
    wide = jnp.broadcast_to(live, (rows, LANES))
    mine = lane == lax.axis_index("row") * rows + sub
    row_live = jnp.sum(jnp.where(mine, wide, 0.0), axis=1, keepdims=True)
    col_live = jnp.where(lane // cols == lax.axis_index("col"), wide, pltpu.roll(wide, cols, 1))
    return row_live * col_live


def panels(normed, weights):
    hidden = weights.shape[1] // 4
    linear = product(weights[...], normed)
    return [jax.nn.sigmoid(linear[(p + 1) * hidden : (p + 2) * hidden]) * linear[p * hidden : (p + 1) * hidden] for p in (0, 2)]


def gate_kernel(normed_ref, gate_ref, gating_ref):
    gating_ref[...] = jax.nn.sigmoid(product(gate_ref[...], normed_ref[...]))


def paired(first, second, live, cols):
    low = lax.broadcasted_iota(jnp.int32, (first.shape[0], LANES), 1) < cols
    by_row = []
    for t in range(live.shape[0] // 2):
        a = first[:, t * LANES : (t + 1) * LANES]
        b = second[:, t * LANES : (t + 1) * LANES]
        for tile in (jnp.where(low, a, pltpu.roll(b, cols, 1)), jnp.where(low, pltpu.roll(a, cols, 1), b)):
            row = len(by_row)
            by_row.append((tile * live[row : row + 1]).astype(BF16))
    return jnp.swapaxes(jnp.stack(by_row, axis=0), 0, 1)


def summed(values):
    chains = values.reshape((values.shape[0] // 8, 8) + values.shape[1:])
    return jnp.sum(jnp.sum(chains, axis=0), axis=0)


def projected(recv_ref, final_ref, rows, cols):
    half = final_ref.shape[0] // 2
    values = jnp.sum(recv_ref[...].reshape(-1, half, rows, LANES).astype(F32), axis=0)
    total = summed(values)
    centred = values - ((total + pltpu.roll(total, cols, 1)) / (2 * half))[None]
    square = summed(centred * centred)
    variance = (square + pltpu.roll(square, cols, 1)) / (2 * half)
    scaled = jnp.swapaxes((centred * lax.rsqrt(variance + EPS)[None]).astype(BF16), 0, 1).astype(F32)
    low = lax.broadcasted_iota(jnp.int32, (half, LANES), 1) < cols
    parts = []
    for t in range(rows // 2):
        a, b = scaled[2 * t], scaled[2 * t + 1]
        upper = jnp.where(low, a, pltpu.roll(b, cols, 1))
        lower = jnp.where(low, pltpu.roll(a, cols, 1), b)
        parts.append(jnp.concatenate([upper, lower], axis=0).astype(BF16))
    return product(final_ref[...], jnp.concatenate(parts, axis=1))


def copies(pairs, done):
    started = [pltpu.make_async_copy(source, target, done.at[n]) for n, (source, target) in enumerate(pairs)]
    for copy in started:
        copy.start()
    return started


def own_index():
    return lax.axis_index("row") * 2 + lax.axis_index("col")


def within_half(index):
    return index & (NEAR - 1)


def chip_of(index):
    return (index >> 1) & 2 | index & 1


def by_owner(index):
    return index & NEAR | (index & SIBLING) << 1 | chip_of(index)


def hand_out(tiles, steps, keep_ref, give_ref):
    me = own_index()
    for n, step in enumerate(steps):
        keep_ref[n] = tiles[me ^ step]
        give_ref[n] = tiles[me ^ (step ^ SIBLING)]


def forward_kernel(keep_ref, got_ref, *out_refs):
    for n, out_ref in enumerate(out_refs):
        out_ref[0] = keep_ref[n + 1]
        out_ref[1] = got_ref[n + 1]


def take_in(refs, steps, tiles, place):
    keep_ref, got_ref, *moved_refs = refs
    me = place(own_index())
    tiles[me] = keep_ref[0]
    tiles[me ^ place(SIBLING)] = got_ref[0]
    for step, moved_ref in zip(steps[1:], moved_refs):
        tiles[me ^ place(step)] = moved_ref[0]
        tiles[me ^ place(step ^ SIBLING)] = moved_ref[1]


def chip_blocks(me, step):
    base = (within_half(me) & ~SIBLING) ^ (within_half(step) & ~SIBLING)
    return base, base | SIBLING


def all_b_kernel(*refs):
    *came_refs, out_ref = refs
    for n, ref in enumerate(came_refs):
        out_ref[n] = ref[1] if n < CHIPS else ref[...]


def first_kernel(rows, cols, pair_hbm, mask_hbm, proj_hbm, *refs):
    both_refs, b_refs = refs[:CHIPS], refs[CHIPS : 2 * CHIPS]
    pair_t_ref, normed_ref, live_ref = refs[2 * CHIPS : 2 * CHIPS + 3]
    pair_ref, mask_ref, proj_ref, weights, wide, by_near, done = refs[2 * CHIPS + 3 :]
    chunks = [slice(at, at + CHUNK) for at in range(0, rows * cols, CHUNK)]
    whole = [(mask_hbm, mask_ref), (proj_hbm, proj_ref)]
    coming = copies([(pair_hbm.at[at], pair_ref.at[at]) for at in chunks] + whole, done)
    for copy in coming[len(chunks) :]:
        copy.wait()
    first_weights(proj_ref, wide, weights)
    live = live_tile(mask_ref, rows, cols)
    live_ref[...] = live
    for copy in coming[: len(chunks)]:
        copy.wait()
    pair = pair_ref[...].T
    pair_t_ref[...] = pair
    normed = over_channels(pair).astype(BF16)
    normed_ref[...] = normed
    me = own_index()
    for p, values in enumerate(panels(normed, weights)):
        half = values.shape[0] // 2
        by_near[...] = paired(values[:half], values[half:], live, cols).reshape(by_near.shape)
        for step, both_ref, b_ref in zip(NEAR_STEPS, both_refs, b_refs):
            for n, block in enumerate(chip_blocks(me, step)):
                both_ref[p, n] = by_near[block]
                if p == 1:
                    b_ref[n] = by_near[block]


def to_chips(normed, weights, live, cols, by_chip, out_ref):
    tiles = paired(*panels(normed, weights), live, cols)
    per_chip = tiles.shape[0] // 2 // CHIPS
    for d in range(CHIPS):
        by_chip[d, :per_chip] = tiles[d * per_chip : (d + 1) * per_chip]
        by_chip[d, per_chip:] = tiles[(CHIPS + d) * per_chip : (CHIPS + d + 1) * per_chip]
    me = chip_of(own_index())
    for n, step in enumerate(NEAR_STEPS):
        out_ref[n] = by_chip[me ^ chip_of(step)]


def middle_kernel(rows, cols, live_ref, weights, final_ref, pair_t_ref, gating_ref, *refs):
    *came_refs, give_ref, middle_ref, normed_ref, came, by_chip = refs
    me = own_index()
    for step, ref in zip(NEAR_STEPS, came_refs):
        for n, block in enumerate(chip_blocks(me, step)):
            came[block] = ref[n]
    middle = pair_t_ref[...] + gating_ref[...] * projected(came, final_ref, rows, cols)
    middle_ref[...] = middle
    normed = over_channels(middle).astype(BF16)
    normed_ref[...] = normed
    to_chips(normed, weights[:, weights.shape[1] // 2 :], live_ref[...], cols, by_chip, give_ref)


def keep_kernel(cols, live_ref, weights, normed_ref, keep_ref, by_chip):
    to_chips(normed_ref[...], weights[:, : weights.shape[1] // 2], live_ref[...], cols, by_chip, keep_ref)


def last_kernel(rows, cols, middle_ref, gating_ref, final_ref, *refs):
    *came_refs, out_hbm, came, out_ref, done = refs
    take_in(came_refs, ALL_STEPS, came, by_owner)
    change = projected(came, final_ref, rows, cols)
    leaving = []
    for n in range(rows * cols // CHUNK):
        at = slice(n * CHUNK, (n + 1) * CHUNK)
        out_ref[at, :] = (middle_ref[:, at] + gating_ref[:, at] * change[:, at]).T
        leaving.append(pltpu.make_async_copy(out_ref.at[at], out_hbm.at[at], done.at[n]))
        leaving[-1].start()
    for copy in leaving:
        copy.wait()


def low_of(x, cols):
    return lax.broadcasted_iota(jnp.int32, x.shape, 1) < cols


def both(ref, e):
    sources = ref.shape[0]
    return [jnp.concatenate([ref[r, e] for r in range(odd, sources, 2)], axis=0) for odd in (0, 1)]


def put(left, right, msg_ref, q):
    rows = msg_ref.shape[2]
    for r in range(msg_ref.shape[0] // 2):
        msg_ref[2 * r, q] = left[r * rows : (r + 1) * rows].astype(BF16)
        msg_ref[2 * r + 1, q] = right[r * rows : (r + 1) * rows].astype(BF16)


def outgoing_kernel(cols, *refs):
    both_refs, far_refs, sibling_ref = refs[:CHIPS], refs[CHIPS : 2 * CHIPS], refs[2 * CHIPS]
    *out_refs, a_ref, b_ref, msg_ref = refs[2 * CHIPS + 1 :]
    me = own_index()
    one = a_ref.shape[1:]
    for n, step in enumerate(NEAR_STEPS):
        a_ref[chip_of(me) ^ chip_of(step)] = both_refs[n][0].reshape(one)
        b_ref[me ^ step] = both_refs[n][1].reshape(one)
        b_ref[me ^ (step ^ SIBLING)] = sibling_ref[n].reshape(one)
        b_ref[me ^ (step ^ NEAR)] = far_refs[n][...].reshape(one)
        b_ref[me ^ (step ^ NEAR ^ SIBLING)] = sibling_ref[CHIPS + n].reshape(one)
    for q in range(msg_ref.shape[1]):
        even, odd = both(a_ref, q)
        low = low_of(even, cols)
        a, a2 = jnp.where(low, even, odd), jnp.where(low, odd, even)
        even, odd = both(b_ref, q)
        low = low_of(even, cols)
        b, b2 = jnp.where(low, even, odd), jnp.where(low, odd, even)
        x = lax.dot_general(a, b, (((1,), (1,)), ((), ())), preferred_element_type=F32)
        y = lax.dot_general(a2, b2, (((1,), (1,)), ((), ())), preferred_element_type=F32)
        low = low_of(x, cols)
        put(jnp.where(low, x, pltpu.roll(y, cols, 1)), jnp.where(low, pltpu.roll(x, cols, 1), y), msg_ref, q)
    for step, out_ref in zip(NEAR_STEPS, out_refs):
        out_ref[...] = msg_ref[chip_of(me) ^ chip_of(step)].reshape(out_ref.shape)


def incoming_kernel(cols, *refs):
    *came_refs, keep_ref, give_ref, recv_ref, msg_ref = refs
    take_in(came_refs, NEAR_STEPS, recv_ref, within_half)
    half = msg_ref.shape[1]

    def mixed(e):
        even, odd = both(recv_ref, e)
        low = low_of(even, cols)
        a, b = jnp.where(low, even, odd), jnp.where(low, odd, even)
        return lax.dot_general(a, b, (((0,), (0,)), ((), ())), preferred_element_type=F32)

    for q in range(half):
        x, y = mixed(q), mixed(q + half)
        low = low_of(x, cols)
        put(jnp.where(low, pltpu.roll(x, cols, 1), y), jnp.where(low, x, pltpu.roll(y, cols, 1)), msg_ref, q)
    hand_out(msg_ref, ALL_STEPS, keep_ref, give_ref)


def call(kernel, out_shape, scratch=(), far=(0, 0), flops=0, transcendentals=0):
    vmem = pl.BlockSpec(memory_space=pltpu.VMEM)
    hbm = pl.BlockSpec(memory_space=pltpu.HBM)
    far_args, far_outs = far

    def run(*args):
        args = [pltpu.with_memory_space_constraint(a, pltpu.HBM) for a in args[:far_args]] + list(args[far_args:])
        return pl.pallas_call(
            kernel,
            out_shape=tuple(out_shape),
            in_specs=[hbm] * far_args + [vmem] * (len(args) - far_args),
            out_specs=(hbm,) * far_outs + (vmem,) * (len(out_shape) - far_outs),
            scratch_shapes=list(scratch),
            compiler_params=pltpu.CompilerParams(vmem_limit_bytes=40 * 1024 * 1024),
            cost_estimate=pl.CostEstimate(
                flops=flops, transcendentals=transcendentals, bytes_accessed=sum(a.size * a.dtype.itemsize for a in (*args, *out_shape))
            ),
        )(*args)

    return run


def by_channel(devices, pair, residue_mask, out_proj, out_gate, out_final, in_proj, in_gate, in_final):
    rows, cols, channels = pair.shape
    hidden = out_proj.shape[2]
    positions = rows * cols
    shape = jax.ShapeDtypeStruct
    axes = ("row", "col")

    def swap(values, step):
        return lax.ppermute(values, axes, [(d, d ^ step) for d in range(devices)])

    def exchange(keep, give, steps):
        got = swap(give, SIBLING)
        moving = call(forward_kernel, [shape((2,) + keep.shape[1:], BF16)] * (len(steps) - 1))(keep, got)
        return (keep, got, *(swap(block, step) for block, step in zip(moving, steps[1:])))

    def exchange_panels(both, b):
        moved = {0: both[0]}
        for step in ALL_STEPS[1:]:
            n = NEAR_STEPS.index(step % NEAR)
            moved[step] = swap(both[n] if step < NEAR else b[n], step)
        near = [moved[step] for step in NEAR_STEPS]
        far = [moved[step ^ NEAR] for step in NEAR_STEPS]
        (all_b,) = call(all_b_kernel, [shape((2 * CHIPS,) + both[0].shape[1:], BF16)])(*near, *far)
        return (*near, *far, swap(all_b, SIBLING))

    def messages(targets, tiles):
        return shape((targets, tiles, rows, LANES), BF16)

    def scratch_tiles(targets, tiles):
        return pltpu.VMEM(messages(targets, tiles).shape, BF16)

    plane = shape((channels, positions), F32)
    half_plane = shape((channels, positions), BF16)
    mask = residue_mask.reshape(1, -1)
    by_position = pltpu.VMEM((positions, channels), F32)
    weights = (channels, 4 * hidden)
    chunks = positions // CHUNK
    pairs = hidden // NEAR // 2
    per_chip = (messages(2, pairs),) * CHIPS
    both_per_chip = (shape((2, 2, pairs, rows, LANES), BF16),) * CHIPS
    all_steps = (messages(len(ALL_STEPS), pairs),) * 2
    gate = call(gate_kernel, [plane], flops=2 * channels * channels * positions, transcendentals=channels * positions)

    far = (pair.reshape(positions, channels), mask, out_proj.reshape(-1, hidden))
    outs = (*both_per_chip, *per_chip, plane, half_plane, shape((rows, LANES), F32))
    scratch = [pltpu.VMEM(a.shape, a.dtype) for a in far]
    wide = pltpu.VMEM((4 * channels, hidden), F32)
    scratch += [pltpu.VMEM(weights, BF16), wide]
    scratch += [scratch_tiles(NEAR, pairs), pltpu.SemaphoreType.DMA((chunks + 2,))]
    outs = call(functools.partial(first_kernel, rows, cols), outs, scratch, (3, 0))(*far)
    pair_t, normed, live = outs[2 * CHIPS :]
    came = exchange_panels(outs[:CHIPS], outs[CHIPS : 2 * CHIPS])
    (weights,) = call(second_weights_kernel, [shape(weights, BF16)], [wide])(in_proj.reshape(-1, hidden))
    gating, weights, came = lax.optimization_barrier((gate(normed, out_gate)[0], weights, came))

    scratch = [scratch_tiles(CHIPS, 2 * pairs), scratch_tiles(devices, 2 * pairs), scratch_tiles(CHIPS, 2 * pairs)]
    own, *others = call(functools.partial(outgoing_kernel, cols), per_chip, scratch)(*came)
    came = (own, *(swap(block, step) for block, step in zip(others, NEAR_STEPS[1:])))

    chip_tiles = scratch_tiles(CHIPS, 2 * pairs)
    half_step = messages(len(NEAR_STEPS), 2 * pairs)
    outs = (half_step, plane, half_plane)
    give, middle, normed = call(functools.partial(middle_kernel, rows, cols), outs, [scratch_tiles(NEAR, pairs), chip_tiles])(
        live, weights, out_final, pair_t, gating, *came
    )
    work = 4 * channels * hidden * positions
    (keep,) = call(functools.partial(keep_kernel, cols), [half_step], [chip_tiles], flops=work)(live, weights, normed)
    came = exchange(keep, give, NEAR_STEPS)
    gating, came = lax.optimization_barrier((gate(normed, in_gate)[0], came))

    scratch = [scratch_tiles(NEAR, 2 * pairs), scratch_tiles(devices, pairs)]
    keep, give = call(functools.partial(incoming_kernel, cols), all_steps, scratch)(*came)
    came = exchange(keep, give, ALL_STEPS)

    scratch = [scratch_tiles(devices, pairs), by_position, pltpu.SemaphoreType.DMA((chunks,))]
    outs = [shape((positions, channels), F32)]
    (out,) = call(functools.partial(last_kernel, rows, cols), outs, scratch, (0, 1))(middle, gating, in_final, *came)
    return out.reshape(rows, cols, channels)


def normalize(values, axis):
    average = jnp.mean(values, axis=axis, keepdims=True)
    centred = values - average
    variance = jnp.mean(centred * centred, axis=axis, keepdims=True)
    return centred * lax.rsqrt(variance + EPS)


def gated_panels(pair, row_live, col_live, proj):
    normed = normalize(pair, 2).astype(BF16)
    linear = jnp.einsum("ijc,cph->phij", normed, proj, preferred_element_type=F32)
    pair_mask = row_live[:, None] * col_live[None, :]
    left_panel = (pair_mask * jax.nn.sigmoid(linear[1]) * linear[0]).astype(BF16)
    right_panel = (pair_mask * jax.nn.sigmoid(linear[3]) * linear[2]).astype(BF16)
    return (normed, left_panel, right_panel)


def update_pair(pair, normed, mixed, gate_w, final_w):
    all_channels = lax.all_gather(mixed, "sub", axis=0, tiled=True)
    scaled = normalize(all_channels, 0).astype(BF16)
    projected = jnp.einsum("hij,hc->ijc", scaled, final_w, preferred_element_type=F32)
    gating = jax.nn.sigmoid(jnp.einsum("ijc,cd->ijd", normed, gate_w, preferred_element_type=F32))
    return pair + gating * projected


def by_position(pair, residue_mask, out_proj, out_gate, out_final, in_proj, in_gate, in_final):
    row_count = pair.shape[0]
    col_count = pair.shape[1]
    row_start = lax.axis_index("row") * row_count
    col_start = lax.axis_index("col") * col_count
    live = residue_mask.astype(F32)
    row_live = lax.dynamic_slice_in_dim(live, row_start, row_count, 0)
    col_live = lax.dynamic_slice_in_dim(live, col_start, col_count, 0)
    normed, left_panel, right_panel = gated_panels(pair, row_live, col_live, out_proj)
    left_rows, right_rows = (
        lax.all_gather(left_panel, "col", axis=2, tiled=True),
        lax.all_gather(right_panel, "col", axis=2, tiled=True),
    )
    turned = lax.all_to_all(right_rows, "row", split_axis=2, concat_axis=1, tiled=True)
    own_right = lax.dynamic_slice_in_dim(turned, col_start, col_count, 1)
    mixed = jnp.einsum(
        "hik,hjk->hij",
        left_rows,
        lax.all_gather(own_right, "row", axis=2, tiled=True),
        preferred_element_type=F32,
    )
    middle = update_pair(pair, normed, mixed, out_gate, out_final)
    normed, left_panel, right_panel = gated_panels(middle, row_live, col_live, in_proj)
    left_rows = lax.all_gather(left_panel, "col", axis=2, tiled=True)
    turned_left = lax.all_to_all(left_rows, "row", split_axis=2, concat_axis=1, tiled=True)
    mixed_in = jnp.einsum(
        "hki,hkj->hij",
        turned_left,
        lax.all_gather(right_panel, "row", axis=1, tiled=True),
        preferred_element_type=F32,
    )
    return update_pair(middle, normed, mixed_in, in_gate, in_final)


def local(axes, pair, residue_mask, out_proj, *rest):
    rows, cols, channels = pair.shape
    hidden = out_proj.shape[2]
    devices = axes["row"] * axes["col"]
    fits = (
        axes["sub"] == 1
        and axes["col"] == 2
        and residue_mask.shape[0] == LANES
        and cols * 2 == LANES
        and rows % 16 == 0
        and rows * cols % CHUNK == 0
        and channels == LANES
        and hidden == channels
        and devices == 2 * NEAR
        and hidden % (2 * NEAR) == 0
        and hidden % 16 == 0
    )
    plan = functools.partial(by_channel, devices) if fits else by_position
    return plan(pair, residue_mask, out_proj, *rest)


def solution(mesh):
    return jax.shard_map(
        functools.partial(local, dict(mesh.shape)),
        mesh=mesh,
        in_specs=(
            P(("groups", "row"), "col", None),
            P("groups"),
            P(None, None, "sub"),
            P(),
            P(),
            P(None, None, "sub"),
            P(),
            P(),
        ),
        out_specs=P(("groups", "row"), "col", None),
        check_vma=False,
    )
```

```python
import functools

import jax
import jax.numpy as jnp
from jax import lax
from jax.experimental import pallas as pl
from jax.experimental.pallas import tpu as pltpu
from jax.sharding import PartitionSpec as P

F32 = jnp.float32
BF16 = jnp.bfloat16
LANES = 128
CHUNK = 512
NEAR = 8
SIBLING = 2
NEAR_STEPS = (0, 5, 4, 1)
ALL_STEPS = (0, 13, 12, 5, 9, 8, 4, 1)
CHIPS = len(NEAR_STEPS)
EPS = 1e-05


def over_channels(values):
    centred = values - jnp.mean(values, axis=0, keepdims=True)
    variance = jnp.mean(centred * centred, axis=0, keepdims=True)
    return centred * lax.rsqrt(variance + EPS)


def product(weight, values):
    return lax.dot_general(weight, values, (((0,), (0,)), ((), ())), preferred_element_type=F32)


def panels_of(proj_ref, wide, channels):
    wide[...] = proj_ref[...].astype(F32)
    return [wide[pl.ds(n, channels, stride=4), :] for n in range(4)]


def first_weights(proj_ref, wide, weights):
    channels, hidden = weights.shape[0], weights.shape[1] // 4
    odd = lax.axis_index("col") == 1
    for n, panel in enumerate(panels_of(proj_ref, wide, channels)):
        panel = jnp.where(odd, pltpu.roll(panel, hidden // 2, 1), panel)
        weights[:, n * hidden : (n + 1) * hidden] = panel.astype(BF16)


def second_weights_kernel(proj_ref, weights, wide):
    channels, hidden = weights.shape[0], weights.shape[1] // 4
    quarter = hidden // 4
    odd = lax.axis_index("col") == 1
    upper = lax.axis_index("row") % 2 == 1
    a, a_gate, b, b_gate = panels_of(proj_ref, wide, channels)
    panels = [jnp.where(odd, b, a), jnp.where(odd, b_gate, a_gate), jnp.where(odd, a, b), jnp.where(odd, a_gate, b_gate)]
    lane = lax.broadcasted_iota(jnp.int32, (channels, hidden), 1)
    kept, given = [], []
    for panel in panels:
        shifted = pltpu.roll(panel, hidden - quarter, 1)
        lower_part = jnp.where(lane < quarter, panel, shifted)
        upper_part = jnp.where(lane < quarter, shifted, pltpu.roll(panel, hidden // 2, 1))
        kept.append(jnp.where(upper, upper_part, lower_part))
        given.append(jnp.where(upper, lower_part, upper_part))
    for n, (x, y) in enumerate(((kept[0], kept[1]), (kept[2], kept[3]), (given[0], given[1]), (given[2], given[3]))):
        both = jnp.where(lane < hidden // 2, x, pltpu.roll(y, hidden // 2, 1))
        weights[:, n * hidden : (n + 1) * hidden] = both.astype(BF16)


def live_tile(mask_ref, rows, cols):
    live = mask_ref[...].astype(F32)
    lane = lax.broadcasted_iota(jnp.int32, (rows, LANES), 1)
    sub = lax.broadcasted_iota(jnp.int32, (rows, LANES), 0)
    wide = jnp.broadcast_to(live, (rows, LANES))
    mine = lane == lax.axis_index("row") * rows + sub
    row_live = jnp.sum(jnp.where(mine, wide, 0.0), axis=1, keepdims=True)
    col_live = jnp.where(lane // cols == lax.axis_index("col"), wide, pltpu.roll(wide, cols, 1))
    return row_live * col_live


def panels(normed, weights):
    hidden = weights.shape[1] // 4
    linear = product(weights[...], normed)
    return [jax.nn.sigmoid(linear[(p + 1) * hidden : (p + 2) * hidden]) * linear[p * hidden : (p + 1) * hidden] for p in (0, 2)]


def gate_kernel(normed_ref, gate_ref, gating_ref):
    gating_ref[...] = jax.nn.sigmoid(product(gate_ref[...], normed_ref[...]))


def paired(first, second, live, cols):
    low = lax.broadcasted_iota(jnp.int32, (first.shape[0], LANES), 1) < cols
    by_row = []
    for t in range(live.shape[0] // 2):
        a = first[:, t * LANES : (t + 1) * LANES]
        b = second[:, t * LANES : (t + 1) * LANES]
        for tile in (jnp.where(low, a, pltpu.roll(b, cols, 1)), jnp.where(low, pltpu.roll(a, cols, 1), b)):
            row = len(by_row)
            by_row.append((tile * live[row : row + 1]).astype(BF16))
    return jnp.swapaxes(jnp.stack(by_row, axis=0), 0, 1)


def summed(values):
    chains = values.reshape((values.shape[0] // 8, 8) + values.shape[1:])
    return jnp.sum(jnp.sum(chains, axis=0), axis=0)


def projected(recv_ref, final_ref, rows, cols):
    half = final_ref.shape[0] // 2
    values = jnp.sum(recv_ref[...].reshape(-1, half, rows, LANES).astype(F32), axis=0)
    total = summed(values)
    centred = values - ((total + pltpu.roll(total, cols, 1)) / (2 * half))[None]
    square = summed(centred * centred)
    variance = (square + pltpu.roll(square, cols, 1)) / (2 * half)
    scaled = jnp.swapaxes((centred * lax.rsqrt(variance + EPS)[None]).astype(BF16), 0, 1).astype(F32)
    low = lax.broadcasted_iota(jnp.int32, (half, LANES), 1) < cols
    parts = []
    for t in range(rows // 2):
        a, b = scaled[2 * t], scaled[2 * t + 1]
        upper = jnp.where(low, a, pltpu.roll(b, cols, 1))
        lower = jnp.where(low, pltpu.roll(a, cols, 1), b)
        parts.append(jnp.concatenate([upper, lower], axis=0).astype(BF16))
    return product(final_ref[...], jnp.concatenate(parts, axis=1))


def copies(pairs, done):
    started = [pltpu.make_async_copy(source, target, done.at[n]) for n, (source, target) in enumerate(pairs)]
    for copy in started:
        copy.start()
    return started


def own_index():
    return lax.axis_index("row") * 2 + lax.axis_index("col")


def within_half(index):
    return index & (NEAR - 1)


def chip_of(index):
    return (index >> 1) & 2 | index & 1


def by_owner(index):
    return index & NEAR | (index & SIBLING) << 1 | chip_of(index)


def hand_out(tiles, steps, keep_ref, give_ref):
    me = own_index()
    for n, step in enumerate(steps):
        keep_ref[n] = tiles[me ^ step]
        give_ref[n] = tiles[me ^ (step ^ SIBLING)]


def forward_kernel(keep_ref, got_ref, *out_refs):
    for n, out_ref in enumerate(out_refs):
        out_ref[0] = keep_ref[n + 1]
        out_ref[1] = got_ref[n + 1]


def take_in(refs, steps, tiles, place):
    keep_ref, got_ref, *moved_refs = refs
    me = place(own_index())
    tiles[me] = keep_ref[0]
    tiles[me ^ place(SIBLING)] = got_ref[0]
    for step, moved_ref in zip(steps[1:], moved_refs):
        tiles[me ^ place(step)] = moved_ref[0]
        tiles[me ^ place(step ^ SIBLING)] = moved_ref[1]


def chip_blocks(me, step):
    base = (within_half(me) & ~SIBLING) ^ (within_half(step) & ~SIBLING)
    return base, base | SIBLING


def all_b_kernel(*refs):
    *came_refs, out_ref = refs
    for n, ref in enumerate(came_refs):
        out_ref[n] = ref[1] if n < CHIPS else ref[...]


def first_kernel(rows, cols, pair_hbm, mask_hbm, proj_hbm, *refs):
    both_refs, b_refs = refs[:CHIPS], refs[CHIPS : 2 * CHIPS]
    pair_t_ref, normed_ref, live_ref = refs[2 * CHIPS : 2 * CHIPS + 3]
    pair_ref, mask_ref, proj_ref, weights, wide, by_near, done = refs[2 * CHIPS + 3 :]
    chunks = [slice(0, rows * cols)]
    whole = [(mask_hbm, mask_ref), (proj_hbm, proj_ref)]
    coming = copies(whole + [(pair_hbm.at[at], pair_ref.at[at]) for at in chunks], done)
    for copy in coming[: len(whole)]:
        copy.wait()
    first_weights(proj_ref, wide, weights)
    live = live_tile(mask_ref, rows, cols)
    live_ref[...] = live
    for copy in coming[len(whole) :]:
        copy.wait()
    pair = pair_ref[...].T
    pair_t_ref[...] = pair
    normed = over_channels(pair).astype(BF16)
    normed_ref[...] = normed
    me = own_index()
    for p, values in enumerate(panels(normed, weights)):
        half = values.shape[0] // 2
        by_near[...] = paired(values[:half], values[half:], live, cols).reshape(by_near.shape)
        for step, both_ref, b_ref in zip(NEAR_STEPS, both_refs, b_refs):
            for n, block in enumerate(chip_blocks(me, step)):
                both_ref[p, n] = by_near[block]
                if p == 1:
                    b_ref[n] = by_near[block]


def to_chips(normed, weights, live, cols, by_chip, out_ref):
    tiles = paired(*panels(normed, weights), live, cols)
    per_chip = tiles.shape[0] // 2 // CHIPS
    for d in range(CHIPS):
        by_chip[d, :per_chip] = tiles[d * per_chip : (d + 1) * per_chip]
        by_chip[d, per_chip:] = tiles[(CHIPS + d) * per_chip : (CHIPS + d + 1) * per_chip]
    me = chip_of(own_index())
    for n, step in enumerate(NEAR_STEPS):
        out_ref[n] = by_chip[me ^ chip_of(step)]


def middle_kernel(rows, cols, live_ref, weights, final_ref, pair_t_ref, gating_ref, *refs):
    *came_refs, give_ref, middle_ref, normed_ref, came, by_chip = refs
    me = own_index()
    for step, ref in zip(NEAR_STEPS, came_refs):
        for n, block in enumerate(chip_blocks(me, step)):
            came[block] = ref[n]
    middle = pair_t_ref[...] + gating_ref[...] * projected(came, final_ref, rows, cols)
    middle_ref[...] = middle
    normed = over_channels(middle).astype(BF16)
    normed_ref[...] = normed
    to_chips(normed, weights[:, weights.shape[1] // 2 :], live_ref[...], cols, by_chip, give_ref)


def keep_kernel(cols, live_ref, weights, normed_ref, keep_ref, by_chip):
    to_chips(normed_ref[...], weights[:, : weights.shape[1] // 2], live_ref[...], cols, by_chip, keep_ref)


def last_kernel(rows, cols, middle_ref, gating_ref, final_ref, *refs):
    *came_refs, out_hbm, came, out_ref, done = refs
    take_in(came_refs, ALL_STEPS, came, by_owner)
    change = projected(came, final_ref, rows, cols)
    leaving = []
    for n in range(rows * cols // CHUNK):
        at = slice(n * CHUNK, (n + 1) * CHUNK)
        out_ref[at, :] = (middle_ref[:, at] + gating_ref[:, at] * change[:, at]).T
        leaving.append(pltpu.make_async_copy(out_ref.at[at], out_hbm.at[at], done.at[n]))
        leaving[-1].start()
    for copy in leaving:
        copy.wait()


def low_of(x, cols):
    return lax.broadcasted_iota(jnp.int32, x.shape, 1) < cols


def both(ref, e):
    sources = ref.shape[0]
    return [jnp.concatenate([ref[r, e] for r in range(odd, sources, 2)], axis=0) for odd in (0, 1)]


def put(left, right, msg_ref, q):
    rows = msg_ref.shape[2]
    for r in range(msg_ref.shape[0] // 2):
        msg_ref[2 * r, q] = left[r * rows : (r + 1) * rows].astype(BF16)
        msg_ref[2 * r + 1, q] = right[r * rows : (r + 1) * rows].astype(BF16)


def outgoing_kernel(cols, *refs):
    both_refs, far_refs, sibling_ref = refs[:CHIPS], refs[CHIPS : 2 * CHIPS], refs[2 * CHIPS]
    *out_refs, a_ref, b_ref, msg_ref = refs[2 * CHIPS + 1 :]
    me = own_index()
    one = a_ref.shape[1:]
    for n, step in enumerate(NEAR_STEPS):
        a_ref[chip_of(me) ^ chip_of(step)] = both_refs[n][0].reshape(one)
        b_ref[me ^ step] = both_refs[n][1].reshape(one)
        b_ref[me ^ (step ^ SIBLING)] = sibling_ref[n].reshape(one)
        b_ref[me ^ (step ^ NEAR)] = far_refs[n][...].reshape(one)
        b_ref[me ^ (step ^ NEAR ^ SIBLING)] = sibling_ref[CHIPS + n].reshape(one)
    for q in range(msg_ref.shape[1]):
        even, odd = both(a_ref, q)
        low = low_of(even, cols)
        a, a2 = jnp.where(low, even, odd), jnp.where(low, odd, even)
        even, odd = both(b_ref, q)
        low = low_of(even, cols)
        b, b2 = jnp.where(low, even, odd), jnp.where(low, odd, even)
        x = lax.dot_general(a, b, (((1,), (1,)), ((), ())), preferred_element_type=F32)
        y = lax.dot_general(a2, b2, (((1,), (1,)), ((), ())), preferred_element_type=F32)
        low = low_of(x, cols)
        put(jnp.where(low, x, pltpu.roll(y, cols, 1)), jnp.where(low, pltpu.roll(x, cols, 1), y), msg_ref, q)
    for step, out_ref in zip(NEAR_STEPS, out_refs):
        out_ref[...] = msg_ref[chip_of(me) ^ chip_of(step)].reshape(out_ref.shape)


def incoming_kernel(cols, *refs):
    *came_refs, keep_ref, give_ref, recv_ref, msg_ref = refs
    take_in(came_refs, NEAR_STEPS, recv_ref, within_half)
    half = msg_ref.shape[1]

    def mixed(e):
        even, odd = both(recv_ref, e)
        low = low_of(even, cols)
        a, b = jnp.where(low, even, odd), jnp.where(low, odd, even)
        return lax.dot_general(a, b, (((0,), (0,)), ((), ())), preferred_element_type=F32)

    for q in range(half):
        x, y = mixed(q), mixed(q + half)
        low = low_of(x, cols)
        put(jnp.where(low, pltpu.roll(x, cols, 1), y), jnp.where(low, x, pltpu.roll(y, cols, 1)), msg_ref, q)
    hand_out(msg_ref, ALL_STEPS, keep_ref, give_ref)


def call(kernel, out_shape, scratch=(), far=(0, 0), flops=0, transcendentals=0):
    vmem = pl.BlockSpec(memory_space=pltpu.VMEM)
    hbm = pl.BlockSpec(memory_space=pltpu.HBM)
    far_args, far_outs = far

    def run(*args):
        args = [pltpu.with_memory_space_constraint(a, pltpu.HBM) for a in args[:far_args]] + list(args[far_args:])
        return pl.pallas_call(
            kernel,
            out_shape=tuple(out_shape),
            in_specs=[hbm] * far_args + [vmem] * (len(args) - far_args),
            out_specs=(hbm,) * far_outs + (vmem,) * (len(out_shape) - far_outs),
            scratch_shapes=list(scratch),
            compiler_params=pltpu.CompilerParams(vmem_limit_bytes=40 * 1024 * 1024),
            cost_estimate=pl.CostEstimate(
                flops=flops, transcendentals=transcendentals, bytes_accessed=sum(a.size * a.dtype.itemsize for a in (*args, *out_shape))
            ),
        )(*args)

    return run


def by_channel(devices, pair, residue_mask, out_proj, out_gate, out_final, in_proj, in_gate, in_final):
    rows, cols, channels = pair.shape
    hidden = out_proj.shape[2]
    positions = rows * cols
    shape = jax.ShapeDtypeStruct
    axes = ("row", "col")

    def swap(values, step):
        return lax.ppermute(values, axes, [(d, d ^ step) for d in range(devices)])

    def exchange(keep, give, steps):
        got = swap(give, SIBLING)
        moving = call(forward_kernel, [shape((2,) + keep.shape[1:], BF16)] * (len(steps) - 1))(keep, got)
        return (keep, got, *(swap(block, step) for block, step in zip(moving, steps[1:])))

    def exchange_panels(both, b):
        moved = {0: both[0]}
        for step in ALL_STEPS[1:]:
            n = NEAR_STEPS.index(step % NEAR)
            moved[step] = swap(both[n] if step < NEAR else b[n], step)
        near = [moved[step] for step in NEAR_STEPS]
        far = [moved[step ^ NEAR] for step in NEAR_STEPS]
        (all_b,) = call(all_b_kernel, [shape((2 * CHIPS,) + both[0].shape[1:], BF16)])(*near, *far)
        return (*near, *far, swap(all_b, SIBLING))

    def messages(targets, tiles):
        return shape((targets, tiles, rows, LANES), BF16)

    def scratch_tiles(targets, tiles):
        return pltpu.VMEM(messages(targets, tiles).shape, BF16)

    plane = shape((channels, positions), F32)
    half_plane = shape((channels, positions), BF16)
    mask = residue_mask.reshape(1, -1)
    by_position = pltpu.VMEM((positions, channels), F32)
    weights = (channels, 4 * hidden)
    chunks = positions // CHUNK
    pairs = hidden // NEAR // 2
    per_chip = (messages(2, pairs),) * CHIPS
    both_per_chip = (shape((2, 2, pairs, rows, LANES), BF16),) * CHIPS
    all_steps = (messages(len(ALL_STEPS), pairs),) * 2
    gate = call(gate_kernel, [plane], flops=2 * channels * channels * positions, transcendentals=channels * positions)

    far = (pair.reshape(positions, channels), mask, out_proj.reshape(-1, hidden))
    outs = (*both_per_chip, *per_chip, plane, half_plane, shape((rows, LANES), F32))
    scratch = [pltpu.VMEM(a.shape, a.dtype) for a in far]
    wide = pltpu.VMEM((4 * channels, hidden), F32)
    scratch += [pltpu.VMEM(weights, BF16), wide]
    scratch += [scratch_tiles(NEAR, pairs), pltpu.SemaphoreType.DMA((chunks + 2,))]
    outs = call(functools.partial(first_kernel, rows, cols), outs, scratch, (3, 0))(*far)
    pair_t, normed, live = outs[2 * CHIPS :]
    came = exchange_panels(outs[:CHIPS], outs[CHIPS : 2 * CHIPS])
    (weights,) = call(second_weights_kernel, [shape(weights, BF16)], [wide])(in_proj.reshape(-1, hidden))
    gating, weights, came = lax.optimization_barrier((gate(normed, out_gate)[0], weights, came))

    scratch = [scratch_tiles(CHIPS, 2 * pairs), scratch_tiles(devices, 2 * pairs), scratch_tiles(CHIPS, 2 * pairs)]
    own, *others = call(functools.partial(outgoing_kernel, cols), per_chip, scratch)(*came)
    came = (own, *(swap(block, step) for block, step in zip(others, NEAR_STEPS[1:])))

    chip_tiles = scratch_tiles(CHIPS, 2 * pairs)
    half_step = messages(len(NEAR_STEPS), 2 * pairs)
    outs = (half_step, plane, half_plane)
    give, middle, normed = call(functools.partial(middle_kernel, rows, cols), outs, [scratch_tiles(NEAR, pairs), chip_tiles])(
        live, weights, out_final, pair_t, gating, *came
    )
    work = 4 * channels * hidden * positions
    (keep,) = call(functools.partial(keep_kernel, cols), [half_step], [chip_tiles], flops=work)(live, weights, normed)
    came = exchange(keep, give, NEAR_STEPS)
    gating, came = lax.optimization_barrier((gate(normed, in_gate)[0], came))

    scratch = [scratch_tiles(NEAR, 2 * pairs), scratch_tiles(devices, pairs)]
    keep, give = call(functools.partial(incoming_kernel, cols), all_steps, scratch)(*came)
    came = exchange(keep, give, ALL_STEPS)

    scratch = [scratch_tiles(devices, pairs), by_position, pltpu.SemaphoreType.DMA((chunks,))]
    outs = [shape((positions, channels), F32)]
    (out,) = call(functools.partial(last_kernel, rows, cols), outs, scratch, (0, 1))(middle, gating, in_final, *came)
    return out.reshape(rows, cols, channels)


def normalize(values, axis):
    average = jnp.mean(values, axis=axis, keepdims=True)
    centred = values - average
    variance = jnp.mean(centred * centred, axis=axis, keepdims=True)
    return centred * lax.rsqrt(variance + EPS)


def gated_panels(pair, row_live, col_live, proj):
    normed = normalize(pair, 2).astype(BF16)
    linear = jnp.einsum("ijc,cph->phij", normed, proj, preferred_element_type=F32)
    pair_mask = row_live[:, None] * col_live[None, :]
    left_panel = (pair_mask * jax.nn.sigmoid(linear[1]) * linear[0]).astype(BF16)
    right_panel = (pair_mask * jax.nn.sigmoid(linear[3]) * linear[2]).astype(BF16)
    return (normed, left_panel, right_panel)


def update_pair(pair, normed, mixed, gate_w, final_w):
    all_channels = lax.all_gather(mixed, "sub", axis=0, tiled=True)
    scaled = normalize(all_channels, 0).astype(BF16)
    projected = jnp.einsum("hij,hc->ijc", scaled, final_w, preferred_element_type=F32)
    gating = jax.nn.sigmoid(jnp.einsum("ijc,cd->ijd", normed, gate_w, preferred_element_type=F32))
    return pair + gating * projected


def by_position(pair, residue_mask, out_proj, out_gate, out_final, in_proj, in_gate, in_final):
    row_count = pair.shape[0]
    col_count = pair.shape[1]
    row_start = lax.axis_index("row") * row_count
    col_start = lax.axis_index("col") * col_count
    live = residue_mask.astype(F32)
    row_live = lax.dynamic_slice_in_dim(live, row_start, row_count, 0)
    col_live = lax.dynamic_slice_in_dim(live, col_start, col_count, 0)
    normed, left_panel, right_panel = gated_panels(pair, row_live, col_live, out_proj)
    left_rows, right_rows = (
        lax.all_gather(left_panel, "col", axis=2, tiled=True),
        lax.all_gather(right_panel, "col", axis=2, tiled=True),
    )
    turned = lax.all_to_all(right_rows, "row", split_axis=2, concat_axis=1, tiled=True)
    own_right = lax.dynamic_slice_in_dim(turned, col_start, col_count, 1)
    mixed = jnp.einsum(
        "hik,hjk->hij",
        left_rows,
        lax.all_gather(own_right, "row", axis=2, tiled=True),
        preferred_element_type=F32,
    )
    middle = update_pair(pair, normed, mixed, out_gate, out_final)
    normed, left_panel, right_panel = gated_panels(middle, row_live, col_live, in_proj)
    left_rows = lax.all_gather(left_panel, "col", axis=2, tiled=True)
    turned_left = lax.all_to_all(left_rows, "row", split_axis=2, concat_axis=1, tiled=True)
    mixed_in = jnp.einsum(
        "hki,hkj->hij",
        turned_left,
        lax.all_gather(right_panel, "row", axis=1, tiled=True),
        preferred_element_type=F32,
    )
    return update_pair(middle, normed, mixed_in, in_gate, in_final)


def local(axes, pair, residue_mask, out_proj, *rest):
    rows, cols, channels = pair.shape
    hidden = out_proj.shape[2]
    devices = axes["row"] * axes["col"]
    fits = (
        axes["sub"] == 1
        and axes["col"] == 2
        and residue_mask.shape[0] == LANES
        and cols * 2 == LANES
        and rows % 16 == 0
        and rows * cols % CHUNK == 0
        and channels == LANES
        and hidden == channels
        and devices == 2 * NEAR
        and hidden % (2 * NEAR) == 0
        and hidden % 16 == 0
    )
    plan = functools.partial(by_channel, devices) if fits else by_position
    return plan(pair, residue_mask, out_proj, *rest)


def solution(mesh):
    return jax.shard_map(
        functools.partial(local, dict(mesh.shape)),
        mesh=mesh,
        in_specs=(
            P(("groups", "row"), "col", None),
            P("groups"),
            P(None, None, "sub"),
            P(),
            P(),
            P(None, None, "sub"),
            P(),
            P(),
        ),
        out_specs=P(("groups", "row"), "col", None),
        check_vma=False,
    )
```

```python
import functools

import jax
import jax.numpy as jnp
from jax import lax
from jax.experimental import pallas as pl
from jax.experimental.pallas import tpu as pltpu
from jax.sharding import PartitionSpec as P

F32 = jnp.float32
BF16 = jnp.bfloat16
LANES = 128
CHUNK = 512
NEAR = 8
SIBLING = 2
NEAR_STEPS = (0, 5, 4, 1)
ALL_STEPS = (0, 13, 12, 5, 9, 8, 4, 1)
CHIPS = len(NEAR_STEPS)
EPS = 1e-05


def over_channels(values):
    centred = values - jnp.mean(values, axis=0, keepdims=True)
    variance = jnp.mean(centred * centred, axis=0, keepdims=True)
    return centred * lax.rsqrt(variance + EPS)


def product(weight, values):
    return lax.dot_general(weight, values, (((0,), (0,)), ((), ())), preferred_element_type=F32)


def panels_of(proj_ref, wide, channels):
    wide[...] = proj_ref[...].astype(F32)
    return [wide[pl.ds(n, channels, stride=4), :] for n in range(4)]


def first_weights(proj_ref, wide, weights):
    channels, hidden = weights.shape[0], weights.shape[1] // 4
    odd = lax.axis_index("col") == 1
    for n, panel in enumerate(panels_of(proj_ref, wide, channels)):
        panel = jnp.where(odd, pltpu.roll(panel, hidden // 2, 1), panel)
        weights[:, n * hidden : (n + 1) * hidden] = panel.astype(BF16)


def second_weights_kernel(proj_ref, weights, wide):
    channels, hidden = weights.shape[0], weights.shape[1] // 4
    quarter = hidden // 4
    odd = lax.axis_index("col") == 1
    upper = lax.axis_index("row") % 2 == 1
    a, a_gate, b, b_gate = panels_of(proj_ref, wide, channels)
    panels = [jnp.where(odd, b, a), jnp.where(odd, b_gate, a_gate), jnp.where(odd, a, b), jnp.where(odd, a_gate, b_gate)]
    lane = lax.broadcasted_iota(jnp.int32, (channels, hidden), 1)
    kept, given = [], []
    for panel in panels:
        shifted = pltpu.roll(panel, hidden - quarter, 1)
        lower_part = jnp.where(lane < quarter, panel, shifted)
        upper_part = jnp.where(lane < quarter, shifted, pltpu.roll(panel, hidden // 2, 1))
        kept.append(jnp.where(upper, upper_part, lower_part))
        given.append(jnp.where(upper, lower_part, upper_part))
    for n, (x, y) in enumerate(((kept[0], kept[1]), (kept[2], kept[3]), (given[0], given[1]), (given[2], given[3]))):
        both = jnp.where(lane < hidden // 2, x, pltpu.roll(y, hidden // 2, 1))
        weights[:, n * hidden : (n + 1) * hidden] = both.astype(BF16)


def live_tile(mask_ref, rows, cols):
    live = mask_ref[...].astype(F32)
    lane = lax.broadcasted_iota(jnp.int32, (rows, LANES), 1)
    sub = lax.broadcasted_iota(jnp.int32, (rows, LANES), 0)
    wide = jnp.broadcast_to(live, (rows, LANES))
    mine = lane == lax.axis_index("row") * rows + sub
    row_live = jnp.sum(jnp.where(mine, wide, 0.0), axis=1, keepdims=True)
    col_live = jnp.where(lane // cols == lax.axis_index("col"), wide, pltpu.roll(wide, cols, 1))
    return row_live * col_live


def panels(normed, weights):
    hidden = weights.shape[1] // 4
    linear = product(weights[...], normed)
    return [jax.nn.sigmoid(linear[(p + 1) * hidden : (p + 2) * hidden]) * linear[p * hidden : (p + 1) * hidden] for p in (0, 2)]


def gate_kernel(normed_ref, gate_ref, gating_ref):
    gating_ref[...] = jax.nn.sigmoid(product(gate_ref[...], normed_ref[...]))


def paired(first, second, live, cols):
    low = lax.broadcasted_iota(jnp.int32, (first.shape[0], LANES), 1) < cols
    by_row = []
    for t in range(live.shape[0] // 2):
        a = first[:, t * LANES : (t + 1) * LANES]
        b = second[:, t * LANES : (t + 1) * LANES]
        for tile in (jnp.where(low, a, pltpu.roll(b, cols, 1)), jnp.where(low, pltpu.roll(a, cols, 1), b)):
            row = len(by_row)
            by_row.append((tile * live[row : row + 1]).astype(BF16))
    return jnp.swapaxes(jnp.stack(by_row, axis=0), 0, 1)


def summed(values):
    chains = values.reshape((values.shape[0] // 8, 8) + values.shape[1:])
    return jnp.sum(jnp.sum(chains, axis=0), axis=0)


def projected(recv_ref, final_ref, rows, cols):
    half = final_ref.shape[0] // 2
    values = jnp.sum(recv_ref[...].reshape(-1, half, rows, LANES).astype(F32), axis=0)
    total = summed(values)
    centred = values - ((total + pltpu.roll(total, cols, 1)) / (2 * half))[None]
    square = summed(centred * centred)
    variance = (square + pltpu.roll(square, cols, 1)) / (2 * half)
    scaled = jnp.swapaxes((centred * lax.rsqrt(variance + EPS)[None]).astype(BF16), 0, 1).astype(F32)
    low = lax.broadcasted_iota(jnp.int32, (half, LANES), 1) < cols
    parts = []
    for t in range(rows // 2):
        a, b = scaled[2 * t], scaled[2 * t + 1]
        upper = jnp.where(low, a, pltpu.roll(b, cols, 1))
        lower = jnp.where(low, pltpu.roll(a, cols, 1), b)
        parts.append(jnp.concatenate([upper, lower], axis=0).astype(BF16))
    return product(final_ref[...], jnp.concatenate(parts, axis=1))


def copies(pairs, done):
    started = [pltpu.make_async_copy(source, target, done.at[n]) for n, (source, target) in enumerate(pairs)]
    for copy in started:
        copy.start()
    return started


def own_index():
    return lax.axis_index("row") * 2 + lax.axis_index("col")


def within_half(index):
    return index & (NEAR - 1)


def chip_of(index):
    return (index >> 1) & 2 | index & 1


def by_owner(index):
    return index & NEAR | (index & SIBLING) << 1 | chip_of(index)


def hand_out(tiles, steps, keep_ref, give_ref):
    me = own_index()
    for n, step in enumerate(steps):
        keep_ref[n] = tiles[me ^ step]
        give_ref[n] = tiles[me ^ (step ^ SIBLING)]


def forward_kernel(keep_ref, got_ref, *out_refs):
    for n, out_ref in enumerate(out_refs):
        out_ref[0] = keep_ref[n + 1]
        out_ref[1] = got_ref[n + 1]


def take_in(refs, steps, tiles, place):
    keep_ref, got_ref, *moved_refs = refs
    me = place(own_index())
    tiles[me] = keep_ref[0]
    tiles[me ^ place(SIBLING)] = got_ref[0]
    for step, moved_ref in zip(steps[1:], moved_refs):
        tiles[me ^ place(step)] = moved_ref[0]
        tiles[me ^ place(step ^ SIBLING)] = moved_ref[1]


def chip_blocks(me, step):
    base = (within_half(me) & ~SIBLING) ^ (within_half(step) & ~SIBLING)
    return base, base | SIBLING


def all_b_kernel(*refs):
    *came_refs, out_ref = refs
    for n, ref in enumerate(came_refs):
        out_ref[n] = ref[1] if n < CHIPS else ref[...]


def first_kernel(rows, cols, pair_hbm, mask_hbm, proj_hbm, *refs):
    both_refs, b_refs = refs[:CHIPS], refs[CHIPS : 2 * CHIPS]
    pair_t_ref, normed_ref, live_ref = refs[2 * CHIPS : 2 * CHIPS + 3]
    pair_ref, mask_ref, proj_ref, weights, wide, by_near, done = refs[2 * CHIPS + 3 :]
    chunks = [slice(0, rows * cols)]
    whole = [(mask_hbm, mask_ref), (proj_hbm, proj_ref)]
    coming = copies(whole + [(pair_hbm.at[at], pair_ref.at[at]) for at in chunks], done)
    for copy in coming[: len(whole)]:
        copy.wait()
    first_weights(proj_ref, wide, weights)
    live = live_tile(mask_ref, rows, cols)
    live_ref[...] = live
    for copy in coming[len(whole) :]:
        copy.wait()
    pair = pair_ref[...].T
    pair_t_ref[...] = pair
    normed = over_channels(pair).astype(BF16)
    normed_ref[...] = normed
    me = own_index()
    for p, values in enumerate(panels(normed, weights)):
        half = values.shape[0] // 2
        by_near[...] = paired(values[:half], values[half:], live, cols).reshape(by_near.shape)
        for step, both_ref, b_ref in zip(NEAR_STEPS, both_refs, b_refs):
            for n, block in enumerate(chip_blocks(me, step)):
                both_ref[p, n] = by_near[block]
                if p == 1:
                    b_ref[n] = by_near[block]


def to_chips(normed, weights, live, cols, by_chip, out_ref):
    tiles = paired(*panels(normed, weights), live, cols)
    per_chip = tiles.shape[0] // 2 // CHIPS
    for d in range(CHIPS):
        by_chip[d, :per_chip] = tiles[d * per_chip : (d + 1) * per_chip]
        by_chip[d, per_chip:] = tiles[(CHIPS + d) * per_chip : (CHIPS + d + 1) * per_chip]
    me = chip_of(own_index())
    for n, step in enumerate(NEAR_STEPS):
        out_ref[n] = by_chip[me ^ chip_of(step)]


def middle_kernel(rows, cols, live_ref, weights, final_ref, pair_t_ref, gating_ref, *refs):
    *came_refs, give_ref, middle_ref, normed_ref, came, by_chip = refs
    me = own_index()
    for step, ref in zip(NEAR_STEPS, came_refs):
        for n, block in enumerate(chip_blocks(me, step)):
            came[block] = ref[n]
    middle = pair_t_ref[...] + gating_ref[...] * projected(came, final_ref, rows, cols)
    middle_ref[...] = middle
    normed = over_channels(middle).astype(BF16)
    normed_ref[...] = normed
    to_chips(normed, weights[:, weights.shape[1] // 2 :], live_ref[...], cols, by_chip, give_ref)


def keep_kernel(cols, live_ref, weights, normed_ref, keep_ref, by_chip):
    to_chips(normed_ref[...], weights[:, : weights.shape[1] // 2], live_ref[...], cols, by_chip, keep_ref)


def last_kernel(rows, cols, middle_ref, gating_ref, final_ref, *refs):
    *came_refs, out_hbm, came, out_ref, done = refs
    take_in(came_refs, ALL_STEPS, came, by_owner)
    change = projected(came, final_ref, rows, cols)
    leaving = []
    for n in range(rows * cols // CHUNK):
        at = slice(n * CHUNK, (n + 1) * CHUNK)
        out_ref[at, :] = (middle_ref[:, at] + gating_ref[:, at] * change[:, at]).T
        leaving.append(pltpu.make_async_copy(out_ref.at[at], out_hbm.at[at], done.at[n]))
        leaving[-1].start()
    for copy in leaving:
        copy.wait()


def low_of(x, cols):
    return lax.broadcasted_iota(jnp.int32, x.shape, 1) < cols


def both(ref, e):
    sources = ref.shape[0]
    return [jnp.concatenate([ref[r, e] for r in range(odd, sources, 2)], axis=0) for odd in (0, 1)]


def put(left, right, msg_ref, q):
    rows = msg_ref.shape[2]
    for r in range(msg_ref.shape[0] // 2):
        msg_ref[2 * r, q] = left[r * rows : (r + 1) * rows].astype(BF16)
        msg_ref[2 * r + 1, q] = right[r * rows : (r + 1) * rows].astype(BF16)


def outgoing_kernel(cols, *refs):
    both_refs, far_refs, sibling_ref = refs[:CHIPS], refs[CHIPS : 2 * CHIPS], refs[2 * CHIPS]
    *out_refs, a_ref, b_ref, msg_ref = refs[2 * CHIPS + 1 :]
    me = own_index()
    one = a_ref.shape[1:]
    for n, step in enumerate(NEAR_STEPS):
        a_ref[chip_of(me) ^ chip_of(step)] = both_refs[n][0].reshape(one)
        b_ref[me ^ step] = both_refs[n][1].reshape(one)
        b_ref[me ^ (step ^ SIBLING)] = sibling_ref[n].reshape(one)
        b_ref[me ^ (step ^ NEAR)] = far_refs[n][...].reshape(one)
        b_ref[me ^ (step ^ NEAR ^ SIBLING)] = sibling_ref[CHIPS + n].reshape(one)
    for q in range(msg_ref.shape[1]):
        even, odd = both(a_ref, q)
        low = low_of(even, cols)
        a, a2 = jnp.where(low, even, odd), jnp.where(low, odd, even)
        even, odd = both(b_ref, q)
        low = low_of(even, cols)
        b, b2 = jnp.where(low, even, odd), jnp.where(low, odd, even)
        x = lax.dot_general(a, b, (((1,), (1,)), ((), ())), preferred_element_type=F32)
        y = lax.dot_general(a2, b2, (((1,), (1,)), ((), ())), preferred_element_type=F32)
        low = low_of(x, cols)
        put(jnp.where(low, x, pltpu.roll(y, cols, 1)), jnp.where(low, pltpu.roll(x, cols, 1), y), msg_ref, q)
    for step, out_ref in zip(NEAR_STEPS, out_refs):
        out_ref[...] = msg_ref[chip_of(me) ^ chip_of(step)].reshape(out_ref.shape)


def incoming_kernel(cols, *refs):
    *came_refs, keep_ref, give_ref, recv_ref, msg_ref = refs
    take_in(came_refs, NEAR_STEPS, recv_ref, within_half)
    half = msg_ref.shape[1]

    def mixed(e):
        even, odd = both(recv_ref, e)
        low = low_of(even, cols)
        a, b = jnp.where(low, even, odd), jnp.where(low, odd, even)
        return lax.dot_general(a, b, (((0,), (0,)), ((), ())), preferred_element_type=F32)

    for q in range(half):
        x, y = mixed(q), mixed(q + half)
        low = low_of(x, cols)
        put(jnp.where(low, pltpu.roll(x, cols, 1), y), jnp.where(low, x, pltpu.roll(y, cols, 1)), msg_ref, q)
    hand_out(msg_ref, ALL_STEPS, keep_ref, give_ref)


def call(kernel, out_shape, scratch=(), far=(0, 0), flops=0, transcendentals=0):
    vmem = pl.BlockSpec(memory_space=pltpu.VMEM)
    hbm = pl.BlockSpec(memory_space=pltpu.HBM)
    far_args, far_outs = far

    def run(*args):
        args = [pltpu.with_memory_space_constraint(a, pltpu.HBM) for a in args[:far_args]] + list(args[far_args:])
        return pl.pallas_call(
            kernel,
            out_shape=tuple(out_shape),
            in_specs=[hbm] * far_args + [vmem] * (len(args) - far_args),
            out_specs=(hbm,) * far_outs + (vmem,) * (len(out_shape) - far_outs),
            scratch_shapes=list(scratch),
            compiler_params=pltpu.CompilerParams(vmem_limit_bytes=40 * 1024 * 1024),
            cost_estimate=pl.CostEstimate(
                flops=flops, transcendentals=transcendentals, bytes_accessed=sum(a.size * a.dtype.itemsize for a in (*args, *out_shape))
            ),
        )(*args)

    return run


def by_channel(devices, pair, residue_mask, out_proj, out_gate, out_final, in_proj, in_gate, in_final):
    rows, cols, channels = pair.shape
    hidden = out_proj.shape[2]
    positions = rows * cols
    shape = jax.ShapeDtypeStruct
    axes = ("row", "col")

    def swap(values, step):
        return lax.ppermute(values, axes, [(d, d ^ step) for d in range(devices)])

    def exchange(keep, give, steps):
        got = swap(give, SIBLING)
        moving = call(forward_kernel, [shape((2,) + keep.shape[1:], BF16)] * (len(steps) - 1))(keep, got)
        return (keep, got, *(swap(block, step) for block, step in zip(moving, steps[1:])))

    def exchange_panels(both, b):
        moved = {0: both[0]}
        for step in ALL_STEPS[1:]:
            n = NEAR_STEPS.index(step % NEAR)
            moved[step] = swap(both[n] if step < NEAR else b[n], step)
        near = [moved[step] for step in NEAR_STEPS]
        far = [moved[step ^ NEAR] for step in NEAR_STEPS]
        (all_b,) = call(all_b_kernel, [shape((2 * CHIPS,) + both[0].shape[1:], BF16)])(*near, *far)
        return (*near, *far, swap(all_b, SIBLING))

    def messages(targets, tiles):
        return shape((targets, tiles, rows, LANES), BF16)

    def scratch_tiles(targets, tiles):
        return pltpu.VMEM(messages(targets, tiles).shape, BF16)

    plane = shape((channels, positions), F32)
    half_plane = shape((channels, positions), BF16)
    mask = residue_mask.reshape(1, -1)
    by_position = pltpu.VMEM((positions, channels), F32)
    weights = (channels, 4 * hidden)
    chunks = positions // CHUNK
    pairs = hidden // NEAR // 2
    per_chip = (messages(2, pairs),) * CHIPS
    both_per_chip = (shape((2, 2, pairs, rows, LANES), BF16),) * CHIPS
    all_steps = (messages(len(ALL_STEPS), pairs),) * 2
    gate = call(gate_kernel, [plane], flops=2 * channels * channels * positions, transcendentals=channels * positions)

    far = (pair.reshape(positions, channels), mask, out_proj.reshape(-1, hidden))
    outs = (*both_per_chip, *per_chip, plane, half_plane, shape((rows, LANES), F32))
    scratch = [pltpu.VMEM(a.shape, a.dtype) for a in far]
    wide = pltpu.VMEM((4 * channels, hidden), F32)
    scratch += [pltpu.VMEM(weights, BF16), wide]
    scratch += [scratch_tiles(NEAR, pairs), pltpu.SemaphoreType.DMA((chunks + 2,))]
    outs = call(functools.partial(first_kernel, rows, cols), outs, scratch, (3, 0))(*far)
    pair_t, normed, live = outs[2 * CHIPS :]
    came = exchange_panels(outs[:CHIPS], outs[CHIPS : 2 * CHIPS])
    (weights,) = call(second_weights_kernel, [shape(weights, BF16)], [wide])(in_proj.reshape(-1, hidden))
    (gating,) = gate(normed, out_gate)

    scratch = [scratch_tiles(CHIPS, 2 * pairs), scratch_tiles(devices, 2 * pairs), scratch_tiles(CHIPS, 2 * pairs)]
    own, *others = call(functools.partial(outgoing_kernel, cols), per_chip, scratch)(*came)
    came = (own, *(swap(block, step) for block, step in zip(others, NEAR_STEPS[1:])))

    chip_tiles = scratch_tiles(CHIPS, 2 * pairs)
    half_step = messages(len(NEAR_STEPS), 2 * pairs)
    outs = (half_step, plane, half_plane)
    give, middle, normed = call(functools.partial(middle_kernel, rows, cols), outs, [scratch_tiles(NEAR, pairs), chip_tiles])(
        live, weights, out_final, pair_t, gating, *came
    )
    work = 4 * channels * hidden * positions
    (keep,) = call(functools.partial(keep_kernel, cols), [half_step], [chip_tiles], flops=work)(live, weights, normed)
    came = exchange(keep, give, NEAR_STEPS)
    gating, came = lax.optimization_barrier((gate(normed, in_gate)[0], came))

    scratch = [scratch_tiles(NEAR, 2 * pairs), scratch_tiles(devices, pairs)]
    keep, give = call(functools.partial(incoming_kernel, cols), all_steps, scratch)(*came)
    came = exchange(keep, give, ALL_STEPS)

    scratch = [scratch_tiles(devices, pairs), by_position, pltpu.SemaphoreType.DMA((chunks,))]
    outs = [shape((positions, channels), F32)]
    (out,) = call(functools.partial(last_kernel, rows, cols), outs, scratch, (0, 1))(middle, gating, in_final, *came)
    return out.reshape(rows, cols, channels)


def normalize(values, axis):
    average = jnp.mean(values, axis=axis, keepdims=True)
    centred = values - average
    variance = jnp.mean(centred * centred, axis=axis, keepdims=True)
    return centred * lax.rsqrt(variance + EPS)


def gated_panels(pair, row_live, col_live, proj):
    normed = normalize(pair, 2).astype(BF16)
    linear = jnp.einsum("ijc,cph->phij", normed, proj, preferred_element_type=F32)
    pair_mask = row_live[:, None] * col_live[None, :]
    left_panel = (pair_mask * jax.nn.sigmoid(linear[1]) * linear[0]).astype(BF16)
    right_panel = (pair_mask * jax.nn.sigmoid(linear[3]) * linear[2]).astype(BF16)
    return (normed, left_panel, right_panel)


def update_pair(pair, normed, mixed, gate_w, final_w):
    all_channels = lax.all_gather(mixed, "sub", axis=0, tiled=True)
    scaled = normalize(all_channels, 0).astype(BF16)
    projected = jnp.einsum("hij,hc->ijc", scaled, final_w, preferred_element_type=F32)
    gating = jax.nn.sigmoid(jnp.einsum("ijc,cd->ijd", normed, gate_w, preferred_element_type=F32))
    return pair + gating * projected


def by_position(pair, residue_mask, out_proj, out_gate, out_final, in_proj, in_gate, in_final):
    row_count = pair.shape[0]
    col_count = pair.shape[1]
    row_start = lax.axis_index("row") * row_count
    col_start = lax.axis_index("col") * col_count
    live = residue_mask.astype(F32)
    row_live = lax.dynamic_slice_in_dim(live, row_start, row_count, 0)
    col_live = lax.dynamic_slice_in_dim(live, col_start, col_count, 0)
    normed, left_panel, right_panel = gated_panels(pair, row_live, col_live, out_proj)
    left_rows, right_rows = (
        lax.all_gather(left_panel, "col", axis=2, tiled=True),
        lax.all_gather(right_panel, "col", axis=2, tiled=True),
    )
    turned = lax.all_to_all(right_rows, "row", split_axis=2, concat_axis=1, tiled=True)
    own_right = lax.dynamic_slice_in_dim(turned, col_start, col_count, 1)
    mixed = jnp.einsum(
        "hik,hjk->hij",
        left_rows,
        lax.all_gather(own_right, "row", axis=2, tiled=True),
        preferred_element_type=F32,
    )
    middle = update_pair(pair, normed, mixed, out_gate, out_final)
    normed, left_panel, right_panel = gated_panels(middle, row_live, col_live, in_proj)
    left_rows = lax.all_gather(left_panel, "col", axis=2, tiled=True)
    turned_left = lax.all_to_all(left_rows, "row", split_axis=2, concat_axis=1, tiled=True)
    mixed_in = jnp.einsum(
        "hki,hkj->hij",
        turned_left,
        lax.all_gather(right_panel, "row", axis=1, tiled=True),
        preferred_element_type=F32,
    )
    return update_pair(middle, normed, mixed_in, in_gate, in_final)


def local(axes, pair, residue_mask, out_proj, *rest):
    rows, cols, channels = pair.shape
    hidden = out_proj.shape[2]
    devices = axes["row"] * axes["col"]
    fits = (
        axes["sub"] == 1
        and axes["col"] == 2
        and residue_mask.shape[0] == LANES
        and cols * 2 == LANES
        and rows % 16 == 0
        and rows * cols % CHUNK == 0
        and channels == LANES
        and hidden == channels
        and devices == 2 * NEAR
        and hidden % (2 * NEAR) == 0
        and hidden % 16 == 0
    )
    plan = functools.partial(by_channel, devices) if fits else by_position
    return plan(pair, residue_mask, out_proj, *rest)


def solution(mesh):
    return jax.shard_map(
        functools.partial(local, dict(mesh.shape)),
        mesh=mesh,
        in_specs=(
            P(("groups", "row"), "col", None),
            P("groups"),
            P(None, None, "sub"),
            P(),
            P(),
            P(None, None, "sub"),
            P(),
            P(),
        ),
        out_specs=P(("groups", "row"), "col", None),
        check_vma=False,
    )
```
